32 devices in a mesh: groups: 2 (over x), row: 16 (over z, y, core).
Axes of the slice: x: 2, y: 2, z: 4, core: 2. Of those that a mesh axis runs over, the one named last changes fastest.
Arguments:
- field: bfloat16 [512, 128, 512], P(('groups', 'row')), parts along dimension 0, may hold values from -6 to 6
- cotangent: bfloat16 [512, 128, 512], P(('groups', 'row')), parts along dimension 0, may hold values from -6 to 6
- row_filters: float32 [2, 4], replicated, may hold values from -0.7 to 0.7
- col_filter_1: bfloat16 [512, 512], replicated, may hold values from -1 to 1, as said below
- col_filter_2: bfloat16 [256, 256], replicated, may hold values from -1 to 1, as said below
- col_filter_3: bfloat16 [128, 128], replicated, may hold values from -1 to 1, as said below
- detail_weight: bfloat16 [3, 3, 128, 128], replicated, may hold values from -0.5 to 0.5
- skip_weight: bfloat16 [128, 128], replicated, may hold values from -0.5 to 0.5
- spectral_weight: float32 [2, 1024, 128, 128], P(None, 'row'), may hold values from -1.5 to 1.5
- row_modes: int32 [32], replicated, may hold values from 0 to 31, as said below
- col_modes: int32 [32], replicated, may hold values from 0 to 63, as said below
Outputs:
- grad_field: float32 [512, 128, 512], P(('groups', 'row')), parts along dimension 0
- grad_detail: float32 [6, 3, 128, 128], P('groups'), parts along dimension 0
- grad_skip: float32 [256, 128], P('groups'), parts along dimension 0
- grad_spectral: float32 [4, 1024, 128, 128], P('groups', 'row'), parts along dimension 0
The draws below stay inside these ranges and needn't reach their ends.
There are 2 independent parts, one for each index of `groups`. The reference program is written for one: setup_inputs(seed, part) draws one part's arguments, and reference() takes and returns one part's arrays. A program takes and returns all parts, laid end to end along the dimension named above; an argument that names none is the same for every part. Nothing has to cross between parts.
Inputs may be any that keep to these rules, and one draw needn't show every extreme that they name: `row_modes`: 32 distinct row frequencies. `col_modes`: 32 distinct column frequencies. `col_filter_1`: zero outside the 128-blocks (j, j) and (j+1 mod n, j). `col_filter_2`: zero outside the 128-blocks (j, j) and (j+1 mod n, j). `col_filter_3`: zero outside the 128-blocks (j, j) and (j+1 mod n, j).
All inputs are finite; a program needn't handle non-finite values.
Results may differ from the reference program's by a relative error of at most 0.02.
Values may be sent and summed in bfloat16 or wider, within the bound.
A program may use at most 128 MiB of HBM per device.

```python
import math
import jax
import jax.numpy as jnp
from jax import lax

C = 128
W = 512
BLOCK = 128
LEVELS = 3
MX = 32
MY = 32
H = 256
COARSE_H = 32
COARSE_W = 64
MODES = 1024


def distinct_modes(key, needed, length):
    inner = jax.random.permutation(key, length - 2).astype(jnp.int32) + 1
    ends = jnp.array([0, length - 1], dtype=jnp.int32)
    chosen = jnp.concatenate([ends, inner[:needed - 2]])
    return jax.random.permutation(jax.random.fold_in(key, 7), chosen)


def draw_row_modes(key, part):
    key = jax.random.fold_in(key, 11)
    return distinct_modes(key, MX, COARSE_H)


def draw_col_modes(key, part):
    key = jax.random.fold_in(key, 13)
    return distinct_modes(key, MY, COARSE_W)


def tap_values(key, power):
    sign_key = jax.random.fold_in(key, 3)
    size_key = jax.random.fold_in(key, 5)
    signs = jnp.where(jax.random.bernoulli(sign_key, 0.5, (2, 4)), 1.0, -1.0)
    fraction = jax.random.uniform(size_key, (2, 4), jnp.float32, 0.0, 1.0) ** power
    lows = jnp.array([0.25, 0.25, 0.5, 0.5], jnp.float32)
    spans = jnp.array([0.15, 0.15, 0.15, 0.15], jnp.float32)
    return (signs * (lows[None, :] + spans[None, :] * fraction)).astype(jnp.float32)


def draw_row_filters(key, part):
    key = jax.random.fold_in(key, 29)
    return tap_values(key, 1.0)


def banded_mask(order):
    blocks = order // BLOCK
    row_block = jnp.arange(order, dtype=jnp.int32) // BLOCK
    col_block = jnp.arange(order, dtype=jnp.int32) // BLOCK
    same = row_block[:, None] == col_block[None, :]
    below = row_block[:, None] == (col_block[None, :] + 1) % blocks
    return jnp.logical_or(same, below)


def banded_values(key, order):
    spread = float(min(order, 2 * BLOCK)) ** (-0.5)
    values = jnp.clip(jax.random.normal(key, (order, order), jnp.float32), -3.0, 3.0)
    kept = jnp.where(banded_mask(order), values * spread, 0.0)
    return kept.astype(jnp.bfloat16)


def draw_col_filter_1(key, part):
    key = jax.random.fold_in(key, 17)
    return banded_values(key, W)


def draw_col_filter_2(key, part):
    key = jax.random.fold_in(key, 19)
    return banded_values(key, W // 2)


def draw_col_filter_3(key, part):
    key = jax.random.fold_in(key, 23)
    return banded_values(key, W // 4)


def block_scale(stream_key, dims, split, least, top_value):
    gain, own = 1.0, jax.random.fold_in(stream_key, 6)
    for position, parts in split:
        steps = jnp.exp(jax.random.uniform(jax.random.fold_in(own, position), (parts,), jnp.float32, least / len(split), top_value / len(split)))
        gain = gain * jnp.repeat(steps, dims[position] // parts).reshape([-1 if axis == position else 1 for axis in range(len(dims))])
    return gain


def centred(rng, dims, deviation, most, pieces=(), kind=jnp.bfloat16):
    drawn = jax.random.normal(rng, dims, jnp.float32) * deviation
    if len(pieces) > 0:
        drawn = block_scale(rng, dims, pieces, -0.22, 0.18) * drawn
    return jnp.clip(drawn, min=-most, max=most).astype(kind)


def setup_inputs(seed: int = 0, part: int = 0) -> dict:
    splits = jax.random.split(jax.random.key(seed), 12)
    part_keys = jax.random.split(jax.random.fold_in(splits[11], part), 12)
    return {
        "field": centred(part_keys[0], (H, C, W), 1.0, 6.0, ((0, 16),)),
        "cotangent": centred(part_keys[1], (H, C, W), 1.0, 6.0, ((0, 16),)),
        "row_filters": draw_row_filters(jax.random.fold_in(splits[11], 71), part),
        "col_filter_1": draw_col_filter_1(jax.random.fold_in(splits[11], 71), part),
        "col_filter_2": draw_col_filter_2(jax.random.fold_in(splits[11], 71), part),
        "col_filter_3": draw_col_filter_3(jax.random.fold_in(splits[11], 71), part),
        "detail_weight": centred(splits[6], (LEVELS, 3, C, C), C ** -0.5, 0.5),
        "skip_weight": centred(splits[7], (C, C), C ** -0.5, 0.5),
        "spectral_weight": centred(splits[8], (2, MODES, C, C), 0.25, 1.5, ((1, 16),), jnp.float32),
        "row_modes": draw_row_modes(jax.random.fold_in(splits[11], 71), part),
        "col_modes": draw_col_modes(jax.random.fold_in(splits[11], 71), part),
    }


def as_float(values):
    return values.astype(jnp.float32)

def rounded(values):
    return lax.optimization_barrier(values.astype(jnp.bfloat16))

def product(form, first_in, second_in):
    return jnp.einsum(form, as_float(first_in), as_float(second_in), precision=lax.Precision.HIGHEST)

def row_pass(values, row_filters):
    spread = as_float(values)
    outputs = []
    for branch in range(2):
        running = row_filters[branch, 0] * spread[0::2]
        for offset in range(1, 4):
            running = running + row_filters[branch, offset] * jnp.roll(spread, -offset, axis=0)[0::2]
        outputs.append(rounded(running))
    return (outputs[0], outputs[1])

def analysis(values, row_filters, matrices):
    band_list = []
    current = values
    for matrix in matrices:
        low_rows, high_rows = row_pass(current, row_filters)
        low_cols = rounded(product('hcw,wv->hcv', low_rows, matrix))
        high_cols = rounded(product('hcw,wv->hcv', high_rows, matrix))
        halfway = low_cols.shape[2] // 2
        current = low_cols[:, :, :halfway]
        band_list.append((low_cols[:, :, halfway:], high_cols[:, :, :halfway], high_cols[:, :, halfway:]))
    return (current, band_list)

def combine_rows(low_now, high_now, low_prev, high_prev, row_filters):
    parities = []
    for parity in range(2):
        running = row_filters[0, parity] * low_now + row_filters[1, parity] * high_now
        running = running + row_filters[0, parity + 2] * low_prev
        running = running + row_filters[1, parity + 2] * high_prev
        parities.append(running)
    stacked = jnp.stack(parities, axis=1)
    return stacked.reshape((2 * low_now.shape[0],) + low_now.shape[1:])

def synthesis(top_array, band_list, row_filters, matrices):
    current = top_array
    for octave in (2, 1, 0):
        band_one, band_two, band_three = band_list[octave]
        low_sum = as_float(rounded(product('hcv,wv->hcw', jnp.concatenate([current, band_one], axis=2), matrices[octave])))
        high_sum = as_float(rounded(product('hcv,wv->hcw', jnp.concatenate([band_two, band_three], axis=2), matrices[octave])))
        current = combine_rows(low_sum, high_sum, jnp.roll(low_sum, 1, axis=0), jnp.roll(high_sum, 1, axis=0), row_filters)
        if octave > 0:
            current = rounded(current)
    return current

def column_tables(col_modes, length):
    positions = jnp.arange(length, dtype=jnp.int32)
    turns = positions[:, None] * col_modes[None, :] % length
    angles = turns.astype(jnp.float32) * (2.0 * math.pi / length)
    return (jnp.cos(angles), jnp.sin(angles))

def row_tables(row_modes, positions, length):
    turns = row_modes[:, None] * positions[None, :] % length
    angles = turns.astype(jnp.float32) * (2.0 * math.pi / length)
    return (jnp.cos(angles), jnp.sin(angles))

def mode_spectrum(coarse, row_modes, col_modes):
    height, channels, columns = coarse.shape
    cos_col, sin_col = column_tables(col_modes, columns)
    real_one = product('hcw,wm->hcm', coarse, cos_col)
    imag_one = -product('hcw,wm->hcm', coarse, sin_col)
    cos_row, sin_row = row_tables(row_modes, jnp.arange(height, dtype=jnp.int32), height)
    real_two = product('ph,hcm->pmc', cos_row, real_one) + product('ph,hcm->pmc', sin_row, imag_one)
    imag_two = product('ph,hcm->pmc', cos_row, imag_one) - product('ph,hcm->pmc', sin_row, real_one)
    return (real_two.reshape(-1, channels), imag_two.reshape(-1, channels))

def spectral_image(real_modes, imag_modes, row_modes, col_modes, height, columns):
    channels = real_modes.shape[1]
    real_grid = real_modes.reshape(row_modes.shape[0], col_modes.shape[0], channels)
    imag_grid = imag_modes.reshape(row_modes.shape[0], col_modes.shape[0], channels)
    cos_row, sin_row = row_tables(row_modes, jnp.arange(height, dtype=jnp.int32), height)
    real_one = product('ph,pmc->hcm', cos_row, real_grid) - product('ph,pmc->hcm', sin_row, imag_grid)
    imag_one = product('ph,pmc->hcm', cos_row, imag_grid) + product('ph,pmc->hcm', sin_row, real_grid)
    cos_col, sin_col = column_tables(col_modes, columns)
    image = product('hcm,wm->hcw', real_one, cos_col) - product('hcm,wm->hcw', imag_one, sin_col)
    return image.astype(jnp.bfloat16)

def mix_modes(real_in, imag_in, weight_real, weight_imag, factor):
    real_out = (product('nc,nco->no', real_in, weight_real) - product('nc,nco->no', imag_in, weight_imag)) * factor
    imag_out = (product('nc,nco->no', real_in, weight_imag) + product('nc,nco->no', imag_in, weight_real)) * factor
    return (real_out, imag_out)

def mix_modes_back(real_in, imag_in, weight_real, weight_imag, factor):
    real_out = (product('no,nco->nc', real_in, weight_real) + product('no,nco->nc', imag_in, weight_imag)) * factor
    imag_out = (product('no,nco->nc', imag_in, weight_real) - product('no,nco->nc', real_in, weight_imag)) * factor
    return (real_out, imag_out)

def reference(field, cotangent, row_filters, col_filter_1, col_filter_2, col_filter_3, detail_weight, skip_weight, spectral_weight, row_modes, col_modes):
    matrices = (col_filter_1, col_filter_2, col_filter_3)
    coarse_field, bands_field = analysis(field, row_filters, matrices)
    height, channels, columns = coarse_field.shape
    factor = 1.0 / (height * columns)
    weight_real = spectral_weight[0]
    weight_imag = spectral_weight[1]
    spec_real, spec_imag = mode_spectrum(coarse_field, row_modes, col_modes)
    out_real, out_imag = mix_modes(spec_real, spec_imag, weight_real, weight_imag, factor)
    coarse_image = spectral_image(out_real, out_imag, row_modes, col_modes, height, columns)
    mixed_field = [tuple((rounded(product('hcw,co->how', bands_field[octave][member], detail_weight[octave, member])) for member in range(3))) for octave in range(3)]
    rebuilt_field = synthesis(coarse_image, mixed_field, row_filters, matrices)
    activation_in = rebuilt_field + product('hcw,co->how', field, skip_weight)
    upstream = rounded(jax.vjp(jax.nn.gelu, activation_in)[1](as_float(cotangent))[0])
    coarse_slope, bands_slope = analysis(upstream, row_filters, matrices)
    back_real, back_imag = mode_spectrum(coarse_slope, row_modes, col_modes)
    turned_real, turned_imag = mix_modes_back(back_real, back_imag, weight_real, weight_imag, factor)
    image_back = spectral_image(turned_real, turned_imag, row_modes, col_modes, height, columns)
    back_bands = [tuple((rounded(product('how,co->hcw', bands_slope[octave][member], detail_weight[octave, member])) for member in range(3))) for octave in range(3)]
    rebuilt_slope = synthesis(image_back, back_bands, row_filters, matrices)
    grad_field = rebuilt_slope + product('how,co->hcw', upstream, skip_weight)
    total_rows = field.shape[0]
    total_cols = field.shape[2]
    grad_skip = product('hcw,how->co', field, upstream) / math.sqrt(total_rows * total_cols)
    grad_detail = jnp.stack([jnp.stack([product('hcw,how->co', bands_field[octave][member], bands_slope[octave][member]) / math.sqrt((total_rows >> octave + 1) * (total_cols >> octave + 1)) for member in range(3)]) for octave in range(3)])
    grad_real = (spec_real[:, :, None] * back_real[:, None, :] + spec_imag[:, :, None] * back_imag[:, None, :]) * factor
    grad_imag = (spec_real[:, :, None] * back_imag[:, None, :] - spec_imag[:, :, None] * back_real[:, None, :]) * factor
    grad_spectral = jnp.stack([grad_real, grad_imag])
    return (grad_field, grad_detail, grad_skip, grad_spectral)
```

```python
import functools
import math

import jax
import jax.numpy as jnp
from jax import lax
from jax.experimental import pallas as pl
from jax.experimental.pallas import tpu as pltpu
from jax.sharding import PartitionSpec as P

MESH = pl.DeviceIdType.MESH
HIGHEST = lax.Precision.HIGHEST
NN = (((1,), (0,)), ((), ()))
NT = (((1,), (1,)), ((), ()))
TN = (((0,), (0,)), ((), ()))


def enter_together(size):
    me = lax.axis_index("row")
    barrier = pltpu.get_barrier_semaphore()

    def greet(step, carry):
        pl.semaphore_signal(
            barrier, inc=1, device_id={"row": lax.rem(me + step, size)}, device_id_type=MESH
        )
        return carry

    lax.fori_loop(1, size, greet, 0)
    pl.semaphore_wait(barrier, size - 1)


def exchange(size, tile, send, land, send_sem, recv_sem):
    me = lax.axis_index("row")

    def copy(step, partner, place):
        return pltpu.make_async_remote_copy(
            src_ref=send.at[pl.ds(pl.multiple_of(partner * tile, tile), tile)],
            dst_ref=land.at[pl.ds(pl.multiple_of(place * tile, tile), tile)],
            send_sem=send_sem.at[step],
            recv_sem=recv_sem.at[step],
            device_id={"row": partner},
            device_id_type=MESH,
        )

    def start(step, carry):
        copy(step, lax.rem(me + step, size), me).start()
        return carry

    def finish(step, carry):
        source = lax.rem(me + size - step, size)
        copy(step, source, source).wait_recv()
        copy(step, lax.rem(me + step, size), me).wait_send()
        return carry

    lax.fori_loop(1, size, start, 0)
    own = pl.ds(pl.multiple_of(me * tile, tile), tile)
    land[own, :] = send[own, :]
    lax.fori_loop(1, size, finish, 0)


def spectral_kernel(
    size,
    near_cols,
    back,
    coarse_ref,
    col_ref,
    row_ref,
    row_inv_ref,
    col_inv_ref,
    weight_hbm,
    image_ref,
    spec_ref,
    weight,
    send_a,
    land_a,
    send_b,
    send_c,
    land_c,
    send_d,
    land_d,
    rotated,
    weight_sem,
    send_sem,
    recv_sem,
):
    fetch = pltpu.make_async_copy(weight_hbm, weight, weight_sem)
    fetch.start()
    enter_together(size)
    rows = coarse_ref.shape[0]
    total = None
    for row in range(rows):
        part = lax.dot_general(
            col_ref[row],
            coarse_ref[row].astype(jnp.float32),
            NT,
            precision=HIGHEST,
            preferred_element_type=jnp.float32,
        )
        total = part if total is None else total + part
    send_a[...] = total
    tile_a = send_a.shape[0] // size
    exchange(size, tile_a, send_a, land_a, send_sem.at[0], recv_sem.at[0])
    send_b[...] = lax.dot_general(
        row_ref[...], land_a[...], NN, precision=HIGHEST, preferred_element_type=jnp.float32
    )
    tile_b = send_b.shape[0] // size
    exchange(size, tile_b, send_b, spec_ref, send_sem.at[1], recv_sem.at[1])
    spec = spec_ref[...]
    count = spec.shape[0]
    even = lax.broadcasted_iota(jnp.int32, spec.shape, 0) % 2 == 0
    turned = jnp.where(even, -pltpu.roll(spec, count - 1, 0), pltpu.roll(spec, 1, 0))
    rotated[...] = -turned if back else turned
    fetch.wait()
    per_tile = tile_b // 2
    modes = weight.shape[1]
    per_row = near_cols
    mode_rows = per_tile // per_row
    dims = NT if back else NN

    def mix(source, carry):
        here = pl.ds(pl.multiple_of(source * tile_b, tile_b), tile_b)
        plain = spec_ref[here, :].astype(jnp.bfloat16)
        turn = rotated[here, :].astype(jnp.bfloat16)
        pair = lax.broadcasted_iota(jnp.int32, (tile_b, plain.shape[1]), 0) // 2
        result = jnp.zeros((tile_b, plain.shape[1]), jnp.float32)
        for member in range(per_tile):
            mode = (member // per_row) * (modes // mode_rows) + source * per_row + member % per_row
            one = lax.dot_general(
                plain,
                weight[0, mode].astype(jnp.bfloat16),
                dims,
                preferred_element_type=jnp.float32,
            )
            two = lax.dot_general(
                turn,
                weight[1, mode].astype(jnp.bfloat16),
                dims,
                preferred_element_type=jnp.float32,
            )
            result = jnp.where(pair == member, one + two, result)
        send_c[here, :] = result
        return carry

    lax.fori_loop(0, size, mix, 0)
    exchange(size, tile_b, send_c, land_c, send_sem.at[2], recv_sem.at[2])
    send_d[...] = lax.dot_general(
        row_inv_ref[...], land_c[...], NN, precision=HIGHEST, preferred_element_type=jnp.float32
    )
    exchange(size, tile_a, send_d, land_d, send_sem.at[3], recv_sem.at[3])
    across = land_d[...].T
    for row in range(rows):
        image_ref[row] = lax.dot_general(
            across, col_inv_ref[row], NN, precision=HIGHEST, preferred_element_type=jnp.float32
        ).astype(jnp.bfloat16)


def spectral_tables(row_modes, col_modes, local_rows, columns, size):
    height = local_rows * size
    mode_rows, mode_cols = row_modes.shape[0], col_modes.shape[0]
    near_rows, near_cols = mode_rows // size, mode_cols // size
    cos_col, sin_col = column_tables(col_modes, columns)
    cos_row, sin_row = row_tables(row_modes, jnp.arange(height, dtype=jnp.int32), height)
    same_row = jnp.eye(local_rows, dtype=jnp.float32)
    wave = jnp.stack([cos_col.T, -sin_col.T], axis=1).reshape(size, near_cols, 2, columns)
    col = jnp.einsum("hg,dmrw->gdhmrw", same_row, wave).reshape(local_rows, -1, columns)
    col_inv = col
    turn = jnp.stack(
        [jnp.stack([cos_row, sin_row], axis=-1), jnp.stack([-sin_row, cos_row], axis=-1)], axis=2
    )
    same_col = jnp.eye(near_cols, dtype=jnp.float32)
    row = jnp.einsum("phrs,mn->pmrhns", turn, same_col)
    row = row.reshape(mode_rows * near_cols * 2, height * near_cols * 2)
    row_inv = row.T * (1.0 / (height * columns))
    return col, row, row_inv, col_inv


def spectral_path(coarse, weight, tables, near_cols, back):
    col, row, row_inv, col_inv = tables
    size = lax.axis_size("row")
    local_rows, channels, columns = coarse.shape
    count_a, count_b = col.shape[1], row.shape[0]
    f32 = jnp.float32
    vmem = pl.BlockSpec(memory_space=pltpu.VMEM)
    image, spec = pl.pallas_call(
        functools.partial(spectral_kernel, size, near_cols, back),
        out_shape=(
            jax.ShapeDtypeStruct(coarse.shape, jnp.bfloat16),
            jax.ShapeDtypeStruct((count_b, channels), f32),
        ),
        in_specs=[vmem] * 5 + [pl.BlockSpec(memory_space=pl.ANY)],
        out_specs=(vmem, vmem),
        scratch_shapes=[
            pltpu.VMEM(weight.shape, f32),
            pltpu.VMEM((count_a, channels), f32),
            pltpu.VMEM((count_a, channels), f32),
            pltpu.VMEM((count_b, channels), f32),
            pltpu.VMEM((count_b, channels), f32),
            pltpu.VMEM((count_b, channels), f32),
            pltpu.VMEM((count_a, channels), f32),
            pltpu.VMEM((count_a, channels), f32),
            pltpu.VMEM((count_b, channels), f32),
            pltpu.SemaphoreType.DMA,
            pltpu.SemaphoreType.DMA((4, size)),
            pltpu.SemaphoreType.DMA((4, size)),
        ],
        compiler_params=pltpu.CompilerParams(
            collective_id=1 if back else 0,
            has_side_effects=True,
            vmem_limit_bytes=40 * 1024 * 1024,
        ),
        cost_estimate=pl.CostEstimate(
            flops=8 * weight.size, bytes_accessed=4 * weight.size, transcendentals=0
        ),
        name="spectral_back" if back else "spectral",
    )(coarse, col, row, row_inv, col_inv, weight)
    return image, spec


def spec_parts(spec, mode_rows, mode_cols, size):
    channels = spec.shape[1]
    grid = spec.reshape(size, mode_rows // size, mode_cols // size, 2, channels)
    grid = jnp.transpose(grid, (3, 1, 0, 2, 4)).reshape(2, -1, channels)
    return grid[0], grid[1]


def shifted(shard, axis, by):
    size = lax.axis_size(axis)
    return lax.ppermute(shard, axis, [(i, (i + by) % size) for i in range(size)])


def as_float(values):
    return values.astype(jnp.float32)


def precise(form, first_in, second_in):
    return jnp.einsum(form, first_in, second_in, precision=lax.Precision.HIGHEST)


def narrow(form, first_in, second_in):
    return jnp.einsum(form, first_in, second_in, preferred_element_type=jnp.float32)


def column_tables(col_modes, length):
    positions = jnp.arange(length, dtype=jnp.int32)
    turns = positions[:, None] * col_modes[None, :] % length
    angles = turns.astype(jnp.float32) * (2.0 * math.pi / length)
    return (jnp.cos(angles), jnp.sin(angles))


def row_tables(row_modes, positions, length):
    turns = row_modes[:, None] * positions[None, :] % length
    angles = turns.astype(jnp.float32) * (2.0 * math.pi / length)
    return (jnp.cos(angles), jnp.sin(angles))


def row_pass(values, row_filters):
    incoming = shifted(values[:2], "row", -1)
    spread = as_float(jnp.concatenate([values, incoming], axis=0))
    row_count = values.shape[0]
    outputs = []
    for branch in range(2):
        running = row_filters[branch, 0] * spread[0:row_count:2]
        for offset in range(1, 4):
            running = (
                running + row_filters[branch, offset] * spread[offset : offset + row_count : 2]
            )
        outputs.append(running.astype(jnp.bfloat16))
    return (outputs[0], outputs[1])


def analysis(values, row_filters, matrices):
    band_list = []
    current = values
    for matrix in matrices:
        low_rows, high_rows = row_pass(current, row_filters)
        low_cols = narrow("hcw,wv->hcv", low_rows, matrix).astype(jnp.bfloat16)
        high_cols = narrow("hcw,wv->hcv", high_rows, matrix).astype(jnp.bfloat16)
        halfway = low_cols.shape[2] // 2
        current = low_cols[:, :, :halfway]
        band_list.append(
            (low_cols[:, :, halfway:], high_cols[:, :, :halfway], high_cols[:, :, halfway:])
        )
    return (current, band_list)


def combine_rows(low_now, high_now, low_prev, high_prev, row_filters):
    parities = []
    for parity in range(2):
        running = row_filters[0, parity] * low_now + row_filters[1, parity] * high_now
        running = running + row_filters[0, parity + 2] * low_prev
        running = running + row_filters[1, parity + 2] * high_prev
        parities.append(running)
    stacked = jnp.stack(parities, axis=1)
    return stacked.reshape((2 * low_now.shape[0],) + low_now.shape[1:])


def synthesis(top_array, band_list, row_filters, matrices):
    current = top_array
    for octave in (2, 1, 0):
        band_one, band_two, band_three = band_list[octave]
        low_sum = narrow(
            "hcv,wv->hcw", jnp.concatenate([current, band_one], axis=2), matrices[octave]
        ).astype(jnp.bfloat16)
        high_sum = narrow(
            "hcv,wv->hcw", jnp.concatenate([band_two, band_three], axis=2), matrices[octave]
        ).astype(jnp.bfloat16)
        edges = jnp.concatenate([low_sum[-1:], high_sum[-1:]], axis=0)
        earlier = shifted(edges, "row", 1)
        low_prev = jnp.concatenate([earlier[0:1], low_sum[:-1]], axis=0)
        high_prev = jnp.concatenate([earlier[1:2], high_sum[:-1]], axis=0)
        current = combine_rows(
            as_float(low_sum),
            as_float(high_sum),
            as_float(low_prev),
            as_float(high_prev),
            row_filters,
        )
        if octave > 0:
            current = current.astype(jnp.bfloat16)
    return current


def owned_modes(coarse, row_modes, col_modes):
    local_rows, channels, columns = coarse.shape
    devices = lax.axis_size("row")
    height = local_rows * devices
    cos_col, sin_col = column_tables(col_modes, columns)
    values = as_float(coarse)
    real_one = precise("hcw,wm->hcm", values, cos_col)
    imag_one = -precise("hcw,wm->hcm", values, sin_col)
    positions = lax.axis_index("row") * local_rows + jnp.arange(local_rows, dtype=jnp.int32)
    cos_row, sin_row = row_tables(row_modes, positions, height)
    real_two = precise("ph,hcm->pmc", cos_row, real_one) + precise("ph,hcm->pmc", sin_row, imag_one)
    imag_two = precise("ph,hcm->pmc", cos_row, imag_one) - precise("ph,hcm->pmc", sin_row, real_one)
    term_all = jnp.stack([real_two.reshape(-1, channels), imag_two.reshape(-1, channels)], axis=1)
    owned = lax.psum_scatter(term_all, "row", scatter_dimension=0, tiled=True)
    return (owned[:, 0], owned[:, 1])


def owned_image(real_owned, imag_owned, row_modes, col_modes, local_rows, columns):
    devices = lax.axis_size("row")
    height = local_rows * devices
    mode_rows = row_modes.shape[0]
    mode_cols = col_modes.shape[0]
    positions = lax.axis_index("row") * local_rows + jnp.arange(local_rows, dtype=jnp.int32)
    real_piece = lax.all_gather(real_owned, "row", axis=0, tiled=True)
    imag_piece = lax.all_gather(imag_owned, "row", axis=0, tiled=True)
    piece_rows = real_piece.shape[0]
    flat = jnp.arange(piece_rows, dtype=jnp.int32)
    row_pick = (flat // mode_cols)[:, None] == jnp.arange(mode_rows, dtype=jnp.int32)[None, :]
    frequency = jnp.sum(jnp.where(row_pick, row_modes[None, :], 0), axis=1)
    column_pick = (
        (flat % mode_cols)[:, None] == jnp.arange(mode_cols, dtype=jnp.int32)[None, :]
    ).astype(jnp.float32)
    turns = positions[:, None] * frequency[None, :] % height
    angles = turns.astype(jnp.float32) * (2.0 * math.pi / height)
    cos_part = jnp.cos(angles)
    sin_part = jnp.sin(angles)
    cos_pick = cos_part[:, :, None] * column_pick[None, :, :]
    sin_pick = sin_part[:, :, None] * column_pick[None, :, :]
    real_sum = precise("hnm,nc->hcm", cos_pick, real_piece) - precise(
        "hnm,nc->hcm", sin_pick, imag_piece
    )
    imag_sum = precise("hnm,nc->hcm", cos_pick, imag_piece) + precise(
        "hnm,nc->hcm", sin_pick, real_piece
    )
    cos_col, sin_col = column_tables(col_modes, columns)
    image = precise("hcm,wm->hcw", real_sum, cos_col) - precise("hcm,wm->hcw", imag_sum, sin_col)
    return image.astype(jnp.bfloat16)


def mix_modes(real_in, imag_in, weight_real, weight_imag, factor):
    real_out = (
        precise("nc,nco->no", real_in, weight_real) - precise("nc,nco->no", imag_in, weight_imag)
    ) * factor
    imag_out = (
        precise("nc,nco->no", real_in, weight_imag) + precise("nc,nco->no", imag_in, weight_real)
    ) * factor
    return (real_out, imag_out)


def mix_modes_back(real_in, imag_in, weight_real, weight_imag, factor):
    real_out = (
        precise("no,nco->nc", real_in, weight_real) + precise("no,nco->nc", imag_in, weight_imag)
    ) * factor
    imag_out = (
        precise("no,nco->nc", imag_in, weight_real) - precise("no,nco->nc", real_in, weight_imag)
    ) * factor
    return (real_out, imag_out)


def per_device(
    field,
    cotangent,
    row_filters,
    col_filter_1,
    col_filter_2,
    col_filter_3,
    detail_weight,
    skip_weight,
    spectral_weight,
    row_modes,
    col_modes,
):
    matrices = (col_filter_1, col_filter_2, col_filter_3)
    devices = lax.axis_size("row")
    coarse_field, bands_field = analysis(field, row_filters, matrices)
    local_rows, channels, columns = coarse_field.shape
    height = local_rows * devices
    factor = 1.0 / (height * columns)
    weight_real = spectral_weight[0]
    weight_imag = spectral_weight[1]
    mode_rows, mode_cols = row_modes.shape[0], col_modes.shape[0]
    whole_tiles = (
        mode_rows % devices == 0
        and mode_cols % devices == 0
        and (2 * local_rows * mode_cols // devices) % 8 == 0
        and (2 * (mode_rows // devices) * (mode_cols // devices)) % 8 == 0
    )
    if whole_tiles:
        near_cols = mode_cols // devices
        tables = spectral_tables(row_modes, col_modes, local_rows, columns, devices)
        coarse_image, spec = spectral_path(coarse_field, spectral_weight, tables, near_cols, False)
        spec_real, spec_imag = spec_parts(spec, mode_rows, mode_cols, devices)
    else:
        spec_real, spec_imag = owned_modes(coarse_field, row_modes, col_modes)
        out_real, out_imag = mix_modes(spec_real, spec_imag, weight_real, weight_imag, factor)
        coarse_image = owned_image(out_real, out_imag, row_modes, col_modes, local_rows, columns)
    mixed_field = [
        tuple(
            (
                narrow(
                    "hcw,co->how", bands_field[octave][member], detail_weight[octave, member]
                ).astype(jnp.bfloat16)
                for member in range(3)
            )
        )
        for octave in range(3)
    ]
    rebuilt_field = synthesis(coarse_image, mixed_field, row_filters, matrices)
    activation_in = rebuilt_field + narrow("hcw,co->how", field, skip_weight)
    upstream = jax.vjp(jax.nn.gelu, activation_in)[1](as_float(cotangent))[0].astype(jnp.bfloat16)
    coarse_slope, bands_slope = analysis(upstream, row_filters, matrices)
    if whole_tiles:
        image_back, spec = spectral_path(coarse_slope, spectral_weight, tables, near_cols, True)
        back_real, back_imag = spec_parts(spec, mode_rows, mode_cols, devices)
    else:
        back_real, back_imag = owned_modes(coarse_slope, row_modes, col_modes)
        turned_real, turned_imag = mix_modes_back(
            back_real, back_imag, weight_real, weight_imag, factor
        )
        image_back = owned_image(
            turned_real, turned_imag, row_modes, col_modes, local_rows, columns
        )
    back_bands = [
        tuple(
            (
                narrow(
                    "how,co->hcw", bands_slope[octave][member], detail_weight[octave, member]
                ).astype(jnp.bfloat16)
                for member in range(3)
            )
        )
        for octave in range(3)
    ]
    rebuilt_slope = synthesis(image_back, back_bands, row_filters, matrices)
    grad_field = rebuilt_slope + narrow("how,co->hcw", upstream, skip_weight)
    skip_local = narrow("hcw,how->co", field, upstream)
    detail_local = jnp.stack(
        [
            jnp.stack(
                [
                    narrow("hcw,how->co", bands_field[octave][member], bands_slope[octave][member])
                    for member in range(3)
                ]
            )
            for octave in range(3)
        ]
    )
    skip_total, detail_total = lax.psum((skip_local, detail_local), "row")
    total_rows = field.shape[0] * devices
    total_cols = field.shape[2]
    grad_skip = skip_total / math.sqrt(total_rows * total_cols)
    divisors = jnp.array(
        [
            [
                math.sqrt((total_rows >> octave + 1) * (total_cols >> octave + 1))
                for member in range(3)
            ]
            for octave in range(3)
        ],
        jnp.float32,
    )
    grad_detail = detail_total / divisors[:, :, None, None]
    grad_real = (
        spec_real[:, :, None] * back_real[:, None, :]
        + spec_imag[:, :, None] * back_imag[:, None, :]
    ) * factor
    grad_imag = (
        spec_real[:, :, None] * back_imag[:, None, :]
        - spec_imag[:, :, None] * back_real[:, None, :]
    ) * factor
    grad_spectral = jnp.stack([grad_real, grad_imag])
    return (grad_field, grad_detail, grad_skip, grad_spectral)


def solution(mesh):
    placed = (
        P(("groups", "row"), None, None),
        P(("groups", "row"), None, None),
        P(),
        P(),
        P(),
        P(),
        P(),
        P(),
        P(None, "row", None, None),
        P(),
        P(),
    )
    return jax.shard_map(
        per_device,
        mesh=mesh,
        in_specs=placed,
        out_specs=(
            P(("groups", "row"), None, None),
            P("groups", None, None, None),
            P("groups", None),
            P("groups", "row", None, None),
        ),
        check_vma=False,
    )
```

```python
import functools
import math

import jax
import jax.numpy as jnp
from jax import lax
from jax.experimental import pallas as pl
from jax.experimental.pallas import tpu as pltpu
from jax.sharding import PartitionSpec as P

MESH = pl.DeviceIdType.MESH
HIGHEST = lax.Precision.HIGHEST
NN = (((1,), (0,)), ((), ()))
NT = (((1,), (1,)), ((), ()))
TN = (((0,), (0,)), ((), ()))


def enter_together(size):
    me = lax.axis_index("row")
    barrier = pltpu.get_barrier_semaphore()

    def greet(step, carry):
        pl.semaphore_signal(
            barrier, inc=1, device_id={"row": lax.rem(me + step, size)}, device_id_type=MESH
        )
        return carry

    lax.fori_loop(1, size, greet, 0)
    pl.semaphore_wait(barrier, size - 1)


def exchange(size, tile, send, land, send_sem, recv_sem):
    me = lax.axis_index("row")

    def copy(step, partner, place):
        return pltpu.make_async_remote_copy(
            src_ref=send.at[pl.ds(pl.multiple_of(partner * tile, tile), tile)],
            dst_ref=land.at[pl.ds(pl.multiple_of(place * tile, tile), tile)],
            send_sem=send_sem.at[step],
            recv_sem=recv_sem.at[step],
            device_id={"row": partner},
            device_id_type=MESH,
        )

    def start(step, carry):
        copy(step, lax.rem(me + step, size), me).start()
        return carry

    def finish(step, carry):
        source = lax.rem(me + size - step, size)
        copy(step, source, source).wait_recv()
        copy(step, lax.rem(me + step, size), me).wait_send()
        return carry

    lax.fori_loop(1, size, start, 0)
    own = pl.ds(pl.multiple_of(me * tile, tile), tile)
    land[own, :] = send[own, :]
    lax.fori_loop(1, size, finish, 0)


def spectral_kernel(
    size,
    near_cols,
    back,
    coarse_ref,
    col_ref,
    row_ref,
    row_inv_ref,
    col_inv_ref,
    weight_hbm,
    image_ref,
    spec_ref,
    weight,
    send_a,
    land_a,
    send_b,
    send_c,
    land_c,
    send_d,
    land_d,
    rotated,
    weight_sem,
    send_sem,
    recv_sem,
):
    fetch = pltpu.make_async_copy(weight_hbm, weight, weight_sem)
    fetch.start()
    enter_together(size)
    rows = coarse_ref.shape[1]
    total = None
    for row in range(rows):
        part = lax.dot_general(
            col_ref[row],
            coarse_ref[0, row].astype(jnp.float32),
            NT,
            precision=HIGHEST,
            preferred_element_type=jnp.float32,
        )
        total = part if total is None else total + part
    send_a[...] = total
    tile_a = send_a.shape[0] // size
    exchange(size, tile_a, send_a, land_a, send_sem.at[0], recv_sem.at[0])
    send_b[...] = lax.dot_general(
        row_ref[...], land_a[...], NN, precision=HIGHEST, preferred_element_type=jnp.float32
    )
    tile_b = send_b.shape[0] // size
    exchange(size, tile_b, send_b, spec_ref, send_sem.at[1], recv_sem.at[1])
    spec = spec_ref[...]
    count = spec.shape[0]
    even = lax.broadcasted_iota(jnp.int32, spec.shape, 0) % 2 == 0
    turned = jnp.where(even, -pltpu.roll(spec, count - 1, 0), pltpu.roll(spec, 1, 0))
    rotated[...] = -turned if back else turned
    fetch.wait()
    per_tile = tile_b // 2
    modes = weight.shape[1]
    per_row = near_cols
    mode_rows = per_tile // per_row
    dims = NT if back else NN

    def mix(source, carry):
        here = pl.ds(pl.multiple_of(source * tile_b, tile_b), tile_b)
        plain = spec_ref[here, :].astype(jnp.bfloat16)
        turn = rotated[here, :].astype(jnp.bfloat16)
        pair = lax.broadcasted_iota(jnp.int32, (tile_b, plain.shape[1]), 0) // 2
        result = jnp.zeros((tile_b, plain.shape[1]), jnp.float32)
        for member in range(per_tile):
            mode = (member // per_row) * (modes // mode_rows) + source * per_row + member % per_row
            one = lax.dot_general(
                plain,
                weight[0, mode].astype(jnp.bfloat16),
                dims,
                preferred_element_type=jnp.float32,
            )
            two = lax.dot_general(
                turn,
                weight[1, mode].astype(jnp.bfloat16),
                dims,
                preferred_element_type=jnp.float32,
            )
            result = jnp.where(pair == member, one + two, result)
        send_c[here, :] = result
        return carry

    lax.fori_loop(0, size, mix, 0)
    exchange(size, tile_b, send_c, land_c, send_sem.at[2], recv_sem.at[2])
    send_d[...] = lax.dot_general(
        row_inv_ref[...], land_c[...], NN, precision=HIGHEST, preferred_element_type=jnp.float32
    )
    exchange(size, tile_a, send_d, land_d, send_sem.at[3], recv_sem.at[3])
    across = land_d[...].T
    for row in range(rows):
        image_ref[row] = lax.dot_general(
            across, col_inv_ref[row], NN, precision=HIGHEST, preferred_element_type=jnp.float32
        ).astype(jnp.bfloat16)


def spectral_tables(row_modes, col_modes, local_rows, columns, size):
    height = local_rows * size
    mode_rows, mode_cols = row_modes.shape[0], col_modes.shape[0]
    near_rows, near_cols = mode_rows // size, mode_cols // size
    cos_col, sin_col = column_tables(col_modes, columns)
    cos_row, sin_row = row_tables(row_modes, jnp.arange(height, dtype=jnp.int32), height)
    same_row = jnp.eye(local_rows, dtype=jnp.float32)
    wave = jnp.stack([cos_col.T, -sin_col.T], axis=1).reshape(size, near_cols, 2, columns)
    col = jnp.einsum("hg,dmrw->gdhmrw", same_row, wave).reshape(local_rows, -1, columns)
    col = jnp.pad(col, ((0, 0), (0, 0), (0, columns)))
    col_inv = col
    turn = jnp.stack(
        [jnp.stack([cos_row, sin_row], axis=-1), jnp.stack([-sin_row, cos_row], axis=-1)], axis=2
    )
    same_col = jnp.eye(near_cols, dtype=jnp.float32)
    row = jnp.einsum("phrs,mn->pmrhns", turn, same_col)
    row = row.reshape(mode_rows * near_cols * 2, height * near_cols * 2)
    row_inv = row.T * (1.0 / (height * columns))
    return col, row, row_inv, col_inv


def spectral_path(coarse, weight, tables, near_cols, back):
    col, row, row_inv, col_inv = tables
    size = lax.axis_size("row")
    channels = coarse.shape[2]
    count_a, count_b = col.shape[1], row.shape[0]
    f32 = jnp.float32
    vmem = pl.BlockSpec(memory_space=pltpu.VMEM)
    image, spec = pl.pallas_call(
        functools.partial(spectral_kernel, size, near_cols, back),
        out_shape=(
            jax.ShapeDtypeStruct(coarse.shape[1:], jnp.bfloat16),
            jax.ShapeDtypeStruct((count_b, channels), f32),
        ),
        in_specs=[vmem] * 5 + [pl.BlockSpec(memory_space=pl.ANY)],
        out_specs=(vmem, vmem),
        scratch_shapes=[
            pltpu.VMEM(weight.shape, f32),
            pltpu.VMEM((count_a, channels), f32),
            pltpu.VMEM((count_a, channels), f32),
            pltpu.VMEM((count_b, channels), f32),
            pltpu.VMEM((count_b, channels), f32),
            pltpu.VMEM((count_b, channels), f32),
            pltpu.VMEM((count_a, channels), f32),
            pltpu.VMEM((count_a, channels), f32),
            pltpu.VMEM((count_b, channels), f32),
            pltpu.SemaphoreType.DMA,
            pltpu.SemaphoreType.DMA((4, size)),
            pltpu.SemaphoreType.DMA((4, size)),
        ],
        compiler_params=pltpu.CompilerParams(
            collective_id=1 if back else 0,
            has_side_effects=True,
            vmem_limit_bytes=40 * 1024 * 1024,
        ),
        cost_estimate=pl.CostEstimate(
            flops=8 * weight.size, bytes_accessed=4 * weight.size, transcendentals=0
        ),
        name="spectral_back" if back else "spectral",
    )(coarse, col, row, row_inv, col_inv, weight)
    return image, spec


def spec_parts(spec, mode_rows, mode_cols, size):
    channels = spec.shape[1]
    grid = spec.reshape(size, mode_rows // size, mode_cols // size, 2, channels)
    grid = jnp.transpose(grid, (3, 1, 0, 2, 4)).reshape(2, -1, channels)
    return grid[0], grid[1]


def as_float(values):
    return values.astype(jnp.float32)


def precise(form, first_in, second_in):
    return jnp.einsum(form, first_in, second_in, precision=lax.Precision.HIGHEST)


def narrow(form, first_in, second_in):
    return jnp.einsum(form, first_in, second_in, preferred_element_type=jnp.float32)


def column_tables(col_modes, length):
    positions = jnp.arange(length, dtype=jnp.int32)
    turns = positions[:, None] * col_modes[None, :] % length
    angles = turns.astype(jnp.float32) * (2.0 * math.pi / length)
    return (jnp.cos(angles), jnp.sin(angles))


def row_tables(row_modes, positions, length):
    turns = row_modes[:, None] * positions[None, :] % length
    angles = turns.astype(jnp.float32) * (2.0 * math.pi / length)
    return (jnp.cos(angles), jnp.sin(angles))


def owned_modes(coarse, row_modes, col_modes):
    local_rows, channels, columns = coarse.shape
    devices = lax.axis_size("row")
    height = local_rows * devices
    cos_col, sin_col = column_tables(col_modes, columns)
    values = as_float(coarse)
    real_one = precise("hcw,wm->hcm", values, cos_col)
    imag_one = -precise("hcw,wm->hcm", values, sin_col)
    positions = lax.axis_index("row") * local_rows + jnp.arange(local_rows, dtype=jnp.int32)
    cos_row, sin_row = row_tables(row_modes, positions, height)
    real_two = precise("ph,hcm->pmc", cos_row, real_one) + precise("ph,hcm->pmc", sin_row, imag_one)
    imag_two = precise("ph,hcm->pmc", cos_row, imag_one) - precise("ph,hcm->pmc", sin_row, real_one)
    term_all = jnp.stack([real_two.reshape(-1, channels), imag_two.reshape(-1, channels)], axis=1)
    owned = lax.psum_scatter(term_all, "row", scatter_dimension=0, tiled=True)
    return (owned[:, 0], owned[:, 1])


def owned_image(real_owned, imag_owned, row_modes, col_modes, local_rows, columns):
    devices = lax.axis_size("row")
    height = local_rows * devices
    mode_rows = row_modes.shape[0]
    mode_cols = col_modes.shape[0]
    positions = lax.axis_index("row") * local_rows + jnp.arange(local_rows, dtype=jnp.int32)
    real_piece = lax.all_gather(real_owned, "row", axis=0, tiled=True)
    imag_piece = lax.all_gather(imag_owned, "row", axis=0, tiled=True)
    piece_rows = real_piece.shape[0]
    flat = jnp.arange(piece_rows, dtype=jnp.int32)
    row_pick = (flat // mode_cols)[:, None] == jnp.arange(mode_rows, dtype=jnp.int32)[None, :]
    frequency = jnp.sum(jnp.where(row_pick, row_modes[None, :], 0), axis=1)
    column_pick = (
        (flat % mode_cols)[:, None] == jnp.arange(mode_cols, dtype=jnp.int32)[None, :]
    ).astype(jnp.float32)
    turns = positions[:, None] * frequency[None, :] % height
    angles = turns.astype(jnp.float32) * (2.0 * math.pi / height)
    cos_part = jnp.cos(angles)
    sin_part = jnp.sin(angles)
    cos_pick = cos_part[:, :, None] * column_pick[None, :, :]
    sin_pick = sin_part[:, :, None] * column_pick[None, :, :]
    real_sum = precise("hnm,nc->hcm", cos_pick, real_piece) - precise(
        "hnm,nc->hcm", sin_pick, imag_piece
    )
    imag_sum = precise("hnm,nc->hcm", cos_pick, imag_piece) + precise(
        "hnm,nc->hcm", sin_pick, real_piece
    )
    cos_col, sin_col = column_tables(col_modes, columns)
    image = precise("hcm,wm->hcw", real_sum, cos_col) - precise("hcm,wm->hcw", imag_sum, sin_col)
    return image.astype(jnp.bfloat16)


def mix_modes(real_in, imag_in, weight_real, weight_imag, factor):
    real_out = (
        precise("nc,nco->no", real_in, weight_real) - precise("nc,nco->no", imag_in, weight_imag)
    ) * factor
    imag_out = (
        precise("nc,nco->no", real_in, weight_imag) + precise("nc,nco->no", imag_in, weight_real)
    ) * factor
    return (real_out, imag_out)


def mix_modes_back(real_in, imag_in, weight_real, weight_imag, factor):
    real_out = (
        precise("no,nco->nc", real_in, weight_real) + precise("no,nco->nc", imag_in, weight_imag)
    ) * factor
    imag_out = (
        precise("no,nco->nc", imag_in, weight_real) - precise("no,nco->nc", real_in, weight_imag)
    ) * factor
    return (real_out, imag_out)


def greet_ring(receives_from):
    barrier = pltpu.get_barrier_semaphore()
    pl.semaphore_signal(barrier, inc=1, device_id={"row": receives_from}, device_id_type=MESH)
    pl.semaphore_wait(barrier, 1)


def analysis_kernel(
    size,
    values,
    taps,
    filter_1,
    filter_2,
    filter_3,
    out_1,
    out_2,
    out_3,
    halo_1,
    halo_2,
    halo_3,
    send_sem,
    recv_sem,
):
    me = lax.axis_index("row")
    above, below = lax.rem(me + size - 1, size), lax.rem(me + 1, size)
    greet_ring(below)

    def copy(level, source, halo):
        return pltpu.make_async_remote_copy(
            src_ref=source,
            dst_ref=halo,
            send_sem=send_sem.at[level],
            recv_sem=recv_sem.at[level],
            device_id={"row": above},
            device_id_type=MESH,
        )

    def one(get, row, matrix, out):
        loaded = [as_float(get(2 * row + offset)) for offset in range(4)]
        halves = []
        for branch in range(2):
            running = taps[branch, 0] * loaded[0]
            for offset in range(1, 4):
                running = running + taps[branch, offset] * loaded[offset]
            halves.append(running.astype(jnp.bfloat16))
        both = jnp.concatenate(halves, axis=0)
        done = jnp.dot(both, matrix[...], preferred_element_type=jnp.float32).astype(jnp.bfloat16)
        count = halves[0].shape[0]
        out[0, row] = done[:count]
        out[1, row] = done[count:]

    def span(get, first, last, matrix, out):
        def body(row, carry):
            one(get, row, matrix, out)
            return carry

        lax.fori_loop(first, last, body, 0)

    def edged(get, halo, count):
        return lambda row: get(row) if row < count else halo[row - count]

    count = values.shape[0]
    half_1, half_2 = filter_1.shape[0] // 2, filter_2.shape[0] // 2
    get_1 = lambda row: values[row]
    get_2 = lambda row: out_1[0, row, :, :half_1]
    get_3 = lambda row: out_2[0, row, :, :half_2]
    first = copy(0, values.at[pl.ds(0, 2)], halo_1)
    first.start()
    span(get_1, 0, 2, filter_1, out_1)
    second = copy(1, out_1.at[0, pl.ds(0, 2), :, pl.ds(0, half_1)], halo_2)
    second.start()
    early = min(6, count // 2 - 1)
    span(get_1, 2, early, filter_1, out_1)
    span(get_2, 0, 2, filter_2, out_2)
    third = copy(2, out_2.at[0, pl.ds(0, 2), :, pl.ds(0, half_2)], halo_3)
    third.start()
    span(get_1, early, count // 2 - 1, filter_1, out_1)
    first.wait()
    one(edged(get_1, halo_1, count), count // 2 - 1, filter_1, out_1)
    span(get_2, 2, count // 4 - 1, filter_2, out_2)
    second.wait()
    one(edged(get_2, halo_2, count // 2), count // 4 - 1, filter_2, out_2)
    span(get_3, 0, count // 8 - 1, filter_3, out_3)
    third.wait()
    one(edged(get_3, halo_3, count // 4), count // 8 - 1, filter_3, out_3)


def analysis_call(values, row_filters, matrices, back):
    size = lax.axis_size("row")
    count, channels, columns = values.shape
    vmem = pl.BlockSpec(memory_space=pltpu.VMEM)
    widths = [columns >> level for level in range(3)]
    return pl.pallas_call(
        functools.partial(analysis_kernel, size),
        out_shape=tuple(
            jax.ShapeDtypeStruct((2, count >> level + 1, channels, widths[level]), jnp.bfloat16)
            for level in range(3)
        ),
        in_specs=[vmem, pl.BlockSpec(memory_space=pltpu.SMEM), vmem, vmem, vmem],
        out_specs=(vmem, vmem, vmem),
        scratch_shapes=[
            *(pltpu.VMEM((2, channels, width), jnp.bfloat16) for width in widths),
            pltpu.SemaphoreType.DMA((3,)),
            pltpu.SemaphoreType.DMA((3,)),
        ],
        compiler_params=pltpu.CompilerParams(
            collective_id=3 if back else 2,
            has_side_effects=True,
            vmem_limit_bytes=40 * 1024 * 1024,
        ),
        name="analysis_back" if back else "analysis",
    )(values, row_filters, *matrices)


def gelu_slope(value):
    scale = math.sqrt(2.0 / math.pi)
    square = value * value
    bend = jnp.tanh(scale * (value + 0.044715 * (square * value)))
    return 0.5 * (1.0 + bend) + 0.5 * value * (1.0 - bend * bend) * (
        scale * (1.0 + 3 * 0.044715 * square)
    )


def synthesis_kernel(
    size,
    back,
    image,
    out_1,
    out_2,
    out_3,
    taps,
    turned_1,
    turned_2,
    turned_3,
    detail,
    skip,
    plain,
    *rest,
):
    if back:
        result, *rest = rest
    else:
        cotangent, result, *rest = rest
    syn_1, syn_2, syn_3, halo_1, halo_2, halo_3, top_1, top_2, send_sem, recv_sem = rest
    me = lax.axis_index("row")
    above, below = lax.rem(me + size - 1, size), lax.rem(me + 1, size)
    greet_ring(above)

    def copy(level, syn, halo):
        return pltpu.make_async_remote_copy(
            src_ref=syn.at[:, syn.shape[1] - 1],
            dst_ref=halo,
            send_sem=send_sem.at[level],
            recv_sem=recv_sem.at[level],
            device_id={"row": below},
            device_id_type=MESH,
        )

    def mixed(level, member, band):
        return jnp.dot(detail[level, member], band, preferred_element_type=jnp.float32).astype(
            jnp.bfloat16
        )

    def one(level, row, top, out, turned, syn):
        half = out.shape[3] // 2
        if half % 128 == 0:
            low = [top[row], mixed(level, 0, out[0, row, :, half:])]
            high = [mixed(level, 1, out[1, row, :, :half]), mixed(level, 2, out[1, row, :, half:])]
            low, high = jnp.concatenate(low, axis=1), jnp.concatenate(high, axis=1)
        else:
            bands, lower = out[1, row], lax.broadcasted_iota(jnp.int32, out.shape[2:], 1) < half
            low = jnp.where(lower, as_float(top[row]), as_float(mixed(level, 0, out[0, row])))
            high = jnp.where(
                lower, as_float(mixed(level, 1, bands)), as_float(mixed(level, 2, bands))
            )
            low, high = low.astype(jnp.bfloat16), high.astype(jnp.bfloat16)
        both = jnp.concatenate([low, high], axis=0)
        done = jnp.dot(both, turned[...], preferred_element_type=jnp.float32).astype(jnp.bfloat16)
        count = low.shape[0]
        syn[0, row] = done[:count]
        syn[1, row] = done[count:]

    def joined(syn, row, previous):
        low_now, high_now = as_float(syn[0, row]), as_float(syn[1, row])
        low_prev, high_prev = as_float(previous(0)), as_float(previous(1))
        pair = []
        for parity in range(2):
            running = taps[0, parity] * low_now + taps[1, parity] * high_now
            running = running + taps[0, parity + 2] * low_prev
            pair.append(running + taps[1, parity + 2] * high_prev)
        return pair

    def combine(syn, row, halo, top):
        previous = (lambda part: halo[part]) if halo is not None else lambda part: syn[part, row - 1]
        pair = joined(syn, row, previous)
        for parity in range(2):
            top[2 * row + parity] = pair[parity].astype(jnp.bfloat16)

    def last(row, halo):
        previous = (
            (lambda part: halo[part]) if halo is not None else lambda part: syn_1[part, row - 1]
        )
        pair = joined(syn_1, row, previous)
        for parity in range(2):
            here = 2 * row + parity
            value = pair[parity] + jnp.dot(
                skip[...], plain[here], preferred_element_type=jnp.float32
            )
            if not back:
                value = (as_float(cotangent[here]) * gelu_slope(value)).astype(jnp.bfloat16)
            result[here] = value

    def span(first, stop, call):
        def body(row, carry):
            call(row)
            return carry

        lax.fori_loop(first, stop, body, 0)

    level_3 = lambda row: one(2, row, image, out_3, turned_3, syn_3)
    level_2 = lambda row: one(1, row, top_2, out_2, turned_2, syn_2)
    level_1 = lambda row: one(0, row, top_1, out_1, turned_1, syn_1)
    rows_3, rows_2, rows_1 = syn_3.shape[1], syn_2.shape[1], syn_1.shape[1]
    level_3(rows_3 - 1)
    third = copy(2, syn_3, halo_3)
    third.start()
    span(0, rows_3 - 1, level_3)
    combine(syn_3, rows_3 - 1, None, top_2)
    level_2(rows_2 - 1)
    second = copy(1, syn_2, halo_2)
    second.start()
    level_2(rows_2 - 2)
    combine(syn_2, rows_2 - 1, None, top_1)
    level_1(rows_1 - 1)
    first = copy(0, syn_1, halo_1)
    first.start()
    level_1(rows_1 - 2)
    last(rows_1 - 1, None)
    span(1, rows_3 - 1, lambda row: combine(syn_3, row, None, top_2))
    third.wait()
    combine(syn_3, 0, halo_3, top_2)
    span(0, rows_2 - 2, level_2)
    span(1, rows_2 - 1, lambda row: combine(syn_2, row, None, top_1))
    span(2, rows_1 - 2, level_1)
    span(3, rows_1 - 1, lambda row: last(row, None))
    second.wait()
    combine(syn_2, 0, halo_2, top_1)
    span(0, 2, level_1)
    span(1, 3, lambda row: last(row, None))
    first.wait()
    last(0, halo_1)


def synthesis_call(image, bands, row_filters, turned, detail, skip, plain, cotangent):
    back = cotangent is None
    size = lax.axis_size("row")
    vmem = pl.BlockSpec(memory_space=pltpu.VMEM)
    smem = pl.BlockSpec(memory_space=pltpu.SMEM)
    channels = plain.shape[1]
    extra = [] if back else [cotangent]
    return pl.pallas_call(
        functools.partial(synthesis_kernel, size, back),
        out_shape=jax.ShapeDtypeStruct(plain.shape, jnp.float32 if back else jnp.bfloat16),
        in_specs=[vmem] * 4 + [smem] + [vmem] * (6 + len(extra)),
        out_specs=vmem,
        scratch_shapes=[
            *(pltpu.VMEM(band.shape, jnp.bfloat16) for band in bands),
            *(pltpu.VMEM((2, channels, band.shape[3]), jnp.bfloat16) for band in bands),
            pltpu.VMEM((plain.shape[0] // 2, channels, bands[0].shape[3] // 2), jnp.bfloat16),
            pltpu.VMEM((plain.shape[0] // 4, channels, bands[1].shape[3] // 2), jnp.bfloat16),
            pltpu.SemaphoreType.DMA((3,)),
            pltpu.SemaphoreType.DMA((3,)),
        ],
        compiler_params=pltpu.CompilerParams(
            collective_id=5 if back else 4,
            has_side_effects=True,
            vmem_limit_bytes=48 * 1024 * 1024,
        ),
        name="synthesis_back" if back else "synthesis",
    )(image, *bands, row_filters, *turned, detail, skip, plain, *extra)


def split_bands(full):
    band_list = []
    for both in full:
        half = both.shape[3] // 2
        band_list.append((both[0, :, :, half:], both[1, :, :, :half], both[1, :, :, half:]))
    return full[2][0, :, :, : full[2].shape[3] // 2], band_list


def per_device(
    field,
    cotangent,
    row_filters,
    col_filter_1,
    col_filter_2,
    col_filter_3,
    detail_weight,
    skip_weight,
    spectral_weight,
    row_modes,
    col_modes,
):
    matrices = (col_filter_1, col_filter_2, col_filter_3)
    devices = lax.axis_size("row")
    full_field = analysis_call(field, row_filters, matrices, False)
    coarse_field, bands_field = split_bands(full_field)
    turned = tuple(matrix.T for matrix in matrices)
    local_rows, channels, columns = coarse_field.shape
    height = local_rows * devices
    factor = 1.0 / (height * columns)
    weight_real = spectral_weight[0]
    weight_imag = spectral_weight[1]
    mode_rows, mode_cols = row_modes.shape[0], col_modes.shape[0]
    whole_tiles = (
        mode_rows % devices == 0
        and mode_cols % devices == 0
        and (2 * local_rows * mode_cols // devices) % 8 == 0
        and (2 * (mode_rows // devices) * (mode_cols // devices)) % 8 == 0
    )
    if whole_tiles:
        near_cols = mode_cols // devices
        tables = spectral_tables(row_modes, col_modes, local_rows, columns, devices)
        coarse_image, spec = spectral_path(full_field[2], spectral_weight, tables, near_cols, False)
        spec_real, spec_imag = spec_parts(spec, mode_rows, mode_cols, devices)
    else:
        spec_real, spec_imag = owned_modes(coarse_field, row_modes, col_modes)
        out_real, out_imag = mix_modes(spec_real, spec_imag, weight_real, weight_imag, factor)
        coarse_image = owned_image(out_real, out_imag, row_modes, col_modes, local_rows, columns)
        coarse_image = jnp.pad(coarse_image, ((0, 0), (0, 0), (0, columns)))
    detail_turned = jnp.swapaxes(detail_weight, 2, 3)
    upstream = synthesis_call(
        coarse_image,
        full_field,
        row_filters,
        turned,
        detail_turned,
        skip_weight.T,
        field,
        cotangent,
    )
    full_slope = analysis_call(upstream, row_filters, matrices, True)
    coarse_slope, bands_slope = split_bands(full_slope)
    if whole_tiles:
        image_back, spec = spectral_path(full_slope[2], spectral_weight, tables, near_cols, True)
        back_real, back_imag = spec_parts(spec, mode_rows, mode_cols, devices)
    else:
        back_real, back_imag = owned_modes(coarse_slope, row_modes, col_modes)
        turned_real, turned_imag = mix_modes_back(
            back_real, back_imag, weight_real, weight_imag, factor
        )
        image_back = owned_image(
            turned_real, turned_imag, row_modes, col_modes, local_rows, columns
        )
        image_back = jnp.pad(image_back, ((0, 0), (0, 0), (0, columns)))
    grad_field = synthesis_call(
        image_back, full_slope, row_filters, turned, detail_weight, skip_weight, upstream, None
    )
    skip_local = narrow("hcw,how->co", field, upstream)
    detail_local = jnp.stack(
        [
            jnp.stack(
                [
                    narrow("hcw,how->co", bands_field[octave][member], bands_slope[octave][member])
                    for member in range(3)
                ]
            )
            for octave in range(3)
        ]
    )
    skip_total, detail_total = lax.psum((skip_local, detail_local), "row")
    total_rows = field.shape[0] * devices
    total_cols = field.shape[2]
    grad_skip = skip_total / math.sqrt(total_rows * total_cols)
    divisors = jnp.array(
        [
            [
                math.sqrt((total_rows >> octave + 1) * (total_cols >> octave + 1))
                for member in range(3)
            ]
            for octave in range(3)
        ],
        jnp.float32,
    )
    grad_detail = detail_total / divisors[:, :, None, None]
    grad_real = (
        spec_real[:, :, None] * back_real[:, None, :]
        + spec_imag[:, :, None] * back_imag[:, None, :]
    ) * factor
    grad_imag = (
        spec_real[:, :, None] * back_imag[:, None, :]
        - spec_imag[:, :, None] * back_real[:, None, :]
    ) * factor
    grad_spectral = jnp.stack([grad_real, grad_imag])
    return (grad_field, grad_detail, grad_skip, grad_spectral)


def solution(mesh):
    placed = (
        P(("groups", "row"), None, None),
        P(("groups", "row"), None, None),
        P(),
        P(),
        P(),
        P(),
        P(),
        P(),
        P(None, "row", None, None),
        P(),
        P(),
    )
    return jax.shard_map(
        per_device,
        mesh=mesh,
        in_specs=placed,
        out_specs=(
            P(("groups", "row"), None, None),
            P("groups", None, None, None),
            P("groups", None),
            P("groups", "row", None, None),
        ),
        check_vma=False,
    )
```

```python
import functools
import math

import jax
import jax.numpy as jnp
from jax import lax
from jax.experimental import pallas as pl
from jax.experimental.pallas import tpu as pltpu
from jax.sharding import PartitionSpec as P

MESH = pl.DeviceIdType.MESH
HIGHEST = lax.Precision.HIGHEST
NN = (((1,), (0,)), ((), ()))
NT = (((1,), (1,)), ((), ()))
TN = (((0,), (0,)), ((), ()))


def enter_together(size):
    me = lax.axis_index("row")
    barrier = pltpu.get_barrier_semaphore()

    def greet(step, carry):
        pl.semaphore_signal(
            barrier, inc=1, device_id={"row": lax.rem(me + step, size)}, device_id_type=MESH
        )
        return carry

    lax.fori_loop(1, size, greet, 0)
    pl.semaphore_wait(barrier, size - 1)


def tiles_copy(size, tile, send, land, send_sem, recv_sem, step):
    me = lax.axis_index("row")
    if step:
        partner = lax.rem(me + step, size)
        source = pl.ds(pl.multiple_of(partner * tile, tile), tile)
        target = pl.ds(pl.multiple_of(me * tile, tile), tile)
    else:
        partner = lax.rem(me + 1, size)
        source = target = pl.ds(0, (size - 1) * tile)
    return pltpu.make_async_remote_copy(
        src_ref=send.at[source],
        dst_ref=land.at[target],
        send_sem=send_sem,
        recv_sem=recv_sem,
        device_id={"row": partner},
        device_id_type=MESH,
    )


def start_exchange(size, tile, send, land, send_sem, recv_sem):
    me = lax.axis_index("row")
    for step in range(1, size):
        tiles_copy(size, tile, send, land, send_sem, recv_sem, step).start()
    own = pl.ds(pl.multiple_of(me * tile, tile), tile)
    land[own, :] = send[own, :]
    return tiles_copy(size, tile, send, land, send_sem, recv_sem, 0)


def channel_product(first, second):
    return lax.dot_general(first, second, NT, preferred_element_type=jnp.float32)


def local_sums(full_field, full_slope, field, upstream, sums, scales, skip_scale):
    channels = field.shape[1]
    for level in range(3):
        left, right = full_field[level], full_slope[level]
        half = left.shape[3] // 2
        if half % 128 == 0:
            halves = (slice(half, None), slice(0, half), slice(half, None))
        else:
            halves = (None, None, None)
        for member, (branch, part) in enumerate(zip((0, 1, 1), halves)):

            def body(row, total):
                if part is not None:
                    return total + channel_product(
                        left[branch, row, :, part], right[branch, row, :, part]
                    )
                lane = lax.broadcasted_iota(jnp.int32, left.shape[2:], 1)
                kept = (lane < half) if member == 1 else (lane >= half)
                wide = jnp.where(kept, as_float(left[branch, row]), 0.0).astype(jnp.bfloat16)
                return total + channel_product(wide, right[branch, row])

            total = lax.fori_loop(
                0, left.shape[1], body, jnp.zeros((channels, channels), jnp.float32)
            )
            start = (level * 3 + member) * channels
            sums[start : start + channels, :] = (total * scales[level]).astype(jnp.bfloat16)
    total = lax.fori_loop(
        0,
        field.shape[0],
        lambda row, total: total + channel_product(field[row], upstream[row]),
        jnp.zeros((channels, channels), jnp.float32),
    )
    sums[9 * channels : 10 * channels, :] = (total * skip_scale).astype(jnp.bfloat16)
    if sums.shape[0] > 10 * channels:
        sums[10 * channels :, :] = jnp.zeros(
            (sums.shape[0] - 10 * channels, channels), jnp.bfloat16
        )


def spectral_kernel(
    size,
    near_cols,
    back,
    scales,
    coarse_ref,
    col_ref,
    row_ref,
    row_inv_ref,
    col_inv_ref,
    weight_hbm,
    *rest,
):
    if back:
        full_field, full_slope = rest[:3], (*rest[3:5], coarse_ref)
        field, upstream, image_ref, spec_ref, sums, *rest = rest[5:]
    else:
        image_ref, spec_ref, *rest = rest
    (
        weight,
        send_a,
        land_a,
        send_b,
        send_c,
        land_c,
        send_d,
        land_d,
        rotated,
        weight_sem,
        send_sem,
        recv_sem,
    ) = rest
    fetch = pltpu.make_async_copy(weight_hbm, weight, weight_sem)
    fetch.start()
    enter_together(size)
    rows = coarse_ref.shape[1]
    total = None
    for row in range(rows):
        part = lax.dot_general(
            col_ref[row],
            coarse_ref[0, row].astype(jnp.float32),
            NT,
            precision=HIGHEST,
            preferred_element_type=jnp.float32,
        )
        total = part if total is None else total + part
    send_a[...] = total
    tile_a = send_a.shape[0] // size
    first = start_exchange(size, tile_a, send_a, land_a, send_sem.at[0], recv_sem.at[0])
    if back:
        local_sums(full_field, full_slope, field, upstream, sums, scales[:3], scales[3])
    first.wait_recv()
    send_b[...] = lax.dot_general(
        row_ref[...], land_a[...], NN, precision=HIGHEST, preferred_element_type=jnp.float32
    )
    tile_b = send_b.shape[0] // size
    second = start_exchange(size, tile_b, send_b, spec_ref, send_sem.at[1], recv_sem.at[1])
    second.wait_recv()
    spec = spec_ref[...]
    count = spec.shape[0]
    even = lax.broadcasted_iota(jnp.int32, spec.shape, 0) % 2 == 0
    turned = jnp.where(even, -pltpu.roll(spec, count - 1, 0), pltpu.roll(spec, 1, 0))
    rotated[...] = -turned if back else turned
    fetch.wait()
    per_tile = tile_b // 2
    modes = weight.shape[1]
    per_row = near_cols
    mode_rows = per_tile // per_row
    dims = NT if back else NN

    def mix(source, carry):
        here = pl.ds(pl.multiple_of(source * tile_b, tile_b), tile_b)
        plain = spec_ref[here, :].astype(jnp.bfloat16)
        turn = rotated[here, :].astype(jnp.bfloat16)
        pair = lax.broadcasted_iota(jnp.int32, (tile_b, plain.shape[1]), 0) // 2
        result = jnp.zeros((tile_b, plain.shape[1]), jnp.float32)
        both = jnp.concatenate([plain, turn], axis=1)
        channels = plain.shape[1]
        for member in range(0, per_tile, 2):
            blocks = []
            for one in (member, member + 1):
                mode = (one // per_row) * (modes // mode_rows) + source * per_row + one % per_row
                blocks.append(
                    jnp.concatenate(
                        [weight[part, mode].astype(jnp.bfloat16) for part in range(2)],
                        axis=1 if back else 0,
                    )
                )
            done = lax.dot_general(
                both,
                jnp.concatenate(blocks, axis=0 if back else 1),
                dims,
                preferred_element_type=jnp.float32,
            )
            result = jnp.where(pair == member, done[:, :channels], result)
            result = jnp.where(pair == member + 1, done[:, channels:], result)
        send_c[here, :] = result
        return carry

    lax.fori_loop(0, size, mix, 0, unroll=2)
    third = start_exchange(size, tile_b, send_c, land_c, send_sem.at[2], recv_sem.at[2])
    third.wait_recv()
    send_d[...] = lax.dot_general(
        row_inv_ref[...], land_c[...], NN, precision=HIGHEST, preferred_element_type=jnp.float32
    )
    fourth = start_exchange(size, tile_a, send_d, land_d, send_sem.at[3], recv_sem.at[3])
    fourth.wait_recv()
    across = land_d[...].T
    for row in range(rows):
        image_ref[row] = lax.dot_general(
            across, col_inv_ref[row], NN, precision=HIGHEST, preferred_element_type=jnp.float32
        ).astype(jnp.bfloat16)
    for sent in (first, second, third, fourth):
        sent.wait_send()


def spectral_tables(row_modes, col_modes, local_rows, columns, size):
    height = local_rows * size
    mode_rows, mode_cols = row_modes.shape[0], col_modes.shape[0]
    near_rows, near_cols = mode_rows // size, mode_cols // size
    count_a, count_b = height * near_cols * 2, mode_rows * near_cols * 2
    where_a, where_b = jnp.arange(count_a), jnp.arange(count_b)
    part_a, part_b = where_a % 2, where_b % 2
    spot = where_a // 2
    block = spot // (near_cols * local_rows)
    col_of = col_modes[block * near_cols + spot % near_cols]
    wide = jnp.arange(2 * columns)
    turns = (col_of[:, None] * wide[None, :] + part_a[:, None] * (columns // 4)) % columns
    col = jnp.cos(turns.astype(jnp.float32) * (2.0 * math.pi / columns))
    same_row = (spot // near_cols % local_rows)[None, :] == jnp.arange(local_rows)[:, None]
    inside = wide < columns
    col = jnp.where(same_row[:, :, None] & inside[None, None, :], col[None], 0.0)
    col_inv = col
    row_of = row_modes[where_b // (2 * near_cols)]
    quarter = (part_b[:, None] - part_a[None, :]) * (height // 4)
    turns = (row_of[:, None] * (where_a // (2 * near_cols))[None, :] + quarter + height) % height
    same_col = (where_b // 2 % near_cols)[:, None] == (where_a // 2 % near_cols)[None, :]
    row = jnp.cos(turns.astype(jnp.float32) * (2.0 * math.pi / height))
    row = jnp.where(same_col, row, 0.0)
    row_inv = row.T * (1.0 / (height * columns))
    return col, row, row_inv, col_inv


def spectral_path(coarse, weight, tables, near_cols, extra, scales, sum_rows):
    back = len(extra) > 0
    col, row, row_inv, col_inv = tables
    size = lax.axis_size("row")
    channels = coarse.shape[2]
    count_a, count_b = col.shape[1], row.shape[0]
    f32 = jnp.float32
    vmem = pl.BlockSpec(memory_space=pltpu.VMEM)
    return pl.pallas_call(
        functools.partial(spectral_kernel, size, near_cols, back, scales),
        out_shape=(
            jax.ShapeDtypeStruct(coarse.shape[1:], jnp.bfloat16),
            jax.ShapeDtypeStruct((count_b, channels), f32),
            *([jax.ShapeDtypeStruct((sum_rows, channels), jnp.bfloat16)] if back else []),
        ),
        in_specs=[vmem] * 5 + [pl.BlockSpec(memory_space=pl.ANY)] + [vmem] * len(extra),
        out_specs=(vmem,) * (3 if back else 2),
        scratch_shapes=[
            pltpu.VMEM(weight.shape, f32),
            pltpu.VMEM((count_a, channels), f32),
            pltpu.VMEM((count_a, channels), f32),
            pltpu.VMEM((count_b, channels), f32),
            pltpu.VMEM((count_b, channels), f32),
            pltpu.VMEM((count_b, channels), f32),
            pltpu.VMEM((count_a, channels), f32),
            pltpu.VMEM((count_a, channels), f32),
            pltpu.VMEM((count_b, channels), f32),
            pltpu.SemaphoreType.DMA,
            pltpu.SemaphoreType.DMA((4,)),
            pltpu.SemaphoreType.DMA((4,)),
        ],
        compiler_params=pltpu.CompilerParams(
            collective_id=1 if back else 0,
            has_side_effects=True,
            vmem_limit_bytes=40 * 1024 * 1024,
        ),
        cost_estimate=pl.CostEstimate(
            flops=8 * weight.size, bytes_accessed=4 * weight.size, transcendentals=0
        ),
        name="spectral_back" if back else "spectral",
    )(coarse, col, row, row_inv, col_inv, weight, *extra)


def spec_parts(spec, mode_rows, mode_cols, size):
    channels = spec.shape[1]
    grid = spec.reshape(size, mode_rows // size, mode_cols // size, 2, channels)
    grid = jnp.transpose(grid, (3, 1, 0, 2, 4)).reshape(2, -1, channels)
    return grid[0], grid[1]


def as_float(values):
    return values.astype(jnp.float32)


def precise(form, first_in, second_in):
    return jnp.einsum(form, first_in, second_in, precision=lax.Precision.HIGHEST)


def narrow(form, first_in, second_in):
    return jnp.einsum(form, first_in, second_in, preferred_element_type=jnp.float32)


def column_tables(col_modes, length):
    positions = jnp.arange(length, dtype=jnp.int32)
    turns = positions[:, None] * col_modes[None, :] % length
    angles = turns.astype(jnp.float32) * (2.0 * math.pi / length)
    return (jnp.cos(angles), jnp.sin(angles))


def row_tables(row_modes, positions, length):
    turns = row_modes[:, None] * positions[None, :] % length
    angles = turns.astype(jnp.float32) * (2.0 * math.pi / length)
    return (jnp.cos(angles), jnp.sin(angles))


def owned_modes(coarse, row_modes, col_modes):
    local_rows, channels, columns = coarse.shape
    devices = lax.axis_size("row")
    height = local_rows * devices
    cos_col, sin_col = column_tables(col_modes, columns)
    values = as_float(coarse)
    real_one = precise("hcw,wm->hcm", values, cos_col)
    imag_one = -precise("hcw,wm->hcm", values, sin_col)
    positions = lax.axis_index("row") * local_rows + jnp.arange(local_rows, dtype=jnp.int32)
    cos_row, sin_row = row_tables(row_modes, positions, height)
    real_two = precise("ph,hcm->pmc", cos_row, real_one) + precise("ph,hcm->pmc", sin_row, imag_one)
    imag_two = precise("ph,hcm->pmc", cos_row, imag_one) - precise("ph,hcm->pmc", sin_row, real_one)
    term_all = jnp.stack([real_two.reshape(-1, channels), imag_two.reshape(-1, channels)], axis=1)
    owned = lax.psum_scatter(term_all, "row", scatter_dimension=0, tiled=True)
    return (owned[:, 0], owned[:, 1])


def owned_image(real_owned, imag_owned, row_modes, col_modes, local_rows, columns):
    devices = lax.axis_size("row")
    height = local_rows * devices
    mode_rows = row_modes.shape[0]
    mode_cols = col_modes.shape[0]
    positions = lax.axis_index("row") * local_rows + jnp.arange(local_rows, dtype=jnp.int32)
    real_piece = lax.all_gather(real_owned, "row", axis=0, tiled=True)
    imag_piece = lax.all_gather(imag_owned, "row", axis=0, tiled=True)
    piece_rows = real_piece.shape[0]
    flat = jnp.arange(piece_rows, dtype=jnp.int32)
    row_pick = (flat // mode_cols)[:, None] == jnp.arange(mode_rows, dtype=jnp.int32)[None, :]
    frequency = jnp.sum(jnp.where(row_pick, row_modes[None, :], 0), axis=1)
    column_pick = (
        (flat % mode_cols)[:, None] == jnp.arange(mode_cols, dtype=jnp.int32)[None, :]
    ).astype(jnp.float32)
    turns = positions[:, None] * frequency[None, :] % height
    angles = turns.astype(jnp.float32) * (2.0 * math.pi / height)
    cos_part = jnp.cos(angles)
    sin_part = jnp.sin(angles)
    cos_pick = cos_part[:, :, None] * column_pick[None, :, :]
    sin_pick = sin_part[:, :, None] * column_pick[None, :, :]
    real_sum = precise("hnm,nc->hcm", cos_pick, real_piece) - precise(
        "hnm,nc->hcm", sin_pick, imag_piece
    )
    imag_sum = precise("hnm,nc->hcm", cos_pick, imag_piece) + precise(
        "hnm,nc->hcm", sin_pick, real_piece
    )
    cos_col, sin_col = column_tables(col_modes, columns)
    image = precise("hcm,wm->hcw", real_sum, cos_col) - precise("hcm,wm->hcw", imag_sum, sin_col)
    return image.astype(jnp.bfloat16)


def mix_modes(real_in, imag_in, weight_real, weight_imag, factor):
    real_out = (
        precise("nc,nco->no", real_in, weight_real) - precise("nc,nco->no", imag_in, weight_imag)
    ) * factor
    imag_out = (
        precise("nc,nco->no", real_in, weight_imag) + precise("nc,nco->no", imag_in, weight_real)
    ) * factor
    return (real_out, imag_out)


def mix_modes_back(real_in, imag_in, weight_real, weight_imag, factor):
    real_out = (
        precise("no,nco->nc", real_in, weight_real) + precise("no,nco->nc", imag_in, weight_imag)
    ) * factor
    imag_out = (
        precise("no,nco->nc", imag_in, weight_real) - precise("no,nco->nc", real_in, weight_imag)
    ) * factor
    return (real_out, imag_out)


def greet_ring(receives_from):
    barrier = pltpu.get_barrier_semaphore()
    pl.semaphore_signal(barrier, inc=1, device_id={"row": receives_from}, device_id_type=MESH)
    pl.semaphore_wait(barrier, 1)


def analysis_kernel(
    size,
    values,
    taps,
    filter_1,
    filter_2,
    filter_3,
    out_1,
    out_2,
    out_3,
    halo_1,
    halo_2,
    halo_3,
    send_sem,
    recv_sem,
):
    me = lax.axis_index("row")
    above, below = lax.rem(me + size - 1, size), lax.rem(me + 1, size)
    greet_ring(below)

    def copy(level, source, halo):
        return pltpu.make_async_remote_copy(
            src_ref=source,
            dst_ref=halo,
            send_sem=send_sem.at[level],
            recv_sem=recv_sem.at[level],
            device_id={"row": above},
            device_id_type=MESH,
        )

    def one(get, row, matrix, out):
        loaded = [as_float(get(2 * row + offset)) for offset in range(4)]
        halves = []
        for branch in range(2):
            running = taps[branch, 0] * loaded[0]
            for offset in range(1, 4):
                running = running + taps[branch, offset] * loaded[offset]
            halves.append(running.astype(jnp.bfloat16))
        both = jnp.concatenate(halves, axis=0)
        done = jnp.dot(both, matrix[...], preferred_element_type=jnp.float32).astype(jnp.bfloat16)
        count = halves[0].shape[0]
        out[0, row] = done[:count]
        out[1, row] = done[count:]

    def span(get, first, last, matrix, out):
        def body(row, carry):
            one(get, row, matrix, out)
            return carry

        lax.fori_loop(first, last, body, 0)

    def edged(get, halo, count):
        return lambda row: get(row) if row < count else halo[row - count]

    count = values.shape[0]
    half_1, half_2 = filter_1.shape[0] // 2, filter_2.shape[0] // 2
    get_1 = lambda row: values[row]
    get_2 = lambda row: out_1[0, row, :, :half_1]
    get_3 = lambda row: out_2[0, row, :, :half_2]
    first = copy(0, values.at[pl.ds(0, 2)], halo_1)
    first.start()
    span(get_1, 0, 2, filter_1, out_1)
    second = copy(1, out_1.at[0, pl.ds(0, 2), :, pl.ds(0, half_1)], halo_2)
    second.start()
    early = min(6, count // 2 - 1)
    span(get_1, 2, early, filter_1, out_1)
    span(get_2, 0, 2, filter_2, out_2)
    third = copy(2, out_2.at[0, pl.ds(0, 2), :, pl.ds(0, half_2)], halo_3)
    third.start()
    span(get_1, early, count // 2 - 1, filter_1, out_1)
    first.wait()
    one(edged(get_1, halo_1, count), count // 2 - 1, filter_1, out_1)
    span(get_2, 2, count // 4 - 1, filter_2, out_2)
    second.wait()
    one(edged(get_2, halo_2, count // 2), count // 4 - 1, filter_2, out_2)
    span(get_3, 0, count // 8 - 1, filter_3, out_3)
    third.wait()
    one(edged(get_3, halo_3, count // 4), count // 8 - 1, filter_3, out_3)


def analysis_call(values, row_filters, matrices, back):
    size = lax.axis_size("row")
    count, channels, columns = values.shape
    vmem = pl.BlockSpec(memory_space=pltpu.VMEM)
    widths = [columns >> level for level in range(3)]
    return pl.pallas_call(
        functools.partial(analysis_kernel, size),
        out_shape=tuple(
            jax.ShapeDtypeStruct((2, count >> level + 1, channels, widths[level]), jnp.bfloat16)
            for level in range(3)
        ),
        in_specs=[vmem, pl.BlockSpec(memory_space=pltpu.SMEM), vmem, vmem, vmem],
        out_specs=(vmem, vmem, vmem),
        scratch_shapes=[
            *(pltpu.VMEM((2, channels, width), jnp.bfloat16) for width in widths),
            pltpu.SemaphoreType.DMA((3,)),
            pltpu.SemaphoreType.DMA((3,)),
        ],
        compiler_params=pltpu.CompilerParams(
            collective_id=3 if back else 2,
            has_side_effects=True,
            vmem_limit_bytes=40 * 1024 * 1024,
        ),
        name="analysis_back" if back else "analysis",
    )(values, row_filters, *matrices)


def gelu_slope(value):
    scale = math.sqrt(2.0 / math.pi)
    square = value * value
    bend = jnp.tanh(scale * (value + 0.044715 * (square * value)))
    return 0.5 * (1.0 + bend) + 0.5 * value * (1.0 - bend * bend) * (
        scale * (1.0 + 3 * 0.044715 * square)
    )


def synthesis_kernel(
    size,
    back,
    image,
    out_1,
    out_2,
    out_3,
    taps,
    turned_1,
    turned_2,
    turned_3,
    detail,
    skip,
    plain,
    *rest,
):
    if back:
        sums, result, gathered, landed, total, send_more, recv_more, *rest = rest
    else:
        cotangent, result, detail_turned, skip_turned, *rest = rest
        for level in range(3):
            for member in range(3):
                detail_turned[level, member] = as_float(detail[level, member]).T.astype(
                    jnp.bfloat16
                )
        skip_turned[...] = as_float(skip[...]).T.astype(jnp.bfloat16)
        detail, skip = detail_turned, skip_turned
    syn_1, syn_2, syn_3, halo_1, halo_2, halo_3, top_1, top_2, send_sem, recv_sem = rest
    me = lax.axis_index("row")
    above, below = lax.rem(me + size - 1, size), lax.rem(me + 1, size)
    if back:
        enter_together(size)
    else:
        greet_ring(above)

    def copy(level, syn, halo):
        return pltpu.make_async_remote_copy(
            src_ref=syn.at[:, syn.shape[1] - 1],
            dst_ref=halo,
            send_sem=send_sem.at[level],
            recv_sem=recv_sem.at[level],
            device_id={"row": below},
            device_id_type=MESH,
        )

    def mixed(level, member, band):
        return jnp.dot(detail[level, member], band, preferred_element_type=jnp.float32).astype(
            jnp.bfloat16
        )

    def one(level, row, top, out, turned, syn):
        half = out.shape[3] // 2
        if half % 128 == 0:
            low = [top[row], mixed(level, 0, out[0, row, :, half:])]
            high = [mixed(level, 1, out[1, row, :, :half]), mixed(level, 2, out[1, row, :, half:])]
            low, high = jnp.concatenate(low, axis=1), jnp.concatenate(high, axis=1)
        else:
            bands, lower = out[1, row], lax.broadcasted_iota(jnp.int32, out.shape[2:], 1) < half
            low = jnp.where(lower, as_float(top[row]), as_float(mixed(level, 0, out[0, row])))
            high = jnp.where(
                lower, as_float(mixed(level, 1, bands)), as_float(mixed(level, 2, bands))
            )
            low, high = low.astype(jnp.bfloat16), high.astype(jnp.bfloat16)
        both = jnp.concatenate([low, high], axis=0)
        done = lax.dot_general(
            both, turned[...], NT, preferred_element_type=jnp.float32
        ).astype(jnp.bfloat16)
        count = low.shape[0]
        syn[0, row] = done[:count]
        syn[1, row] = done[count:]

    def joined(syn, row, previous):
        low_now, high_now = as_float(syn[0, row]), as_float(syn[1, row])
        low_prev, high_prev = as_float(previous(0)), as_float(previous(1))
        pair = []
        for parity in range(2):
            running = taps[0, parity] * low_now + taps[1, parity] * high_now
            running = running + taps[0, parity + 2] * low_prev
            pair.append(running + taps[1, parity + 2] * high_prev)
        return pair

    def combine(syn, row, halo, top):
        previous = (lambda part: halo[part]) if halo is not None else lambda part: syn[part, row - 1]
        pair = joined(syn, row, previous)
        for parity in range(2):
            top[2 * row + parity] = pair[parity].astype(jnp.bfloat16)

    def last(row, halo):
        previous = (
            (lambda part: halo[part]) if halo is not None else lambda part: syn_1[part, row - 1]
        )
        pair = joined(syn_1, row, previous)
        for parity in range(2):
            here = 2 * row + parity
            value = pair[parity] + jnp.dot(
                skip[...], plain[here], preferred_element_type=jnp.float32
            )
            if not back:
                value = (as_float(cotangent[here]) * gelu_slope(value)).astype(jnp.bfloat16)
            result[here] = value

    def span(first, stop, call):
        def body(row, carry):
            call(row)
            return carry

        lax.fori_loop(first, stop, body, 0)

    level_3 = lambda row: one(2, row, image, out_3, turned_3, syn_3)
    level_2 = lambda row: one(1, row, top_2, out_2, turned_2, syn_2)
    level_1 = lambda row: one(0, row, top_1, out_1, turned_1, syn_1)
    rows_3, rows_2, rows_1 = syn_3.shape[1], syn_2.shape[1], syn_1.shape[1]
    level_3(rows_3 - 1)
    third = copy(2, syn_3, halo_3)
    third.start()
    if back:
        chunk = sums.shape[0] // size
        scatter = start_exchange(size, chunk, sums, landed, send_more.at[0], recv_more.at[0])
    span(0, rows_3 - 1, level_3)
    combine(syn_3, rows_3 - 1, None, top_2)
    level_2(rows_2 - 1)
    second = copy(1, syn_2, halo_2)
    second.start()
    level_2(rows_2 - 2)
    combine(syn_2, rows_2 - 1, None, top_1)
    level_1(rows_1 - 1)
    first = copy(0, syn_1, halo_1)
    first.start()
    level_1(rows_1 - 2)
    last(rows_1 - 1, None)
    span(1, rows_3 - 1, lambda row: combine(syn_3, row, None, top_2))
    third.wait()
    combine(syn_3, 0, halo_3, top_2)
    span(0, rows_2 - 2, level_2)
    span(1, rows_2 - 1, lambda row: combine(syn_2, row, None, top_1))
    span(2, rows_1 - 2, level_1)
    if back:
        scatter.wait_recv()
        whole = as_float(landed[0:chunk, :])
        for step in range(1, size):
            whole = whole + as_float(landed[step * chunk : (step + 1) * chunk, :])
        total[...] = whole.astype(jnp.bfloat16)
        target = pl.ds(pl.multiple_of(me * chunk, chunk), chunk)
        for step in range(1, size):
            pltpu.make_async_remote_copy(
                src_ref=total,
                dst_ref=gathered.at[target],
                send_sem=send_more.at[1],
                recv_sem=recv_more.at[1],
                device_id={"row": lax.rem(me + step, size)},
                device_id_type=MESH,
            ).start()
        gathered[target, :] = total[...]
    span(3, rows_1 - 1, lambda row: last(row, None))
    second.wait()
    combine(syn_2, 0, halo_2, top_1)
    span(0, 2, level_1)
    span(1, 3, lambda row: last(row, None))
    first.wait()
    last(0, halo_1)
    if back:
        scatter.wait_send()
        tiles_copy(size, chunk, landed, gathered, send_more.at[1], recv_more.at[1], 0).wait()


def synthesis_call(image, bands, row_filters, matrices, detail, skip, plain, extra, back):
    size = lax.axis_size("row")
    vmem = pl.BlockSpec(memory_space=pltpu.VMEM)
    smem = pl.BlockSpec(memory_space=pltpu.SMEM)
    channels = plain.shape[1]
    result = jax.ShapeDtypeStruct(plain.shape, jnp.float32 if back else jnp.bfloat16)
    own = [pltpu.VMEM(detail.shape, jnp.bfloat16), pltpu.VMEM(skip.shape, jnp.bfloat16)]
    if back:
        result = (result, jax.ShapeDtypeStruct(extra.shape, jnp.bfloat16))
        own = [
            pltpu.VMEM(extra.shape, jnp.bfloat16),
            pltpu.VMEM((extra.shape[0] // size, channels), jnp.bfloat16),
            pltpu.SemaphoreType.DMA((2,)),
            pltpu.SemaphoreType.DMA((2,)),
        ]
    return pl.pallas_call(
        functools.partial(synthesis_kernel, size, back),
        out_shape=result,
        in_specs=[vmem] * 4 + [smem] + [vmem] * 7,
        out_specs=(vmem, vmem) if back else vmem,
        scratch_shapes=[
            *own,
            *(pltpu.VMEM(band.shape, jnp.bfloat16) for band in bands),
            *(pltpu.VMEM((2, channels, band.shape[3]), jnp.bfloat16) for band in bands),
            pltpu.VMEM((plain.shape[0] // 2, channels, bands[0].shape[3] // 2), jnp.bfloat16),
            pltpu.VMEM((plain.shape[0] // 4, channels, bands[1].shape[3] // 2), jnp.bfloat16),
            pltpu.SemaphoreType.DMA((3,)),
            pltpu.SemaphoreType.DMA((3,)),
        ],
        compiler_params=pltpu.CompilerParams(
            collective_id=5 if back else 4,
            has_side_effects=True,
            vmem_limit_bytes=48 * 1024 * 1024,
        ),
        name="synthesis_back" if back else "synthesis",
    )(image, *bands, row_filters, *matrices, detail, skip, plain, extra)


def split_bands(full):
    band_list = []
    for both in full:
        half = both.shape[3] // 2
        band_list.append((both[0, :, :, half:], both[1, :, :, :half], both[1, :, :, half:]))
    return full[2][0, :, :, : full[2].shape[3] // 2], band_list


def per_device(
    field,
    cotangent,
    row_filters,
    col_filter_1,
    col_filter_2,
    col_filter_3,
    detail_weight,
    skip_weight,
    spectral_weight,
    row_modes,
    col_modes,
):
    matrices = (col_filter_1, col_filter_2, col_filter_3)
    devices = lax.axis_size("row")
    full_field = analysis_call(field, row_filters, matrices, False)
    coarse_field, bands_field = split_bands(full_field)
    total_rows, total_cols = field.shape[0] * devices, field.shape[2]
    scales = [
        1.0 / math.sqrt((total_rows >> octave + 1) * (total_cols >> octave + 1))
        for octave in range(3)
    ] + [1.0 / math.sqrt(total_rows * total_cols)]
    sum_rows = 10 * field.shape[1]
    sum_rows = -(-sum_rows // (16 * devices)) * 16 * devices
    local_rows, channels, columns = coarse_field.shape
    height = local_rows * devices
    factor = 1.0 / (height * columns)
    weight_real = spectral_weight[0]
    weight_imag = spectral_weight[1]
    mode_rows, mode_cols = row_modes.shape[0], col_modes.shape[0]
    whole_tiles = (
        mode_rows % devices == 0
        and mode_cols % devices == 0
        and (2 * local_rows * mode_cols // devices) % 8 == 0
        and (2 * (mode_rows // devices) * (mode_cols // devices)) % 8 == 0
    )
    if whole_tiles:
        near_cols = mode_cols // devices
        tables = spectral_tables(row_modes, col_modes, local_rows, columns, devices)
        coarse_image, spec = spectral_path(
            full_field[2], spectral_weight, tables, near_cols, (), scales, sum_rows
        )
        spec_real, spec_imag = spec_parts(spec, mode_rows, mode_cols, devices)
    else:
        spec_real, spec_imag = owned_modes(coarse_field, row_modes, col_modes)
        out_real, out_imag = mix_modes(spec_real, spec_imag, weight_real, weight_imag, factor)
        coarse_image = owned_image(out_real, out_imag, row_modes, col_modes, local_rows, columns)
        coarse_image = jnp.pad(coarse_image, ((0, 0), (0, 0), (0, columns)))
    upstream = synthesis_call(
        coarse_image,
        full_field,
        row_filters,
        matrices,
        detail_weight,
        skip_weight,
        field,
        cotangent,
        False,
    )
    full_slope = analysis_call(upstream, row_filters, matrices, True)
    coarse_slope, bands_slope = split_bands(full_slope)
    if whole_tiles:
        extra = (*full_field, *full_slope[:2], field, upstream)
        image_back, spec, sums = spectral_path(
            full_slope[2], spectral_weight, tables, near_cols, extra, scales, sum_rows
        )
        back_real, back_imag = spec_parts(spec, mode_rows, mode_cols, devices)
    else:
        back_real, back_imag = owned_modes(coarse_slope, row_modes, col_modes)
        turned_real, turned_imag = mix_modes_back(
            back_real, back_imag, weight_real, weight_imag, factor
        )
        image_back = owned_image(
            turned_real, turned_imag, row_modes, col_modes, local_rows, columns
        )
        image_back = jnp.pad(image_back, ((0, 0), (0, 0), (0, columns)))
        shares = [
            narrow("hcw,how->co", bands_field[octave][member], bands_slope[octave][member])
            * scales[octave]
            for octave in range(3)
            for member in range(3)
        ] + [narrow("hcw,how->co", field, upstream) * scales[3]]
        sums = jnp.concatenate(shares, axis=0).astype(jnp.bfloat16)
        sums = jnp.pad(sums, ((0, sum_rows - sums.shape[0]), (0, 0)))
    grad_field, gathered = synthesis_call(
        image_back,
        full_slope,
        row_filters,
        matrices,
        detail_weight,
        skip_weight,
        upstream,
        sums,
        True,
    )
    gathered = as_float(gathered[: 10 * channels])
    grad_detail = gathered[: 9 * channels].reshape(3, 3, channels, channels)
    grad_skip = gathered[9 * channels :]
    grad_real = (
        spec_real[:, :, None] * back_real[:, None, :]
        + spec_imag[:, :, None] * back_imag[:, None, :]
    ) * factor
    grad_imag = (
        spec_real[:, :, None] * back_imag[:, None, :]
        - spec_imag[:, :, None] * back_real[:, None, :]
    ) * factor
    grad_spectral = jnp.stack([grad_real, grad_imag])
    return (grad_field, grad_detail, grad_skip, grad_spectral)


def solution(mesh):
    placed = (
        P(("groups", "row"), None, None),
        P(("groups", "row"), None, None),
        P(),
        P(),
        P(),
        P(),
        P(),
        P(),
        P(None, "row", None, None),
        P(),
        P(),
    )
    return jax.shard_map(
        per_device,
        mesh=mesh,
        in_specs=placed,
        out_specs=(
            P(("groups", "row"), None, None),
            P("groups", None, None, None),
            P("groups", None),
            P("groups", "row", None, None),
        ),
        check_vma=False,
    )
```

```python
import functools
import math

import jax
import jax.numpy as jnp
from jax import lax
from jax.experimental import pallas as pl
from jax.experimental.pallas import tpu as pltpu
from jax.sharding import PartitionSpec as P

MESH = pl.DeviceIdType.MESH
HIGHEST = lax.Precision.HIGHEST
NN = (((1,), (0,)), ((), ()))
NT = (((1,), (1,)), ((), ()))
TN = (((0,), (0,)), ((), ()))


def greet_all(size):
    me = lax.axis_index("row")
    barrier = pltpu.get_barrier_semaphore()
    for step in range(1, size):
        pl.semaphore_signal(
            barrier, inc=1, device_id={"row": lax.rem(me + step, size)}, device_id_type=MESH
        )


def hear_all(size):
    pl.semaphore_wait(pltpu.get_barrier_semaphore(), size - 1)


def tiles_copy(size, tile, send, land, send_sem, recv_sem, step):
    me = lax.axis_index("row")
    if step:
        partner = lax.rem(me + step, size)
        source = pl.ds(pl.multiple_of(partner * tile, tile), tile)
        target = pl.ds(pl.multiple_of(me * tile, tile), tile)
    else:
        partner = lax.rem(me + 1, size)
        source = target = pl.ds(0, (size - 1) * tile)
    return pltpu.make_async_remote_copy(
        src_ref=send.at[source],
        dst_ref=land.at[target],
        send_sem=send_sem,
        recv_sem=recv_sem,
        device_id={"row": partner},
        device_id_type=MESH,
    )


def start_exchange(size, tile, send, land, send_sem, recv_sem):
    me = lax.axis_index("row")
    for step in range(1, size):
        tiles_copy(size, tile, send, land, send_sem, recv_sem, step).start()
    own = pl.ds(pl.multiple_of(me * tile, tile), tile)
    land[own, :] = send[own, :]
    return tiles_copy(size, tile, send, land, send_sem, recv_sem, 0)


def channel_product(first, second):
    return lax.dot_general(first, second, NT, preferred_element_type=jnp.float32)


def local_sums(full_field, full_slope, field, upstream, sums, scales, skip_scale):
    channels = field.shape[1]
    for level in range(3):
        left, right = full_field[level], full_slope[level]
        half = left.shape[3] // 2
        if half % 128 == 0:
            halves = (slice(half, None), slice(0, half), slice(half, None))
        else:
            halves = (None, None, None)
        for member, (branch, part) in enumerate(zip((0, 1, 1), halves)):

            def body(row, total):
                if part is not None:
                    return total + channel_product(
                        left[branch, row, :, part], right[branch, row, :, part]
                    )
                lane = lax.broadcasted_iota(jnp.int32, left.shape[2:], 1)
                kept = (lane < half) if member == 1 else (lane >= half)
                wide = jnp.where(kept, as_float(left[branch, row]), 0.0).astype(jnp.bfloat16)
                return total + channel_product(wide, right[branch, row])

            total = lax.fori_loop(
                0, left.shape[1], body, jnp.zeros((channels, channels), jnp.float32)
            )
            start = (level * 3 + member) * channels
            sums[start : start + channels, :] = (total * scales[level]).astype(jnp.bfloat16)
    total = lax.fori_loop(
        0,
        field.shape[0],
        lambda row, total: total + channel_product(field[row], upstream[row]),
        jnp.zeros((channels, channels), jnp.float32),
    )
    sums[9 * channels : 10 * channels, :] = (total * skip_scale).astype(jnp.bfloat16)
    if sums.shape[0] > 10 * channels:
        sums[10 * channels :, :] = jnp.zeros(
            (sums.shape[0] - 10 * channels, channels), jnp.bfloat16
        )


def spectral_kernel(
    size,
    near_cols,
    back,
    scales,
    coarse_ref,
    col_ref,
    row_ref,
    row_inv_ref,
    col_inv_ref,
    weight_hbm,
    *rest,
):
    if back:
        full_field, full_slope = rest[:3], (*rest[3:5], coarse_ref)
        field, upstream, image_ref, spec_ref, share, sums, landed, more_sem, *rest = rest[5:]
    else:
        image_ref, spec_ref, *rest = rest
    (
        weight,
        send_a,
        land_a,
        send_b,
        send_c,
        land_c,
        send_d,
        land_d,
        rotated,
        weight_sem,
        send_sem,
        recv_sem,
    ) = rest
    fetch = pltpu.make_async_copy(weight_hbm, weight, weight_sem)
    fetch.start()
    greet_all(size)
    rows = coarse_ref.shape[1]
    total = None
    for row in range(rows):
        part = lax.dot_general(
            col_ref[row],
            coarse_ref[0, row].astype(jnp.float32),
            NT,
            precision=HIGHEST,
            preferred_element_type=jnp.float32,
        )
        total = part if total is None else total + part
    send_a[...] = total
    hear_all(size)
    tile_a = send_a.shape[0] // size
    first = start_exchange(size, tile_a, send_a, land_a, send_sem.at[0], recv_sem.at[0])
    if back:
        local_sums(full_field, full_slope, field, upstream, sums, scales[:3], scales[3])
    first.wait_recv()
    send_b[...] = lax.dot_general(
        row_ref[...], land_a[...], NN, precision=HIGHEST, preferred_element_type=jnp.float32
    )
    tile_b = send_b.shape[0] // size
    second = start_exchange(size, tile_b, send_b, spec_ref, send_sem.at[1], recv_sem.at[1])
    if back:
        chunk = sums.shape[0] // size
        scatter = start_exchange(size, chunk, sums, landed, more_sem.at[0], more_sem.at[1])
    second.wait_recv()
    spec = spec_ref[...]
    count = spec.shape[0]
    even = lax.broadcasted_iota(jnp.int32, spec.shape, 0) % 2 == 0
    turned = jnp.where(even, -pltpu.roll(spec, count - 1, 0), pltpu.roll(spec, 1, 0))
    rotated[...] = -turned if back else turned
    fetch.wait()
    per_tile = tile_b // 2
    modes = weight.shape[1]
    per_row = near_cols
    mode_rows = per_tile // per_row
    dims = NT if back else NN

    def mix(source, carry):
        here = pl.ds(pl.multiple_of(source * tile_b, tile_b), tile_b)
        plain = spec_ref[here, :].astype(jnp.bfloat16)
        turn = rotated[here, :].astype(jnp.bfloat16)
        pair = lax.broadcasted_iota(jnp.int32, (tile_b, plain.shape[1]), 0) // 2
        result = jnp.zeros((tile_b, plain.shape[1]), jnp.float32)
        both = jnp.concatenate([plain, turn], axis=1)
        channels = plain.shape[1]
        for member in range(0, per_tile, 2):
            blocks = []
            for one in (member, member + 1):
                mode = (one // per_row) * (modes // mode_rows) + source * per_row + one % per_row
                blocks.append(
                    jnp.concatenate(
                        [weight[part, mode].astype(jnp.bfloat16) for part in range(2)],
                        axis=1 if back else 0,
                    )
                )
            done = lax.dot_general(
                both,
                jnp.concatenate(blocks, axis=0 if back else 1),
                dims,
                preferred_element_type=jnp.float32,
            )
            result = jnp.where(pair == member, done[:, :channels], result)
            result = jnp.where(pair == member + 1, done[:, channels:], result)
        send_c[here, :] = result
        return carry

    lax.fori_loop(0, size, mix, 0, unroll=2)
    third = start_exchange(size, tile_b, send_c, land_c, send_sem.at[2], recv_sem.at[2])
    third.wait_recv()
    send_d[...] = lax.dot_general(
        row_inv_ref[...], land_c[...], NN, precision=HIGHEST, preferred_element_type=jnp.float32
    )
    fourth = start_exchange(size, tile_a, send_d, land_d, send_sem.at[3], recv_sem.at[3])
    if back:
        scatter.wait_recv()
        whole = as_float(landed[0:chunk, :])
        for step in range(1, size):
            whole = whole + as_float(landed[step * chunk : (step + 1) * chunk, :])
        share[...] = whole.astype(jnp.bfloat16)
        scatter.wait_send()
    fourth.wait_recv()
    across = land_d[...].T
    for row in range(rows):
        image_ref[row] = lax.dot_general(
            across, col_inv_ref[row], NN, precision=HIGHEST, preferred_element_type=jnp.float32
        ).astype(jnp.bfloat16)
    for sent in (first, second, third, fourth):
        sent.wait_send()


def picked(modes, places):
    same = places[:, None] == jnp.arange(modes.shape[0])[None, :]
    return jnp.sum(jnp.where(same, modes[None, :], 0), axis=1)


def spectral_tables(row_modes, col_modes, local_rows, columns, size):
    height = local_rows * size
    mode_rows, mode_cols = row_modes.shape[0], col_modes.shape[0]
    near_rows, near_cols = mode_rows // size, mode_cols // size
    count_a, count_b = height * near_cols * 2, mode_rows * near_cols * 2
    where_a, where_b = jnp.arange(count_a), jnp.arange(count_b)
    part_a, part_b = where_a % 2, where_b % 2
    spot = where_a // 2
    block = spot // (near_cols * local_rows)
    col_of = picked(col_modes, block * near_cols + spot % near_cols)
    wide = jnp.arange(2 * columns)
    turns = (col_of[:, None] * wide[None, :] + part_a[:, None] * (columns // 4)) % columns
    col = jnp.cos(turns.astype(jnp.float32) * (2.0 * math.pi / columns))
    same_row = (spot // near_cols % local_rows)[None, :] == jnp.arange(local_rows)[:, None]
    inside = wide < columns
    col = jnp.where(same_row[:, :, None] & inside[None, None, :], col[None], 0.0)
    col_inv = col
    row_of = picked(row_modes, where_b // (2 * near_cols))
    quarter = (part_b[:, None] - part_a[None, :]) * (height // 4)
    turns = (row_of[:, None] * (where_a // (2 * near_cols))[None, :] + quarter + height) % height
    same_col = (where_b // 2 % near_cols)[:, None] == (where_a // 2 % near_cols)[None, :]
    row = jnp.cos(turns.astype(jnp.float32) * (2.0 * math.pi / height))
    row = jnp.where(same_col, row, 0.0)
    row_inv = row.T * (1.0 / (height * columns))
    return col, row, row_inv, col_inv


def spectral_path(coarse, weight, tables, near_cols, extra, scales, sum_rows):
    back = len(extra) > 0
    col, row, row_inv, col_inv = tables
    size = lax.axis_size("row")
    channels = coarse.shape[2]
    count_a, count_b = col.shape[1], row.shape[0]
    f32 = jnp.float32
    vmem = pl.BlockSpec(memory_space=pltpu.VMEM)
    return pl.pallas_call(
        functools.partial(spectral_kernel, size, near_cols, back, scales),
        out_shape=(
            jax.ShapeDtypeStruct(coarse.shape[1:], jnp.bfloat16),
            jax.ShapeDtypeStruct((count_b, channels), f32),
            *([jax.ShapeDtypeStruct((sum_rows // size, channels), jnp.bfloat16)] if back else []),
        ),
        in_specs=[vmem] * 5 + [pl.BlockSpec(memory_space=pltpu.HBM)] + [vmem] * len(extra),
        out_specs=(vmem,) * (3 if back else 2),
        scratch_shapes=[
            *(
                [
                    pltpu.VMEM((sum_rows, channels), jnp.bfloat16),
                    pltpu.VMEM((sum_rows, channels), jnp.bfloat16),
                    pltpu.SemaphoreType.DMA((2,)),
                ]
                if back
                else []
            ),
            pltpu.VMEM(weight.shape, f32),
            pltpu.VMEM((count_a, channels), f32),
            pltpu.VMEM((count_a, channels), f32),
            pltpu.VMEM((count_b, channels), f32),
            pltpu.VMEM((count_b, channels), f32),
            pltpu.VMEM((count_b, channels), f32),
            pltpu.VMEM((count_a, channels), f32),
            pltpu.VMEM((count_a, channels), f32),
            pltpu.VMEM((count_b, channels), f32),
            pltpu.SemaphoreType.DMA,
            pltpu.SemaphoreType.DMA((4,)),
            pltpu.SemaphoreType.DMA((4,)),
        ],
        compiler_params=pltpu.CompilerParams(
            collective_id=1 if back else 0,
            has_side_effects=True,
            vmem_limit_bytes=24 * 1024 * 1024,
        ),
        cost_estimate=pl.CostEstimate(
            flops=8 * weight.size, bytes_accessed=4 * weight.size, transcendentals=0
        ),
        name="spectral_back" if back else "spectral",
    )(coarse, col, row, row_inv, col_inv, weight, *extra)


def outer_kernel(factor, field_ref, slope_ref, out_ref):
    slope = slope_ref[...] * factor
    count = slope.shape[0]
    even = lax.broadcasted_iota(jnp.int32, slope.shape, 0) % 2 == 0
    turned = jnp.where(even, pltpu.roll(slope, count - 1, 0), -pltpu.roll(slope, 1, 0))
    both = jnp.concatenate([slope, turned], axis=1)
    across = field_ref[...].T
    channels = across.shape[0]
    pair = lax.broadcasted_iota(jnp.int32, across.shape, 1) // 2
    near_cols = out_ref.shape[3]
    for mode in range(count // 2):
        done = jnp.dot(
            jnp.where(pair == mode, across, 0.0), both, preferred_element_type=jnp.float32
        )
        for part in range(2):
            out_ref[part, mode // near_cols, 0, mode % near_cols] = done[
                :, part * channels : (part + 1) * channels
            ]


def outer_products(spec_field, spec_slope, near_rows, near_cols, factor):
    size = lax.axis_size("row")
    count, channels = spec_field.shape
    tile = count // size
    shape = (2, near_rows, size, near_cols, channels, channels)
    spec = pl.BlockSpec((tile, channels), lambda block: (block, 0))
    result = pl.pallas_call(
        functools.partial(outer_kernel, factor),
        grid=(size,),
        out_shape=jax.ShapeDtypeStruct(shape, jnp.float32),
        in_specs=[spec, spec],
        out_specs=pl.BlockSpec(
            (2, near_rows, 1, near_cols, channels, channels),
            lambda block: (0, 0, block, 0, 0, 0),
        ),
        name="outer_products",
    )(spec_field, spec_slope)
    return result.reshape(2, -1, channels, channels)


def as_float(values):
    return values.astype(jnp.float32)


def precise(form, first_in, second_in):
    return jnp.einsum(form, first_in, second_in, precision=lax.Precision.HIGHEST)


def narrow(form, first_in, second_in):
    return jnp.einsum(form, first_in, second_in, preferred_element_type=jnp.float32)


def column_tables(col_modes, length):
    positions = jnp.arange(length, dtype=jnp.int32)
    turns = positions[:, None] * col_modes[None, :] % length
    angles = turns.astype(jnp.float32) * (2.0 * math.pi / length)
    return (jnp.cos(angles), jnp.sin(angles))


def row_tables(row_modes, positions, length):
    turns = row_modes[:, None] * positions[None, :] % length
    angles = turns.astype(jnp.float32) * (2.0 * math.pi / length)
    return (jnp.cos(angles), jnp.sin(angles))


def owned_modes(coarse, row_modes, col_modes):
    local_rows, channels, columns = coarse.shape
    devices = lax.axis_size("row")
    height = local_rows * devices
    cos_col, sin_col = column_tables(col_modes, columns)
    values = as_float(coarse)
    real_one = precise("hcw,wm->hcm", values, cos_col)
    imag_one = -precise("hcw,wm->hcm", values, sin_col)
    positions = lax.axis_index("row") * local_rows + jnp.arange(local_rows, dtype=jnp.int32)
    cos_row, sin_row = row_tables(row_modes, positions, height)
    real_two = precise("ph,hcm->pmc", cos_row, real_one) + precise("ph,hcm->pmc", sin_row, imag_one)
    imag_two = precise("ph,hcm->pmc", cos_row, imag_one) - precise("ph,hcm->pmc", sin_row, real_one)
    term_all = jnp.stack([real_two.reshape(-1, channels), imag_two.reshape(-1, channels)], axis=1)
    owned = lax.psum_scatter(term_all, "row", scatter_dimension=0, tiled=True)
    return (owned[:, 0], owned[:, 1])


def owned_image(real_owned, imag_owned, row_modes, col_modes, local_rows, columns):
    devices = lax.axis_size("row")
    height = local_rows * devices
    mode_rows = row_modes.shape[0]
    mode_cols = col_modes.shape[0]
    positions = lax.axis_index("row") * local_rows + jnp.arange(local_rows, dtype=jnp.int32)
    real_piece = lax.all_gather(real_owned, "row", axis=0, tiled=True)
    imag_piece = lax.all_gather(imag_owned, "row", axis=0, tiled=True)
    piece_rows = real_piece.shape[0]
    flat = jnp.arange(piece_rows, dtype=jnp.int32)
    row_pick = (flat // mode_cols)[:, None] == jnp.arange(mode_rows, dtype=jnp.int32)[None, :]
    frequency = jnp.sum(jnp.where(row_pick, row_modes[None, :], 0), axis=1)
    column_pick = (
        (flat % mode_cols)[:, None] == jnp.arange(mode_cols, dtype=jnp.int32)[None, :]
    ).astype(jnp.float32)
    turns = positions[:, None] * frequency[None, :] % height
    angles = turns.astype(jnp.float32) * (2.0 * math.pi / height)
    cos_part = jnp.cos(angles)
    sin_part = jnp.sin(angles)
    cos_pick = cos_part[:, :, None] * column_pick[None, :, :]
    sin_pick = sin_part[:, :, None] * column_pick[None, :, :]
    real_sum = precise("hnm,nc->hcm", cos_pick, real_piece) - precise(
        "hnm,nc->hcm", sin_pick, imag_piece
    )
    imag_sum = precise("hnm,nc->hcm", cos_pick, imag_piece) + precise(
        "hnm,nc->hcm", sin_pick, real_piece
    )
    cos_col, sin_col = column_tables(col_modes, columns)
    image = precise("hcm,wm->hcw", real_sum, cos_col) - precise("hcm,wm->hcw", imag_sum, sin_col)
    return image.astype(jnp.bfloat16)


def mix_modes(real_in, imag_in, weight_real, weight_imag, factor):
    real_out = (
        precise("nc,nco->no", real_in, weight_real) - precise("nc,nco->no", imag_in, weight_imag)
    ) * factor
    imag_out = (
        precise("nc,nco->no", real_in, weight_imag) + precise("nc,nco->no", imag_in, weight_real)
    ) * factor
    return (real_out, imag_out)


def mix_modes_back(real_in, imag_in, weight_real, weight_imag, factor):
    real_out = (
        precise("no,nco->nc", real_in, weight_real) + precise("no,nco->nc", imag_in, weight_imag)
    ) * factor
    imag_out = (
        precise("no,nco->nc", imag_in, weight_real) - precise("no,nco->nc", real_in, weight_imag)
    ) * factor
    return (real_out, imag_out)


def greet_ring(receives_from):
    barrier = pltpu.get_barrier_semaphore()
    pl.semaphore_signal(barrier, inc=1, device_id={"row": receives_from}, device_id_type=MESH)
    pl.semaphore_wait(barrier, 1)


def analysis_kernel(
    size,
    values,
    taps,
    filter_1,
    filter_2,
    filter_3,
    out_1,
    out_2,
    out_3,
    halo_1,
    halo_2,
    halo_3,
    send_sem,
    recv_sem,
):
    me = lax.axis_index("row")
    above, below = lax.rem(me + size - 1, size), lax.rem(me + 1, size)
    greet_ring(below)

    def copy(level, source, halo):
        return pltpu.make_async_remote_copy(
            src_ref=source,
            dst_ref=halo,
            send_sem=send_sem.at[level],
            recv_sem=recv_sem.at[level],
            device_id={"row": above},
            device_id_type=MESH,
        )

    def one(get, row, matrix, out):
        loaded = [as_float(get(2 * row + offset)) for offset in range(4)]
        halves = []
        for branch in range(2):
            running = taps[branch, 0] * loaded[0]
            for offset in range(1, 4):
                running = running + taps[branch, offset] * loaded[offset]
            halves.append(running.astype(jnp.bfloat16))
        both = jnp.concatenate(halves, axis=0)
        done = jnp.dot(both, matrix[...], preferred_element_type=jnp.float32).astype(jnp.bfloat16)
        count = halves[0].shape[0]
        out[0, row] = done[:count]
        out[1, row] = done[count:]

    def span(get, first, last, matrix, out):
        def body(row, carry):
            one(get, row, matrix, out)
            return carry

        lax.fori_loop(first, last, body, 0)

    def edged(get, halo, count):
        return lambda row: get(row) if row < count else halo[row - count]

    count = values.shape[0]
    half_1, half_2 = filter_1.shape[0] // 2, filter_2.shape[0] // 2
    get_1 = lambda row: values[row]
    get_2 = lambda row: out_1[0, row, :, :half_1]
    get_3 = lambda row: out_2[0, row, :, :half_2]
    first = copy(0, values.at[pl.ds(0, 2)], halo_1)
    first.start()
    span(get_1, 0, 2, filter_1, out_1)
    second = copy(1, out_1.at[0, pl.ds(0, 2), :, pl.ds(0, half_1)], halo_2)
    second.start()
    early = min(6, count // 2 - 1)
    span(get_1, 2, early, filter_1, out_1)
    span(get_2, 0, 2, filter_2, out_2)
    third = copy(2, out_2.at[0, pl.ds(0, 2), :, pl.ds(0, half_2)], halo_3)
    third.start()
    span(get_1, early, count // 2 - 1, filter_1, out_1)
    first.wait()
    one(edged(get_1, halo_1, count), count // 2 - 1, filter_1, out_1)
    span(get_2, 2, count // 4 - 1, filter_2, out_2)
    second.wait()
    one(edged(get_2, halo_2, count // 2), count // 4 - 1, filter_2, out_2)
    span(get_3, 0, count // 8 - 1, filter_3, out_3)
    third.wait()
    one(edged(get_3, halo_3, count // 4), count // 8 - 1, filter_3, out_3)


def analysis_call(values, row_filters, matrices, back):
    size = lax.axis_size("row")
    count, channels, columns = values.shape
    vmem = pl.BlockSpec(memory_space=pltpu.VMEM)
    widths = [columns >> level for level in range(3)]
    return pl.pallas_call(
        functools.partial(analysis_kernel, size),
        out_shape=tuple(
            jax.ShapeDtypeStruct((2, count >> level + 1, channels, widths[level]), jnp.bfloat16)
            for level in range(3)
        ),
        in_specs=[vmem, pl.BlockSpec(memory_space=pltpu.SMEM), vmem, vmem, vmem],
        out_specs=(vmem, vmem, vmem),
        scratch_shapes=[
            *(pltpu.VMEM((2, channels, width), jnp.bfloat16) for width in widths),
            pltpu.SemaphoreType.DMA((3,)),
            pltpu.SemaphoreType.DMA((3,)),
        ],
        compiler_params=pltpu.CompilerParams(
            collective_id=3 if back else 2,
            has_side_effects=True,
            vmem_limit_bytes=24 * 1024 * 1024,
        ),
        cost_estimate=pl.CostEstimate(
            flops=6 * values.size * columns, bytes_accessed=16 * values.size, transcendentals=0
        ),
        name="analysis_back" if back else "analysis",
    )(values, row_filters, *matrices)


def gelu_slope(value):
    scale = math.sqrt(2.0 / math.pi)
    square = value * value
    bend = jnp.tanh(scale * (value + 0.044715 * (square * value)))
    return 0.5 * (1.0 + bend) + 0.5 * value * (1.0 - bend * bend) * (
        scale * (1.0 + 3 * 0.044715 * square)
    )


def synthesis_kernel(
    size,
    back,
    image,
    out_1,
    out_2,
    out_3,
    taps,
    turned_1,
    turned_2,
    turned_3,
    detail,
    skip,
    plain,
    *rest,
):
    if back:
        share, result, gathered, send_more, recv_more, *rest = rest
    else:
        cotangent, result, detail_turned, skip_turned, *rest = rest
        for level in range(3):
            for member in range(3):
                detail_turned[level, member] = as_float(detail[level, member]).T.astype(
                    jnp.bfloat16
                )
        skip_turned[...] = as_float(skip[...]).T.astype(jnp.bfloat16)
        detail, skip = detail_turned, skip_turned
    syn_1, syn_2, syn_3, halo_1, halo_2, halo_3, top_1, top_2, send_sem, recv_sem = rest
    me = lax.axis_index("row")
    above, below = lax.rem(me + size - 1, size), lax.rem(me + 1, size)
    if back:
        greet_all(size)
        hear_all(size)
    else:
        greet_ring(above)

    def copy(level, syn, halo):
        return pltpu.make_async_remote_copy(
            src_ref=syn.at[:, syn.shape[1] - 1],
            dst_ref=halo,
            send_sem=send_sem.at[level],
            recv_sem=recv_sem.at[level],
            device_id={"row": below},
            device_id_type=MESH,
        )

    def mixed(level, member, band):
        return jnp.dot(detail[level, member], band, preferred_element_type=jnp.float32).astype(
            jnp.bfloat16
        )

    def one(level, row, top, out, turned, syn):
        half = out.shape[3] // 2
        if half % 128 == 0:
            low = [top[row], mixed(level, 0, out[0, row, :, half:])]
            high = [mixed(level, 1, out[1, row, :, :half]), mixed(level, 2, out[1, row, :, half:])]
            low, high = jnp.concatenate(low, axis=1), jnp.concatenate(high, axis=1)
        else:
            bands, lower = out[1, row], lax.broadcasted_iota(jnp.int32, out.shape[2:], 1) < half
            low = jnp.where(lower, as_float(top[row]), as_float(mixed(level, 0, out[0, row])))
            high = jnp.where(
                lower, as_float(mixed(level, 1, bands)), as_float(mixed(level, 2, bands))
            )
            low, high = low.astype(jnp.bfloat16), high.astype(jnp.bfloat16)
        both = jnp.concatenate([low, high], axis=0)
        done = lax.dot_general(
            both, turned[...], NT, preferred_element_type=jnp.float32
        ).astype(jnp.bfloat16)
        count = low.shape[0]
        syn[0, row] = done[:count]
        syn[1, row] = done[count:]

    def joined(syn, row, previous):
        low_now, high_now = as_float(syn[0, row]), as_float(syn[1, row])
        low_prev, high_prev = as_float(previous(0)), as_float(previous(1))
        pair = []
        for parity in range(2):
            running = taps[0, parity] * low_now + taps[1, parity] * high_now
            running = running + taps[0, parity + 2] * low_prev
            pair.append(running + taps[1, parity + 2] * high_prev)
        return pair

    def combine(syn, row, halo, top):
        previous = (lambda part: halo[part]) if halo is not None else lambda part: syn[part, row - 1]
        pair = joined(syn, row, previous)
        for parity in range(2):
            top[2 * row + parity] = pair[parity].astype(jnp.bfloat16)

    def last(row, halo):
        previous = (
            (lambda part: halo[part]) if halo is not None else lambda part: syn_1[part, row - 1]
        )
        pair = joined(syn_1, row, previous)
        for parity in range(2):
            here = 2 * row + parity
            value = pair[parity] + jnp.dot(
                skip[...], plain[here], preferred_element_type=jnp.float32
            )
            if not back:
                value = (as_float(cotangent[here]) * gelu_slope(value)).astype(jnp.bfloat16)
            result[here] = value

    def span(first, stop, call):
        def body(row, carry):
            call(row)
            return carry

        lax.fori_loop(first, stop, body, 0)

    level_3 = lambda row: one(2, row, image, out_3, turned_3, syn_3)
    level_2 = lambda row: one(1, row, top_2, out_2, turned_2, syn_2)
    level_1 = lambda row: one(0, row, top_1, out_1, turned_1, syn_1)
    rows_3, rows_2, rows_1 = syn_3.shape[1], syn_2.shape[1], syn_1.shape[1]
    level_3(rows_3 - 1)
    third = copy(2, syn_3, halo_3)
    third.start()
    if back:
        chunk = share.shape[0]
        target = pl.ds(pl.multiple_of(me * chunk, chunk), chunk)
        for step in range(1, size):
            pltpu.make_async_remote_copy(
                src_ref=share,
                dst_ref=gathered.at[target],
                send_sem=send_more.at[0],
                recv_sem=recv_more.at[0],
                device_id={"row": lax.rem(me + step, size)},
                device_id_type=MESH,
            ).start()
        gathered[target, :] = share[...]
    span(0, rows_3 - 1, level_3)
    combine(syn_3, rows_3 - 1, None, top_2)
    level_2(rows_2 - 1)
    second = copy(1, syn_2, halo_2)
    second.start()
    level_2(rows_2 - 2)
    combine(syn_2, rows_2 - 1, None, top_1)
    level_1(rows_1 - 1)
    first = copy(0, syn_1, halo_1)
    first.start()
    level_1(rows_1 - 2)
    last(rows_1 - 1, None)
    span(1, rows_3 - 1, lambda row: combine(syn_3, row, None, top_2))
    third.wait()
    combine(syn_3, 0, halo_3, top_2)
    span(0, rows_2 - 2, level_2)
    span(1, rows_2 - 1, lambda row: combine(syn_2, row, None, top_1))
    span(2, rows_1 - 2, level_1)
    span(3, rows_1 - 1, lambda row: last(row, None))
    second.wait()
    combine(syn_2, 0, halo_2, top_1)
    span(0, 2, level_1)
    span(1, 3, lambda row: last(row, None))
    first.wait()
    last(0, halo_1)
    if back:
        tiles_copy(size, chunk, gathered, gathered, send_more.at[0], recv_more.at[0], 0).wait()


def synthesis_call(image, bands, row_filters, matrices, detail, skip, plain, extra, back):
    size = lax.axis_size("row")
    vmem = pl.BlockSpec(memory_space=pltpu.VMEM)
    smem = pl.BlockSpec(memory_space=pltpu.SMEM)
    channels = plain.shape[1]
    result = jax.ShapeDtypeStruct(plain.shape, jnp.float32 if back else jnp.bfloat16)
    own = [pltpu.VMEM(detail.shape, jnp.bfloat16), pltpu.VMEM(skip.shape, jnp.bfloat16)]
    if back:
        whole = (extra.shape[0] * size, channels)
        result = (result, jax.ShapeDtypeStruct(whole, jnp.bfloat16))
        own = [pltpu.SemaphoreType.DMA((1,)), pltpu.SemaphoreType.DMA((1,))]
    return pl.pallas_call(
        functools.partial(synthesis_kernel, size, back),
        out_shape=result,
        in_specs=[vmem] * 4 + [smem] + [vmem] * 7,
        out_specs=(vmem, vmem) if back else vmem,
        scratch_shapes=[
            *own,
            *(pltpu.VMEM(band.shape, jnp.bfloat16) for band in bands),
            *(pltpu.VMEM((2, channels, band.shape[3]), jnp.bfloat16) for band in bands),
            pltpu.VMEM((plain.shape[0] // 2, channels, bands[0].shape[3] // 2), jnp.bfloat16),
            pltpu.VMEM((plain.shape[0] // 4, channels, bands[1].shape[3] // 2), jnp.bfloat16),
            pltpu.SemaphoreType.DMA((3,)),
            pltpu.SemaphoreType.DMA((3,)),
        ],
        compiler_params=pltpu.CompilerParams(
            collective_id=5 if back else 4,
            has_side_effects=True,
            vmem_limit_bytes=48 * 1024 * 1024,
        ),
        cost_estimate=pl.CostEstimate(
            flops=6 * plain.size * plain.shape[2],
            bytes_accessed=32 * plain.size,
            transcendentals=plain.size,
        ),
        name="synthesis_back" if back else "synthesis",
    )(image, *bands, row_filters, *matrices, detail, skip, plain, extra)


def split_bands(full):
    band_list = []
    for both in full:
        half = both.shape[3] // 2
        band_list.append((both[0, :, :, half:], both[1, :, :, :half], both[1, :, :, half:]))
    return full[2][0, :, :, : full[2].shape[3] // 2], band_list


def per_device(
    field,
    cotangent,
    row_filters,
    col_filter_1,
    col_filter_2,
    col_filter_3,
    detail_weight,
    skip_weight,
    spectral_weight,
    row_modes,
    col_modes,
):
    matrices = (col_filter_1, col_filter_2, col_filter_3)
    devices = lax.axis_size("row")
    full_field = analysis_call(field, row_filters, matrices, False)
    coarse_field, bands_field = split_bands(full_field)
    total_rows, total_cols = field.shape[0] * devices, field.shape[2]
    scales = [
        1.0 / math.sqrt((total_rows >> octave + 1) * (total_cols >> octave + 1))
        for octave in range(3)
    ] + [1.0 / math.sqrt(total_rows * total_cols)]
    sum_rows = 10 * field.shape[1]
    sum_rows = -(-sum_rows // (16 * devices)) * 16 * devices
    local_rows, channels, columns = coarse_field.shape
    height = local_rows * devices
    factor = 1.0 / (height * columns)
    weight_real = spectral_weight[0]
    weight_imag = spectral_weight[1]
    mode_rows, mode_cols = row_modes.shape[0], col_modes.shape[0]
    whole_tiles = (
        mode_rows % devices == 0
        and mode_cols % devices == 0
        and (2 * local_rows * mode_cols // devices) % 8 == 0
        and (2 * (mode_rows // devices) * (mode_cols // devices)) % 8 == 0
    )
    if whole_tiles:
        near_cols = mode_cols // devices
        tables = spectral_tables(row_modes, col_modes, local_rows, columns, devices)
        coarse_image, spec_field = spectral_path(
            full_field[2], spectral_weight, tables, near_cols, (), scales, sum_rows
        )
    else:
        spec_real, spec_imag = owned_modes(coarse_field, row_modes, col_modes)
        out_real, out_imag = mix_modes(spec_real, spec_imag, weight_real, weight_imag, factor)
        coarse_image = owned_image(out_real, out_imag, row_modes, col_modes, local_rows, columns)
        coarse_image = jnp.pad(coarse_image, ((0, 0), (0, 0), (0, columns)))
    upstream = synthesis_call(
        coarse_image,
        full_field,
        row_filters,
        matrices,
        detail_weight,
        skip_weight,
        field,
        cotangent,
        False,
    )
    full_slope = analysis_call(upstream, row_filters, matrices, True)
    coarse_slope, bands_slope = split_bands(full_slope)
    if whole_tiles:
        extra = (*full_field, *full_slope[:2], field, upstream)
        image_back, spec_back, share = spectral_path(
            full_slope[2], spectral_weight, tables, near_cols, extra, scales, sum_rows
        )
    else:
        back_real, back_imag = owned_modes(coarse_slope, row_modes, col_modes)
        turned_real, turned_imag = mix_modes_back(
            back_real, back_imag, weight_real, weight_imag, factor
        )
        image_back = owned_image(
            turned_real, turned_imag, row_modes, col_modes, local_rows, columns
        )
        image_back = jnp.pad(image_back, ((0, 0), (0, 0), (0, columns)))
        shares = [
            narrow("hcw,how->co", bands_field[octave][member], bands_slope[octave][member])
            * scales[octave]
            for octave in range(3)
            for member in range(3)
        ] + [narrow("hcw,how->co", field, upstream) * scales[3]]
        sums = jnp.concatenate(shares, axis=0)
        sums = jnp.pad(sums, ((0, sum_rows - sums.shape[0]), (0, 0)))
        share = lax.psum_scatter(sums, "row", scatter_dimension=0, tiled=True)
        share = share.astype(jnp.bfloat16)
    grad_field, gathered = synthesis_call(
        image_back,
        full_slope,
        row_filters,
        matrices,
        detail_weight,
        skip_weight,
        upstream,
        share,
        True,
    )
    gathered = as_float(gathered[: 10 * channels])
    grad_detail = gathered[: 9 * channels].reshape(3, 3, channels, channels)
    grad_skip = gathered[9 * channels :]
    if whole_tiles:
        near_rows = mode_rows // devices
        grad_spectral = outer_products(spec_field, spec_back, near_rows, near_cols, factor)
    else:
        grad_real = (
            spec_real[:, :, None] * back_real[:, None, :]
            + spec_imag[:, :, None] * back_imag[:, None, :]
        ) * factor
        grad_imag = (
            spec_real[:, :, None] * back_imag[:, None, :]
            - spec_imag[:, :, None] * back_real[:, None, :]
        ) * factor
        grad_spectral = jnp.stack([grad_real, grad_imag])
    return (grad_field, grad_detail, grad_skip, grad_spectral)


def solution(mesh):
    placed = (
        P(("groups", "row"), None, None),
        P(("groups", "row"), None, None),
        P(),
        P(),
        P(),
        P(),
        P(),
        P(),
        P(None, "row", None, None),
        P(),
        P(),
    )
    return jax.shard_map(
        per_device,
        mesh=mesh,
        in_specs=placed,
        out_specs=(
            P(("groups", "row"), None, None),
            P("groups", None, None, None),
            P("groups", None),
            P("groups", "row", None, None),
        ),
        check_vma=False,
    )
```

```python
import functools
import math

import jax
import jax.numpy as jnp
from jax import lax
from jax.experimental import pallas as pl
from jax.experimental.pallas import tpu as pltpu
from jax.sharding import PartitionSpec as P

MESH = pl.DeviceIdType.MESH
NN = (((1,), (0,)), ((), ()))
NT = (((1,), (1,)), ((), ()))


def greet_all(size):
    me = lax.axis_index("row")
    barrier = pltpu.get_barrier_semaphore()
    for step in range(1, size):
        pl.semaphore_signal(
            barrier, inc=1, device_id={"row": lax.rem(me + step, size)}, device_id_type=MESH
        )


def hear_all(size):
    pl.semaphore_wait(pltpu.get_barrier_semaphore(), size - 1)


def tiles_copy(size, tile, send, land, send_sem, recv_sem, step):
    me = lax.axis_index("row")
    if step:
        partner = lax.rem(me + step, size)
        source = pl.ds(pl.multiple_of(partner * tile, tile), tile)
        target = pl.ds(pl.multiple_of(me * tile, tile), tile)
    else:
        partner = lax.rem(me + 1, size)
        source = target = pl.ds(0, (size - 1) * tile)
    return pltpu.make_async_remote_copy(
        src_ref=send.at[source],
        dst_ref=land.at[target],
        send_sem=send_sem,
        recv_sem=recv_sem,
        device_id={"row": partner},
        device_id_type=MESH,
    )


def start_exchange(size, tile, send, land, send_sem, recv_sem):
    me = lax.axis_index("row")
    for step in range(1, size):
        tiles_copy(size, tile, send, land, send_sem, recv_sem, step).start()
    own = pl.ds(pl.multiple_of(me * tile, tile), tile)
    land[own, :] = send[own, :]
    return tiles_copy(size, tile, send, land, send_sem, recv_sem, 0)


def channel_product(first, second):
    return lax.dot_general(first, second, NT, preferred_element_type=jnp.float32)


def local_sums(full_field, full_slope, skip_share, sums, scales, skip_scale):
    channels = skip_share.shape[0]
    for level in range(3):
        left, right = full_field[level], full_slope[level]
        half = left.shape[3] // 2
        if half % 128 == 0:
            halves = (slice(half, None), slice(0, half), slice(half, None))
        else:
            halves = (None, None, None)
        for member, (branch, part) in enumerate(zip((0, 1, 1), halves)):

            def body(row, total):
                if part is not None:
                    return total + channel_product(
                        left[branch, row, :, part], right[branch, row, :, part]
                    )
                lane = lax.broadcasted_iota(jnp.int32, left.shape[2:], 1)
                kept = (lane < half) if member == 1 else (lane >= half)
                wide = jnp.where(kept, as_float(left[branch, row]), 0.0).astype(jnp.bfloat16)
                return total + channel_product(wide, right[branch, row])

            total = lax.fori_loop(
                0, left.shape[1], body, jnp.zeros((channels, channels), jnp.float32)
            )
            start = (level * 3 + member) * channels
            sums[start : start + channels, :] = (total * scales[level]).astype(jnp.bfloat16)
    sums[9 * channels : 10 * channels, :] = (skip_share[...] * skip_scale).astype(
        jnp.bfloat16
    )
    if sums.shape[0] > 10 * channels:
        sums[10 * channels :, :] = jnp.zeros(
            (sums.shape[0] - 10 * channels, channels), jnp.bfloat16
        )


def spectral_kernel(
    size,
    near_cols,
    back,
    scales,
    coarse_ref,
    col_ref,
    row_ref,
    row_inv_ref,
    col_inv_ref,
    weight,
    *rest,
):
    if back:
        full_field, full_slope = rest[:3], (*rest[3:5], coarse_ref)
        skip_share, image_ref, spec_ref, share, sums, landed, more_sem, *rest = rest[5:]
    else:
        image_ref, spec_ref, *rest = rest
    (
        send_a,
        land_a,
        send_b,
        send_c,
        land_c,
        send_d,
        land_d,
        rotated,
        send_sem,
        recv_sem,
    ) = rest
    greet_all(size)
    rows = coarse_ref.shape[1]
    total = None
    for row in range(rows):
        part = lax.dot_general(
            col_ref[row].astype(jnp.bfloat16),
            coarse_ref[0, row],
            NT,
            preferred_element_type=jnp.float32,
        )
        total = part if total is None else total + part
    send_a[...] = total
    hear_all(size)
    tile_a = send_a.shape[0] // size
    first = start_exchange(size, tile_a, send_a, land_a, send_sem.at[0], recv_sem.at[0])
    if back:
        local_sums(full_field, full_slope, skip_share, sums, scales[:3], scales[3])
    first.wait_recv()
    send_b[...] = lax.dot_general(
        row_ref[...].astype(jnp.bfloat16),
        land_a[...].astype(jnp.bfloat16),
        NN,
        preferred_element_type=jnp.float32,
    )
    tile_b = send_b.shape[0] // size
    second = start_exchange(size, tile_b, send_b, spec_ref, send_sem.at[1], recv_sem.at[1])
    if back:
        chunk = sums.shape[0] // size
        scatter = start_exchange(size, chunk, sums, landed, more_sem.at[0], more_sem.at[1])
    second.wait_recv()
    spec = spec_ref[...]
    count = spec.shape[0]
    even = lax.broadcasted_iota(jnp.int32, spec.shape, 0) % 2 == 0
    turned = jnp.where(even, -pltpu.roll(spec, count - 1, 0), pltpu.roll(spec, 1, 0))
    rotated[...] = -turned if back else turned
    per_tile = tile_b // 2
    modes = weight.shape[1]
    per_row = near_cols
    mode_rows = per_tile // per_row
    dims = NT if back else NN

    def mix(source, carry):
        here = pl.ds(pl.multiple_of(source * tile_b, tile_b), tile_b)
        plain = spec_ref[here, :].astype(jnp.bfloat16)
        turn = rotated[here, :].astype(jnp.bfloat16)
        pair = lax.broadcasted_iota(jnp.int32, (tile_b, plain.shape[1]), 0) // 2
        result = jnp.zeros((tile_b, plain.shape[1]), jnp.float32)
        both = jnp.concatenate([plain, turn], axis=1)
        channels = plain.shape[1]
        for member in range(0, per_tile, 2):
            blocks = []
            for one in (member, member + 1):
                mode = (one // per_row) * (modes // mode_rows) + source * per_row + one % per_row
                blocks.append(
                    jnp.concatenate(
                        [weight[part, mode].astype(jnp.bfloat16) for part in range(2)],
                        axis=1 if back else 0,
                    )
                )
            done = lax.dot_general(
                both,
                jnp.concatenate(blocks, axis=0 if back else 1),
                dims,
                preferred_element_type=jnp.float32,
            )
            result = jnp.where(pair == member, done[:, :channels], result)
            result = jnp.where(pair == member + 1, done[:, channels:], result)
        send_c[here, :] = result
        return carry

    lax.fori_loop(0, size, mix, 0, unroll=2)
    third = start_exchange(size, tile_b, send_c, land_c, send_sem.at[2], recv_sem.at[2])
    third.wait_recv()
    send_d[...] = lax.dot_general(
        row_inv_ref[...].astype(jnp.bfloat16),
        land_c[...].astype(jnp.bfloat16),
        NN,
        preferred_element_type=jnp.float32,
    )
    fourth = start_exchange(size, tile_a, send_d, land_d, send_sem.at[3], recv_sem.at[3])
    if back:
        scatter.wait_recv()
        whole = as_float(landed[0:chunk, :])
        for step in range(1, size):
            whole = whole + as_float(landed[step * chunk : (step + 1) * chunk, :])
        share[...] = whole.astype(jnp.bfloat16)
        scatter.wait_send()
    fourth.wait_recv()
    across = land_d[...].T.astype(jnp.bfloat16)
    for row in range(rows):
        image_ref[row] = lax.dot_general(
            across,
            col_inv_ref[row].astype(jnp.bfloat16),
            NN,
            preferred_element_type=jnp.float32,
        ).astype(jnp.bfloat16)
    for sent in (first, second, third, fourth):
        sent.wait_send()


def picked(modes, places):
    same = places[:, None] == jnp.arange(modes.shape[0])[None, :]
    return jnp.sum(jnp.where(same, modes[None, :], 0), axis=1)


def spectral_tables(row_modes, col_modes, local_rows, columns, size):
    height = local_rows * size
    mode_rows, mode_cols = row_modes.shape[0], col_modes.shape[0]
    near_rows, near_cols = mode_rows // size, mode_cols // size
    count_a, count_b = height * near_cols * 2, mode_rows * near_cols * 2
    where_a, where_b = jnp.arange(count_a), jnp.arange(count_b)
    part_a, part_b = where_a % 2, where_b % 2
    spot = where_a // 2
    block = spot // (near_cols * local_rows)
    col_of = picked(col_modes, block * near_cols + spot % near_cols)
    wide = jnp.arange(2 * columns)
    turns = (col_of[:, None] * wide[None, :] + part_a[:, None] * (columns // 4)) % columns
    col = jnp.cos(turns.astype(jnp.float32) * (2.0 * math.pi / columns))
    same_row = (spot // near_cols % local_rows)[None, :] == jnp.arange(local_rows)[:, None]
    inside = wide < columns
    col = jnp.where(same_row[:, :, None] & inside[None, None, :], col[None], 0.0)
    col_inv = col
    row_of = picked(row_modes, where_b // (2 * near_cols))
    quarter = (part_b[:, None] - part_a[None, :]) * (height // 4)
    turns = (row_of[:, None] * (where_a // (2 * near_cols))[None, :] + quarter + height) % height
    same_col = (where_b // 2 % near_cols)[:, None] == (where_a // 2 % near_cols)[None, :]
    row = jnp.cos(turns.astype(jnp.float32) * (2.0 * math.pi / height))
    row = jnp.where(same_col, row, 0.0)
    row_inv = row.T * (1.0 / (height * columns))
    return col, row, row_inv, col_inv


def spectral_path(coarse, weight, tables, near_cols, extra, scales, sum_rows):
    back = len(extra) > 0
    col, row, row_inv, col_inv = tables
    size = lax.axis_size("row")
    channels = coarse.shape[2]
    count_a, count_b = col.shape[1], row.shape[0]
    f32 = jnp.float32
    vmem = pl.BlockSpec(memory_space=pltpu.VMEM)
    return pl.pallas_call(
        functools.partial(spectral_kernel, size, near_cols, back, scales),
        out_shape=(
            jax.ShapeDtypeStruct(coarse.shape[1:], jnp.bfloat16),
            jax.ShapeDtypeStruct((count_b, channels), f32),
            *([jax.ShapeDtypeStruct((sum_rows // size, channels), jnp.bfloat16)] if back else []),
        ),
        in_specs=[vmem] * (6 + len(extra)),
        out_specs=(vmem,) * (3 if back else 2),
        scratch_shapes=[
            *(
                [
                    pltpu.VMEM((sum_rows, channels), jnp.bfloat16),
                    pltpu.VMEM((sum_rows, channels), jnp.bfloat16),
                    pltpu.SemaphoreType.DMA((2,)),
                ]
                if back
                else []
            ),
            pltpu.VMEM((count_a, channels), f32),
            pltpu.VMEM((count_a, channels), f32),
            pltpu.VMEM((count_b, channels), f32),
            pltpu.VMEM((count_b, channels), f32),
            pltpu.VMEM((count_b, channels), f32),
            pltpu.VMEM((count_a, channels), f32),
            pltpu.VMEM((count_a, channels), f32),
            pltpu.VMEM((count_b, channels), f32),
            pltpu.SemaphoreType.DMA((4,)),
            pltpu.SemaphoreType.DMA((4,)),
        ],
        compiler_params=pltpu.CompilerParams(
            collective_id=1 if back else 0,
            has_side_effects=True,
            vmem_limit_bytes=24 * 1024 * 1024,
        ),
        cost_estimate=pl.CostEstimate(
            flops=8 * weight.size, bytes_accessed=4 * weight.size, transcendentals=0
        ),
        name="spectral_back" if back else "spectral",
    )(coarse, col, row, row_inv, col_inv, weight, *extra)


def spec_parts(spec, mode_rows, mode_cols, size):
    channels = spec.shape[1]
    grid = spec.reshape(size, mode_rows // size, mode_cols // size, 2, channels)
    grid = jnp.transpose(grid, (3, 1, 0, 2, 4)).reshape(2, -1, channels)
    return grid[0], grid[1]


def as_float(values):
    return values.astype(jnp.float32)


def precise(form, first_in, second_in):
    return jnp.einsum(form, first_in, second_in, precision=lax.Precision.HIGHEST)


def narrow(form, first_in, second_in):
    return jnp.einsum(form, first_in, second_in, preferred_element_type=jnp.float32)


def column_tables(col_modes, length):
    positions = jnp.arange(length, dtype=jnp.int32)
    turns = positions[:, None] * col_modes[None, :] % length
    angles = turns.astype(jnp.float32) * (2.0 * math.pi / length)
    return (jnp.cos(angles), jnp.sin(angles))


def row_tables(row_modes, positions, length):
    turns = row_modes[:, None] * positions[None, :] % length
    angles = turns.astype(jnp.float32) * (2.0 * math.pi / length)
    return (jnp.cos(angles), jnp.sin(angles))


def owned_modes(coarse, row_modes, col_modes):
    local_rows, channels, columns = coarse.shape
    devices = lax.axis_size("row")
    height = local_rows * devices
    cos_col, sin_col = column_tables(col_modes, columns)
    values = as_float(coarse)
    real_one = precise("hcw,wm->hcm", values, cos_col)
    imag_one = -precise("hcw,wm->hcm", values, sin_col)
    positions = lax.axis_index("row") * local_rows + jnp.arange(local_rows, dtype=jnp.int32)
    cos_row, sin_row = row_tables(row_modes, positions, height)
    real_two = precise("ph,hcm->pmc", cos_row, real_one) + precise("ph,hcm->pmc", sin_row, imag_one)
    imag_two = precise("ph,hcm->pmc", cos_row, imag_one) - precise("ph,hcm->pmc", sin_row, real_one)
    term_all = jnp.stack([real_two.reshape(-1, channels), imag_two.reshape(-1, channels)], axis=1)
    owned = lax.psum_scatter(term_all, "row", scatter_dimension=0, tiled=True)
    return (owned[:, 0], owned[:, 1])


def owned_image(real_owned, imag_owned, row_modes, col_modes, local_rows, columns):
    devices = lax.axis_size("row")
    height = local_rows * devices
    mode_rows = row_modes.shape[0]
    mode_cols = col_modes.shape[0]
    positions = lax.axis_index("row") * local_rows + jnp.arange(local_rows, dtype=jnp.int32)
    real_piece = lax.all_gather(real_owned, "row", axis=0, tiled=True)
    imag_piece = lax.all_gather(imag_owned, "row", axis=0, tiled=True)
    piece_rows = real_piece.shape[0]
    flat = jnp.arange(piece_rows, dtype=jnp.int32)
    row_pick = (flat // mode_cols)[:, None] == jnp.arange(mode_rows, dtype=jnp.int32)[None, :]
    frequency = jnp.sum(jnp.where(row_pick, row_modes[None, :], 0), axis=1)
    column_pick = (
        (flat % mode_cols)[:, None] == jnp.arange(mode_cols, dtype=jnp.int32)[None, :]
    ).astype(jnp.float32)
    turns = positions[:, None] * frequency[None, :] % height
    angles = turns.astype(jnp.float32) * (2.0 * math.pi / height)
    cos_part = jnp.cos(angles)
    sin_part = jnp.sin(angles)
    cos_pick = cos_part[:, :, None] * column_pick[None, :, :]
    sin_pick = sin_part[:, :, None] * column_pick[None, :, :]
    real_sum = precise("hnm,nc->hcm", cos_pick, real_piece) - precise(
        "hnm,nc->hcm", sin_pick, imag_piece
    )
    imag_sum = precise("hnm,nc->hcm", cos_pick, imag_piece) + precise(
        "hnm,nc->hcm", sin_pick, real_piece
    )
    cos_col, sin_col = column_tables(col_modes, columns)
    image = precise("hcm,wm->hcw", real_sum, cos_col) - precise("hcm,wm->hcw", imag_sum, sin_col)
    return image.astype(jnp.bfloat16)


def mix_modes(real_in, imag_in, weight_real, weight_imag, factor):
    real_out = (
        precise("nc,nco->no", real_in, weight_real) - precise("nc,nco->no", imag_in, weight_imag)
    ) * factor
    imag_out = (
        precise("nc,nco->no", real_in, weight_imag) + precise("nc,nco->no", imag_in, weight_real)
    ) * factor
    return (real_out, imag_out)


def mix_modes_back(real_in, imag_in, weight_real, weight_imag, factor):
    real_out = (
        precise("no,nco->nc", real_in, weight_real) + precise("no,nco->nc", imag_in, weight_imag)
    ) * factor
    imag_out = (
        precise("no,nco->nc", imag_in, weight_real) - precise("no,nco->nc", real_in, weight_imag)
    ) * factor
    return (real_out, imag_out)


def greet_ring(receives_from):
    barrier = pltpu.get_barrier_semaphore()
    pl.semaphore_signal(barrier, inc=1, device_id={"row": receives_from}, device_id_type=MESH)
    pl.semaphore_wait(barrier, 1)


def analysis_kernel(
    size,
    values,
    taps,
    filter_1,
    filter_2,
    filter_3,
    out_1,
    out_2,
    out_3,
    halo_1,
    halo_2,
    halo_3,
    send_sem,
    recv_sem,
):
    me = lax.axis_index("row")
    above, below = lax.rem(me + size - 1, size), lax.rem(me + 1, size)
    greet_ring(below)

    def copy(level, source, halo):
        return pltpu.make_async_remote_copy(
            src_ref=source,
            dst_ref=halo,
            send_sem=send_sem.at[level],
            recv_sem=recv_sem.at[level],
            device_id={"row": above},
            device_id_type=MESH,
        )

    def one(get, row, matrix, out):
        loaded = [as_float(get(2 * row + offset)) for offset in range(4)]
        halves = []
        for branch in range(2):
            running = taps[branch, 0] * loaded[0]
            for offset in range(1, 4):
                running = running + taps[branch, offset] * loaded[offset]
            halves.append(running.astype(jnp.bfloat16))
        both = jnp.concatenate(halves, axis=0)
        done = jnp.dot(both, matrix[...], preferred_element_type=jnp.float32).astype(jnp.bfloat16)
        count = halves[0].shape[0]
        out[0, row] = done[:count]
        out[1, row] = done[count:]

    def span(get, first, last, matrix, out):
        def body(row, carry):
            one(get, row, matrix, out)
            return carry

        lax.fori_loop(first, last, body, 0)

    def edged(get, halo, count):
        return lambda row: get(row) if row < count else halo[row - count]

    count = values.shape[0]
    half_1, half_2 = filter_1.shape[0] // 2, filter_2.shape[0] // 2
    get_1 = lambda row: values[row]
    get_2 = lambda row: out_1[0, row, :, :half_1]
    get_3 = lambda row: out_2[0, row, :, :half_2]
    first = copy(0, values.at[pl.ds(0, 2)], halo_1)
    first.start()
    span(get_1, 0, 2, filter_1, out_1)
    second = copy(1, out_1.at[0, pl.ds(0, 2), :, pl.ds(0, half_1)], halo_2)
    second.start()
    early = min(6, count // 2 - 1)
    span(get_1, 2, early, filter_1, out_1)
    span(get_2, 0, 2, filter_2, out_2)
    third = copy(2, out_2.at[0, pl.ds(0, 2), :, pl.ds(0, half_2)], halo_3)
    third.start()
    span(get_1, early, count // 2 - 1, filter_1, out_1)
    first.wait()
    one(edged(get_1, halo_1, count), count // 2 - 1, filter_1, out_1)
    span(get_2, 2, count // 4 - 1, filter_2, out_2)
    second.wait()
    one(edged(get_2, halo_2, count // 2), count // 4 - 1, filter_2, out_2)
    span(get_3, 0, count // 8 - 1, filter_3, out_3)
    third.wait()
    one(edged(get_3, halo_3, count // 4), count // 8 - 1, filter_3, out_3)


def analysis_call(values, row_filters, matrices, back):
    size = lax.axis_size("row")
    count, channels, columns = values.shape
    vmem = pl.BlockSpec(memory_space=pltpu.VMEM)
    widths = [columns >> level for level in range(3)]
    return pl.pallas_call(
        functools.partial(analysis_kernel, size),
        out_shape=tuple(
            jax.ShapeDtypeStruct((2, count >> level + 1, channels, widths[level]), jnp.bfloat16)
            for level in range(3)
        ),
        in_specs=[vmem, pl.BlockSpec(memory_space=pltpu.SMEM), vmem, vmem, vmem],
        out_specs=(vmem, vmem, vmem),
        scratch_shapes=[
            *(pltpu.VMEM((2, channels, width), jnp.bfloat16) for width in widths),
            pltpu.SemaphoreType.DMA((3,)),
            pltpu.SemaphoreType.DMA((3,)),
        ],
        compiler_params=pltpu.CompilerParams(
            collective_id=3 if back else 2,
            has_side_effects=True,
            vmem_limit_bytes=24 * 1024 * 1024,
        ),
        cost_estimate=pl.CostEstimate(
            flops=6 * values.size * columns, bytes_accessed=16 * values.size, transcendentals=0
        ),
        name="analysis_back" if back else "analysis",
    )(values, row_filters, *matrices)


def gelu_slope(value):
    scale = math.sqrt(2.0 / math.pi)
    square = value * value
    bend = jnp.tanh(scale * (value + 0.044715 * (square * value)))
    return 0.5 * (1.0 + bend) + 0.5 * value * (1.0 - bend * bend) * (
        scale * (1.0 + 3 * 0.044715 * square)
    )


def synthesis_kernel(
    size,
    back,
    image,
    out_1,
    out_2,
    out_3,
    taps,
    turned_1,
    turned_2,
    turned_3,
    detail,
    skip,
    plain,
    *rest,
):
    if back:
        share, result, gathered, send_more, recv_more, *rest = rest
    else:
        cotangent, result, skip_share, detail_turned, skip_turned, *rest = rest
        skip_share[...] = jnp.zeros_like(skip_share)
        for level in range(3):
            for member in range(3):
                detail_turned[level, member] = as_float(detail[level, member]).T.astype(
                    jnp.bfloat16
                )
        skip_turned[...] = as_float(skip[...]).T.astype(jnp.bfloat16)
        detail, skip = detail_turned, skip_turned
    syn_1, syn_2, syn_3, halo_1, halo_2, halo_3, top_1, top_2, send_sem, recv_sem = rest
    me = lax.axis_index("row")
    above, below = lax.rem(me + size - 1, size), lax.rem(me + 1, size)
    if back:
        greet_all(size)
        hear_all(size)
    else:
        greet_ring(above)

    def copy(level, syn, halo):
        return pltpu.make_async_remote_copy(
            src_ref=syn.at[:, syn.shape[1] - 1],
            dst_ref=halo,
            send_sem=send_sem.at[level],
            recv_sem=recv_sem.at[level],
            device_id={"row": below},
            device_id_type=MESH,
        )

    def mixed(level, member, band):
        return jnp.dot(detail[level, member], band, preferred_element_type=jnp.float32).astype(
            jnp.bfloat16
        )

    def one(level, row, top, out, turned, syn):
        half = out.shape[3] // 2
        if half % 128 == 0:
            low = [top[row], mixed(level, 0, out[0, row, :, half:])]
            high = [mixed(level, 1, out[1, row, :, :half]), mixed(level, 2, out[1, row, :, half:])]
            low, high = jnp.concatenate(low, axis=1), jnp.concatenate(high, axis=1)
        else:
            bands, lower = out[1, row], lax.broadcasted_iota(jnp.int32, out.shape[2:], 1) < half
            low = jnp.where(lower, as_float(top[row]), as_float(mixed(level, 0, out[0, row])))
            high = jnp.where(
                lower, as_float(mixed(level, 1, bands)), as_float(mixed(level, 2, bands))
            )
            low, high = low.astype(jnp.bfloat16), high.astype(jnp.bfloat16)
        both = jnp.concatenate([low, high], axis=0)
        done = lax.dot_general(
            both, turned[...], NT, preferred_element_type=jnp.float32
        ).astype(jnp.bfloat16)
        count = low.shape[0]
        syn[0, row] = done[:count]
        syn[1, row] = done[count:]

    def joined(syn, row, previous):
        low_now, high_now = as_float(syn[0, row]), as_float(syn[1, row])
        low_prev, high_prev = as_float(previous(0)), as_float(previous(1))
        pair = []
        for parity in range(2):
            running = taps[0, parity] * low_now + taps[1, parity] * high_now
            running = running + taps[0, parity + 2] * low_prev
            pair.append(running + taps[1, parity + 2] * high_prev)
        return pair

    def combine(syn, row, halo, top):
        previous = (lambda part: halo[part]) if halo is not None else lambda part: syn[part, row - 1]
        pair = joined(syn, row, previous)
        for parity in range(2):
            top[2 * row + parity] = pair[parity].astype(jnp.bfloat16)

    def last(row, halo):
        previous = (
            (lambda part: halo[part]) if halo is not None else lambda part: syn_1[part, row - 1]
        )
        pair = joined(syn_1, row, previous)
        for parity in range(2):
            here = 2 * row + parity
            value = pair[parity] + jnp.dot(
                skip[...], plain[here], preferred_element_type=jnp.float32
            )
            if not back:
                value = (as_float(cotangent[here]) * gelu_slope(value)).astype(jnp.bfloat16)
                skip_share[...] += channel_product(plain[here], value)
            result[here] = value

    def span(first, stop, call):
        def body(row, carry):
            call(row)
            return carry

        lax.fori_loop(first, stop, body, 0)

    level_3 = lambda row: one(2, row, image, out_3, turned_3, syn_3)
    level_2 = lambda row: one(1, row, top_2, out_2, turned_2, syn_2)
    level_1 = lambda row: one(0, row, top_1, out_1, turned_1, syn_1)
    rows_3, rows_2, rows_1 = syn_3.shape[1], syn_2.shape[1], syn_1.shape[1]
    level_3(rows_3 - 1)
    third = copy(2, syn_3, halo_3)
    third.start()
    if back:
        chunk = share.shape[0]
        target = pl.ds(pl.multiple_of(me * chunk, chunk), chunk)
        for step in range(1, size):
            pltpu.make_async_remote_copy(
                src_ref=share,
                dst_ref=gathered.at[target],
                send_sem=send_more.at[0],
                recv_sem=recv_more.at[0],
                device_id={"row": lax.rem(me + step, size)},
                device_id_type=MESH,
            ).start()
        gathered[target, :] = share[...]
    span(0, rows_3 - 1, level_3)
    combine(syn_3, rows_3 - 1, None, top_2)
    level_2(rows_2 - 1)
    second = copy(1, syn_2, halo_2)
    second.start()
    level_2(rows_2 - 2)
    combine(syn_2, rows_2 - 1, None, top_1)
    level_1(rows_1 - 1)
    first = copy(0, syn_1, halo_1)
    first.start()
    level_1(rows_1 - 2)
    last(rows_1 - 1, None)
    span(1, rows_3 - 1, lambda row: combine(syn_3, row, None, top_2))
    third.wait()
    combine(syn_3, 0, halo_3, top_2)
    span(0, rows_2 - 2, level_2)
    span(1, rows_2 - 1, lambda row: combine(syn_2, row, None, top_1))
    span(2, rows_1 - 2, level_1)
    span(3, rows_1 - 1, lambda row: last(row, None))
    second.wait()
    combine(syn_2, 0, halo_2, top_1)
    span(0, 2, level_1)
    span(1, 3, lambda row: last(row, None))
    first.wait()
    last(0, halo_1)
    if back:
        tiles_copy(size, chunk, gathered, gathered, send_more.at[0], recv_more.at[0], 0).wait()


def synthesis_call(image, bands, row_filters, matrices, detail, skip, plain, extra, back):
    size = lax.axis_size("row")
    vmem = pl.BlockSpec(memory_space=pltpu.VMEM)
    smem = pl.BlockSpec(memory_space=pltpu.SMEM)
    channels = plain.shape[1]
    result = jax.ShapeDtypeStruct(plain.shape, jnp.float32 if back else jnp.bfloat16)
    own = [pltpu.VMEM(detail.shape, jnp.bfloat16), pltpu.VMEM(skip.shape, jnp.bfloat16)]
    second = jax.ShapeDtypeStruct(skip.shape, jnp.float32)
    if back:
        whole = (extra.shape[0] * size, channels)
        second = jax.ShapeDtypeStruct(whole, jnp.bfloat16)
        own = [pltpu.SemaphoreType.DMA((1,)), pltpu.SemaphoreType.DMA((1,))]
    return pl.pallas_call(
        functools.partial(synthesis_kernel, size, back),
        out_shape=(result, second),
        in_specs=[vmem] * 4 + [smem] + [vmem] * 7,
        out_specs=(vmem, vmem),
        scratch_shapes=[
            *own,
            *(pltpu.VMEM(band.shape, jnp.bfloat16) for band in bands),
            *(pltpu.VMEM((2, channels, band.shape[3]), jnp.bfloat16) for band in bands),
            pltpu.VMEM((plain.shape[0] // 2, channels, bands[0].shape[3] // 2), jnp.bfloat16),
            pltpu.VMEM((plain.shape[0] // 4, channels, bands[1].shape[3] // 2), jnp.bfloat16),
            pltpu.SemaphoreType.DMA((3,)),
            pltpu.SemaphoreType.DMA((3,)),
        ],
        compiler_params=pltpu.CompilerParams(
            collective_id=5 if back else 4,
            has_side_effects=True,
            vmem_limit_bytes=24 * 1024 * 1024,
        ),
        cost_estimate=pl.CostEstimate(
            flops=6 * plain.size * plain.shape[2],
            bytes_accessed=32 * plain.size,
            transcendentals=plain.size,
        ),
        name="synthesis_back" if back else "synthesis",
    )(image, *bands, row_filters, *matrices, detail, skip, plain, extra)


def split_bands(full):
    band_list = []
    for both in full:
        half = both.shape[3] // 2
        band_list.append((both[0, :, :, half:], both[1, :, :, :half], both[1, :, :, half:]))
    return full[2][0, :, :, : full[2].shape[3] // 2], band_list


def per_device(
    field,
    cotangent,
    row_filters,
    col_filter_1,
    col_filter_2,
    col_filter_3,
    detail_weight,
    skip_weight,
    spectral_weight,
    row_modes,
    col_modes,
):
    matrices = (col_filter_1, col_filter_2, col_filter_3)
    devices = lax.axis_size("row")
    full_field = analysis_call(field, row_filters, matrices, False)
    coarse_field, bands_field = split_bands(full_field)
    total_rows, total_cols = field.shape[0] * devices, field.shape[2]
    scales = [
        1.0 / math.sqrt((total_rows >> octave + 1) * (total_cols >> octave + 1))
        for octave in range(3)
    ] + [1.0 / math.sqrt(total_rows * total_cols)]
    sum_rows = 10 * field.shape[1]
    sum_rows = -(-sum_rows // (16 * devices)) * 16 * devices
    local_rows, channels, columns = coarse_field.shape
    height = local_rows * devices
    factor = 1.0 / (height * columns)
    weight_real = spectral_weight[0]
    weight_imag = spectral_weight[1]
    mode_rows, mode_cols = row_modes.shape[0], col_modes.shape[0]
    whole_tiles = (
        mode_rows % devices == 0
        and mode_cols % devices == 0
        and (2 * local_rows * mode_cols // devices) % 8 == 0
        and (2 * (mode_rows // devices) * (mode_cols // devices)) % 8 == 0
    )
    if whole_tiles:
        near_cols = mode_cols // devices
        tables = spectral_tables(row_modes, col_modes, local_rows, columns, devices)
        coarse_image, spec_field = spectral_path(
            full_field[2], spectral_weight, tables, near_cols, (), scales, sum_rows
        )
    else:
        spec_real, spec_imag = owned_modes(coarse_field, row_modes, col_modes)
        out_real, out_imag = mix_modes(spec_real, spec_imag, weight_real, weight_imag, factor)
        coarse_image = owned_image(out_real, out_imag, row_modes, col_modes, local_rows, columns)
        coarse_image = jnp.pad(coarse_image, ((0, 0), (0, 0), (0, columns)))
    upstream, skip_share = synthesis_call(
        coarse_image,
        full_field,
        row_filters,
        matrices,
        detail_weight,
        skip_weight,
        field,
        cotangent,
        False,
    )
    full_slope = analysis_call(upstream, row_filters, matrices, True)
    coarse_slope, bands_slope = split_bands(full_slope)
    if whole_tiles:
        extra = (*full_field, *full_slope[:2], skip_share)
        image_back, spec_back, share = spectral_path(
            full_slope[2], spectral_weight, tables, near_cols, extra, scales, sum_rows
        )
    else:
        back_real, back_imag = owned_modes(coarse_slope, row_modes, col_modes)
        turned_real, turned_imag = mix_modes_back(
            back_real, back_imag, weight_real, weight_imag, factor
        )
        image_back = owned_image(
            turned_real, turned_imag, row_modes, col_modes, local_rows, columns
        )
        image_back = jnp.pad(image_back, ((0, 0), (0, 0), (0, columns)))
        shares = [
            narrow("hcw,how->co", bands_field[octave][member], bands_slope[octave][member])
            * scales[octave]
            for octave in range(3)
            for member in range(3)
        ] + [skip_share * scales[3]]
        sums = jnp.concatenate(shares, axis=0)
        sums = jnp.pad(sums, ((0, sum_rows - sums.shape[0]), (0, 0)))
        share = lax.psum_scatter(sums, "row", scatter_dimension=0, tiled=True)
        share = share.astype(jnp.bfloat16)
    grad_field, gathered = synthesis_call(
        image_back,
        full_slope,
        row_filters,
        matrices,
        detail_weight,
        skip_weight,
        upstream,
        share,
        True,
    )
    gathered = as_float(gathered[: 10 * channels])
    grad_detail = gathered[: 9 * channels].reshape(3, 3, channels, channels)
    grad_skip = gathered[9 * channels :]
    if whole_tiles:
        spec_real, spec_imag = spec_parts(spec_field, mode_rows, mode_cols, devices)
        back_real, back_imag = spec_parts(spec_back, mode_rows, mode_cols, devices)
    beside_real = jnp.stack([back_real, back_imag]) * factor
    beside_imag = jnp.stack([back_imag, -back_real]) * factor
    grad_spectral = (
        spec_real[None, :, :, None] * beside_real[:, :, None, :]
        + spec_imag[None, :, :, None] * beside_imag[:, :, None, :]
    )
    return (grad_field, grad_detail, grad_skip, grad_spectral)


def solution(mesh):
    placed = (
        P(("groups", "row"), None, None),
        P(("groups", "row"), None, None),
        P(),
        P(),
        P(),
        P(),
        P(),
        P(),
        P(None, "row", None, None),
        P(),
        P(),
    )
    return jax.shard_map(
        per_device,
        mesh=mesh,
        in_specs=placed,
        out_specs=(
            P(("groups", "row"), None, None),
            P("groups", None, None, None),
            P("groups", None),
            P("groups", "row", None, None),
        ),
        check_vma=False,
    )
```

```python
import functools
import math

import jax
import jax.numpy as jnp
from jax import lax
from jax.experimental import pallas as pl
from jax.experimental.pallas import tpu as pltpu
from jax.sharding import PartitionSpec as P

MESH = pl.DeviceIdType.MESH
NN = (((1,), (0,)), ((), ()))
NT = (((1,), (1,)), ((), ()))


def greet_all(size):
    me = lax.axis_index("row")
    barrier = pltpu.get_barrier_semaphore()
    for step in range(1, size):
        pl.semaphore_signal(
            barrier, inc=1, device_id={"row": lax.rem(me + step, size)}, device_id_type=MESH
        )


def hear_all(size):
    pl.semaphore_wait(pltpu.get_barrier_semaphore(), size - 1)


def tiles_copy(size, tile, send, land, send_sem, recv_sem, step):
    me = lax.axis_index("row")
    if step:
        partner = lax.rem(me + step, size)
        source = pl.ds(pl.multiple_of(partner * tile, tile), tile)
        target = pl.ds(pl.multiple_of(me * tile, tile), tile)
    else:
        partner = lax.rem(me + 1, size)
        source = target = pl.ds(0, (size - 1) * tile)
    return pltpu.make_async_remote_copy(
        src_ref=send.at[source],
        dst_ref=land.at[target],
        send_sem=send_sem,
        recv_sem=recv_sem,
        device_id={"row": partner},
        device_id_type=MESH,
    )


def start_exchange(size, tile, send, land, send_sem, recv_sem):
    me = lax.axis_index("row")
    for step in range(1, size):
        tiles_copy(size, tile, send, land, send_sem, recv_sem, step).start()
    own = pl.ds(pl.multiple_of(me * tile, tile), tile)
    land[own, :] = send[own, :]
    return tiles_copy(size, tile, send, land, send_sem, recv_sem, 0)


def channel_product(first, second):
    return lax.dot_general(first, second, NT, preferred_element_type=jnp.float32)


def local_sums(full_field, full_slope, skip_share, sums, scales, skip_scale):
    channels = skip_share.shape[0]
    for level in range(3):
        left, right = full_field[level], full_slope[level]
        half = left.shape[3] // 2
        if half % 128 == 0:
            halves = (slice(half, None), slice(0, half), slice(half, None))
        else:
            halves = (None, None, None)
        for member, (branch, part) in enumerate(zip((0, 1, 1), halves)):

            def body(row, total):
                if part is not None:
                    return total + channel_product(
                        left[branch, row, :, part], right[branch, row, :, part]
                    )
                lane = lax.broadcasted_iota(jnp.int32, left.shape[2:], 1)
                kept = (lane < half) if member == 1 else (lane >= half)
                wide = jnp.where(kept, as_float(left[branch, row]), 0.0).astype(jnp.bfloat16)
                return total + channel_product(wide, right[branch, row])

            total = lax.fori_loop(
                0, left.shape[1], body, jnp.zeros((channels, channels), jnp.float32), unroll=True
            )
            start = (level * 3 + member) * channels
            sums[start : start + channels, :] = (total * scales[level]).astype(jnp.bfloat16)
    sums[9 * channels : 10 * channels, :] = (skip_share[...] * skip_scale).astype(
        jnp.bfloat16
    )
    if sums.shape[0] > 10 * channels:
        sums[10 * channels :, :] = jnp.zeros(
            (sums.shape[0] - 10 * channels, channels), jnp.bfloat16
        )


def spectral_kernel(
    size,
    near_cols,
    back,
    scales,
    coarse_ref,
    col_ref,
    row_ref,
    row_inv_ref,
    col_inv_ref,
    weight,
    *rest,
):
    if back:
        full_field, full_slope = rest[:3], (*rest[3:5], coarse_ref)
        skip_share, image_ref, spec_ref, share, sums, landed, more_sem, *rest = rest[5:]
    else:
        image_ref, spec_ref, *rest = rest
    (
        send_a,
        land_a,
        send_b,
        send_c,
        land_c,
        send_d,
        land_d,
        rotated,
        send_sem,
        recv_sem,
    ) = rest
    greet_all(size)
    rows = coarse_ref.shape[1]
    total = None
    for row in range(rows):
        part = lax.dot_general(
            col_ref[row].astype(jnp.bfloat16),
            coarse_ref[0, row],
            NT,
            preferred_element_type=jnp.float32,
        )
        total = part if total is None else total + part
    send_a[...] = total
    hear_all(size)
    tile_a = send_a.shape[0] // size
    first = start_exchange(size, tile_a, send_a, land_a, send_sem.at[0], recv_sem.at[0])
    if back:
        local_sums(full_field, full_slope, skip_share, sums, scales[:3], scales[3])
    first.wait_recv()
    send_b[...] = lax.dot_general(
        row_ref[...].astype(jnp.bfloat16),
        land_a[...].astype(jnp.bfloat16),
        NN,
        preferred_element_type=jnp.float32,
    )
    tile_b = send_b.shape[0] // size
    second = start_exchange(size, tile_b, send_b, spec_ref, send_sem.at[1], recv_sem.at[1])
    if back:
        chunk = sums.shape[0] // size
        scatter = start_exchange(size, chunk, sums, landed, more_sem.at[0], more_sem.at[1])
    second.wait_recv()
    spec = spec_ref[...]
    count = spec.shape[0]
    even = lax.broadcasted_iota(jnp.int32, spec.shape, 0) % 2 == 0
    turned = jnp.where(even, -pltpu.roll(spec, count - 1, 0), pltpu.roll(spec, 1, 0))
    rotated[...] = -turned if back else turned
    per_tile = tile_b // 2
    modes = weight.shape[1]
    per_row = near_cols
    mode_rows = per_tile // per_row
    dims = NT if back else NN

    def mix(source, carry):
        here = pl.ds(pl.multiple_of(source * tile_b, tile_b), tile_b)
        plain = spec_ref[here, :].astype(jnp.bfloat16)
        turn = rotated[here, :].astype(jnp.bfloat16)
        pair = lax.broadcasted_iota(jnp.int32, (tile_b, plain.shape[1]), 0) // 2
        result = jnp.zeros((tile_b, plain.shape[1]), jnp.float32)
        both = jnp.concatenate([plain, turn], axis=1)
        channels = plain.shape[1]
        for member in range(0, per_tile, 2):
            blocks = []
            for one in (member, member + 1):
                mode = (one // per_row) * (modes // mode_rows) + source * per_row + one % per_row
                blocks.append(
                    jnp.concatenate(
                        [weight[part, mode].astype(jnp.bfloat16) for part in range(2)],
                        axis=1 if back else 0,
                    )
                )
            done = lax.dot_general(
                both,
                jnp.concatenate(blocks, axis=0 if back else 1),
                dims,
                preferred_element_type=jnp.float32,
            )
            result = jnp.where(pair == member, done[:, :channels], result)
            result = jnp.where(pair == member + 1, done[:, channels:], result)
        send_c[here, :] = result
        return carry

    lax.fori_loop(0, size, mix, 0, unroll=4 if size % 4 == 0 else 1)
    third = start_exchange(size, tile_b, send_c, land_c, send_sem.at[2], recv_sem.at[2])
    third.wait_recv()
    send_d[...] = lax.dot_general(
        row_inv_ref[...].astype(jnp.bfloat16),
        land_c[...].astype(jnp.bfloat16),
        NN,
        preferred_element_type=jnp.float32,
    )
    fourth = start_exchange(size, tile_a, send_d, land_d, send_sem.at[3], recv_sem.at[3])
    if back:
        scatter.wait_recv()
        whole = as_float(landed[0:chunk, :])
        for step in range(1, size):
            whole = whole + as_float(landed[step * chunk : (step + 1) * chunk, :])
        share[...] = whole.astype(jnp.bfloat16)
        scatter.wait_send()
    fourth.wait_recv()
    across = land_d[...].T.astype(jnp.bfloat16)
    for row in range(rows):
        image_ref[row] = lax.dot_general(
            across,
            col_inv_ref[row].astype(jnp.bfloat16),
            NN,
            preferred_element_type=jnp.float32,
        ).astype(jnp.bfloat16)
    for sent in (first, second, third, fourth):
        sent.wait_send()


def picked(modes, places):
    same = places[:, None] == jnp.arange(modes.shape[0])[None, :]
    return jnp.sum(jnp.where(same, modes[None, :], 0), axis=1)


def spectral_tables(row_modes, col_modes, local_rows, columns, size):
    height = local_rows * size
    mode_rows, mode_cols = row_modes.shape[0], col_modes.shape[0]
    near_rows, near_cols = mode_rows // size, mode_cols // size
    count_a, count_b = height * near_cols * 2, mode_rows * near_cols * 2
    where_a, where_b = jnp.arange(count_a), jnp.arange(count_b)
    part_a, part_b = where_a % 2, where_b % 2
    spot = where_a // 2
    block = spot // (near_cols * local_rows)
    col_of = picked(col_modes, block * near_cols + spot % near_cols)
    wide = jnp.arange(2 * columns)
    turns = (col_of[:, None] * wide[None, :] + part_a[:, None] * (columns // 4)) % columns
    col = jnp.cos(turns.astype(jnp.float32) * (2.0 * math.pi / columns))
    same_row = (spot // near_cols % local_rows)[None, :] == jnp.arange(local_rows)[:, None]
    inside = wide < columns
    col = jnp.where(same_row[:, :, None] & inside[None, None, :], col[None], 0.0)
    col_inv = col
    row_of = picked(row_modes, where_b // (2 * near_cols))
    quarter = (part_b[:, None] - part_a[None, :]) * (height // 4)
    turns = (row_of[:, None] * (where_a // (2 * near_cols))[None, :] + quarter + height) % height
    same_col = (where_b // 2 % near_cols)[:, None] == (where_a // 2 % near_cols)[None, :]
    row = jnp.cos(turns.astype(jnp.float32) * (2.0 * math.pi / height))
    row = jnp.where(same_col, row, 0.0)
    row_inv = row.T * (1.0 / (height * columns))
    return col, row, row_inv, col_inv


def spectral_path(coarse, weight, tables, near_cols, extra, scales, sum_rows):
    back = len(extra) > 0
    col, row, row_inv, col_inv = tables
    size = lax.axis_size("row")
    channels = coarse.shape[2]
    count_a, count_b = col.shape[1], row.shape[0]
    f32 = jnp.float32
    vmem = pl.BlockSpec(memory_space=pltpu.VMEM)
    return pl.pallas_call(
        functools.partial(spectral_kernel, size, near_cols, back, scales),
        out_shape=(
            jax.ShapeDtypeStruct(coarse.shape[1:], jnp.bfloat16),
            jax.ShapeDtypeStruct((count_b, channels), f32),
            *([jax.ShapeDtypeStruct((sum_rows // size, channels), jnp.bfloat16)] if back else []),
        ),
        in_specs=[vmem] * (6 + len(extra)),
        out_specs=(vmem,) * (3 if back else 2),
        scratch_shapes=[
            *(
                [
                    pltpu.VMEM((sum_rows, channels), jnp.bfloat16),
                    pltpu.VMEM((sum_rows, channels), jnp.bfloat16),
                    pltpu.SemaphoreType.DMA((2,)),
                ]
                if back
                else []
            ),
            pltpu.VMEM((count_a, channels), f32),
            pltpu.VMEM((count_a, channels), f32),
            pltpu.VMEM((count_b, channels), f32),
            pltpu.VMEM((count_b, channels), f32),
            pltpu.VMEM((count_b, channels), f32),
            pltpu.VMEM((count_a, channels), f32),
            pltpu.VMEM((count_a, channels), f32),
            pltpu.VMEM((count_b, channels), f32),
            pltpu.SemaphoreType.DMA((4,)),
            pltpu.SemaphoreType.DMA((4,)),
        ],
        compiler_params=pltpu.CompilerParams(
            collective_id=1 if back else 0,
            has_side_effects=True,
            vmem_limit_bytes=24 * 1024 * 1024,
        ),
        cost_estimate=pl.CostEstimate(
            flops=8 * weight.size, bytes_accessed=4 * weight.size, transcendentals=0
        ),
        name="spectral_back" if back else "spectral",
    )(coarse, col, row, row_inv, col_inv, weight, *extra)


def spec_parts(spec, mode_rows, mode_cols, size):
    channels = spec.shape[1]
    grid = spec.reshape(size, mode_rows // size, mode_cols // size, 2, channels)
    grid = jnp.transpose(grid, (3, 1, 0, 2, 4)).reshape(2, -1, channels)
    return grid[0], grid[1]


def as_float(values):
    return values.astype(jnp.float32)


def precise(form, first_in, second_in):
    return jnp.einsum(form, first_in, second_in, precision=lax.Precision.HIGHEST)


def narrow(form, first_in, second_in):
    return jnp.einsum(form, first_in, second_in, preferred_element_type=jnp.float32)


def column_tables(col_modes, length):
    positions = jnp.arange(length, dtype=jnp.int32)
    turns = positions[:, None] * col_modes[None, :] % length
    angles = turns.astype(jnp.float32) * (2.0 * math.pi / length)
    return (jnp.cos(angles), jnp.sin(angles))


def row_tables(row_modes, positions, length):
    turns = row_modes[:, None] * positions[None, :] % length
    angles = turns.astype(jnp.float32) * (2.0 * math.pi / length)
    return (jnp.cos(angles), jnp.sin(angles))


def owned_modes(coarse, row_modes, col_modes):
    local_rows, channels, columns = coarse.shape
    devices = lax.axis_size("row")
    height = local_rows * devices
    cos_col, sin_col = column_tables(col_modes, columns)
    values = as_float(coarse)
    real_one = precise("hcw,wm->hcm", values, cos_col)
    imag_one = -precise("hcw,wm->hcm", values, sin_col)
    positions = lax.axis_index("row") * local_rows + jnp.arange(local_rows, dtype=jnp.int32)
    cos_row, sin_row = row_tables(row_modes, positions, height)
    real_two = precise("ph,hcm->pmc", cos_row, real_one) + precise("ph,hcm->pmc", sin_row, imag_one)
    imag_two = precise("ph,hcm->pmc", cos_row, imag_one) - precise("ph,hcm->pmc", sin_row, real_one)
    term_all = jnp.stack([real_two.reshape(-1, channels), imag_two.reshape(-1, channels)], axis=1)
    owned = lax.psum_scatter(term_all, "row", scatter_dimension=0, tiled=True)
    return (owned[:, 0], owned[:, 1])


def owned_image(real_owned, imag_owned, row_modes, col_modes, local_rows, columns):
    devices = lax.axis_size("row")
    height = local_rows * devices
    mode_rows = row_modes.shape[0]
    mode_cols = col_modes.shape[0]
    positions = lax.axis_index("row") * local_rows + jnp.arange(local_rows, dtype=jnp.int32)
    real_piece = lax.all_gather(real_owned, "row", axis=0, tiled=True)
    imag_piece = lax.all_gather(imag_owned, "row", axis=0, tiled=True)
    piece_rows = real_piece.shape[0]
    flat = jnp.arange(piece_rows, dtype=jnp.int32)
    row_pick = (flat // mode_cols)[:, None] == jnp.arange(mode_rows, dtype=jnp.int32)[None, :]
    frequency = jnp.sum(jnp.where(row_pick, row_modes[None, :], 0), axis=1)
    column_pick = (
        (flat % mode_cols)[:, None] == jnp.arange(mode_cols, dtype=jnp.int32)[None, :]
    ).astype(jnp.float32)
    turns = positions[:, None] * frequency[None, :] % height
    angles = turns.astype(jnp.float32) * (2.0 * math.pi / height)
    cos_part = jnp.cos(angles)
    sin_part = jnp.sin(angles)
    cos_pick = cos_part[:, :, None] * column_pick[None, :, :]
    sin_pick = sin_part[:, :, None] * column_pick[None, :, :]
    real_sum = precise("hnm,nc->hcm", cos_pick, real_piece) - precise(
        "hnm,nc->hcm", sin_pick, imag_piece
    )
    imag_sum = precise("hnm,nc->hcm", cos_pick, imag_piece) + precise(
        "hnm,nc->hcm", sin_pick, real_piece
    )
    cos_col, sin_col = column_tables(col_modes, columns)
    image = precise("hcm,wm->hcw", real_sum, cos_col) - precise("hcm,wm->hcw", imag_sum, sin_col)
    return image.astype(jnp.bfloat16)


def mix_modes(real_in, imag_in, weight_real, weight_imag, factor):
    real_out = (
        precise("nc,nco->no", real_in, weight_real) - precise("nc,nco->no", imag_in, weight_imag)
    ) * factor
    imag_out = (
        precise("nc,nco->no", real_in, weight_imag) + precise("nc,nco->no", imag_in, weight_real)
    ) * factor
    return (real_out, imag_out)


def mix_modes_back(real_in, imag_in, weight_real, weight_imag, factor):
    real_out = (
        precise("no,nco->nc", real_in, weight_real) + precise("no,nco->nc", imag_in, weight_imag)
    ) * factor
    imag_out = (
        precise("no,nco->nc", imag_in, weight_real) - precise("no,nco->nc", real_in, weight_imag)
    ) * factor
    return (real_out, imag_out)


def greet_ring(receives_from):
    barrier = pltpu.get_barrier_semaphore()
    pl.semaphore_signal(barrier, inc=1, device_id={"row": receives_from}, device_id_type=MESH)
    pl.semaphore_wait(barrier, 1)


def analysis_kernel(
    size,
    values,
    taps,
    filter_1,
    filter_2,
    filter_3,
    out_1,
    out_2,
    out_3,
    halo_1,
    halo_2,
    halo_3,
    send_sem,
    recv_sem,
):
    me = lax.axis_index("row")
    above, below = lax.rem(me + size - 1, size), lax.rem(me + 1, size)
    greet_ring(below)

    def copy(level, source, halo):
        return pltpu.make_async_remote_copy(
            src_ref=source,
            dst_ref=halo,
            send_sem=send_sem.at[level],
            recv_sem=recv_sem.at[level],
            device_id={"row": above},
            device_id_type=MESH,
        )

    def one(get, row, matrix, out):
        loaded = [as_float(get(2 * row + offset)) for offset in range(4)]
        halves = []
        for branch in range(2):
            running = taps[branch, 0] * loaded[0]
            for offset in range(1, 4):
                running = running + taps[branch, offset] * loaded[offset]
            halves.append(running.astype(jnp.bfloat16))
        both = jnp.concatenate(halves, axis=0)
        done = jnp.dot(both, matrix[...], preferred_element_type=jnp.float32).astype(jnp.bfloat16)
        count = halves[0].shape[0]
        out[0, row] = done[:count]
        out[1, row] = done[count:]

    def span(get, first, last, matrix, out):
        def body(row, carry):
            one(get, row, matrix, out)
            return carry

        lax.fori_loop(first, last, body, 0, unroll=1 if (last - first) % 2 else 2)

    def edged(get, halo, count):
        return lambda row: get(row) if row < count else halo[row - count]

    count = values.shape[0]
    half_1, half_2 = filter_1.shape[0] // 2, filter_2.shape[0] // 2
    get_1 = lambda row: values[row]
    get_2 = lambda row: out_1[0, row, :, :half_1]
    get_3 = lambda row: out_2[0, row, :, :half_2]
    first = copy(0, values.at[pl.ds(0, 2)], halo_1)
    first.start()
    span(get_1, 0, 2, filter_1, out_1)
    second = copy(1, out_1.at[0, pl.ds(0, 2), :, pl.ds(0, half_1)], halo_2)
    second.start()
    early = min(6, count // 2 - 1)
    span(get_1, 2, early, filter_1, out_1)
    span(get_2, 0, 2, filter_2, out_2)
    third = copy(2, out_2.at[0, pl.ds(0, 2), :, pl.ds(0, half_2)], halo_3)
    third.start()
    span(get_1, early, count // 2 - 1, filter_1, out_1)
    first.wait()
    one(edged(get_1, halo_1, count), count // 2 - 1, filter_1, out_1)
    span(get_2, 2, count // 4 - 1, filter_2, out_2)
    second.wait()
    one(edged(get_2, halo_2, count // 2), count // 4 - 1, filter_2, out_2)
    span(get_3, 0, count // 8 - 1, filter_3, out_3)
    third.wait()
    one(edged(get_3, halo_3, count // 4), count // 8 - 1, filter_3, out_3)


def analysis_call(values, row_filters, matrices, back):
    size = lax.axis_size("row")
    count, channels, columns = values.shape
    vmem = pl.BlockSpec(memory_space=pltpu.VMEM)
    widths = [columns >> level for level in range(3)]
    return pl.pallas_call(
        functools.partial(analysis_kernel, size),
        out_shape=tuple(
            jax.ShapeDtypeStruct((2, count >> level + 1, channels, widths[level]), jnp.bfloat16)
            for level in range(3)
        ),
        in_specs=[vmem, pl.BlockSpec(memory_space=pltpu.SMEM), vmem, vmem, vmem],
        out_specs=(vmem, vmem, vmem),
        scratch_shapes=[
            *(pltpu.VMEM((2, channels, width), jnp.bfloat16) for width in widths),
            pltpu.SemaphoreType.DMA((3,)),
            pltpu.SemaphoreType.DMA((3,)),
        ],
        compiler_params=pltpu.CompilerParams(
            collective_id=3 if back else 2,
            has_side_effects=True,
            vmem_limit_bytes=24 * 1024 * 1024,
        ),
        cost_estimate=pl.CostEstimate(
            flops=6 * values.size * columns, bytes_accessed=16 * values.size, transcendentals=0
        ),
        name="analysis_back" if back else "analysis",
    )(values, row_filters, *matrices)


def gelu_slope(value):
    scale = math.sqrt(2.0 / math.pi)
    square = value * value
    bend = jnp.tanh(scale * (value + 0.044715 * (square * value)))
    return 0.5 * (1.0 + bend) + 0.5 * value * (1.0 - bend * bend) * (
        scale * (1.0 + 3 * 0.044715 * square)
    )


def synthesis_kernel(
    size,
    back,
    image,
    out_1,
    out_2,
    out_3,
    taps,
    turned_1,
    turned_2,
    turned_3,
    detail,
    skip,
    plain,
    *rest,
):
    if back:
        share, result, gathered, send_more, recv_more, *rest = rest
    else:
        cotangent, result, skip_share, detail_turned, skip_turned, *rest = rest
        skip_share[...] = jnp.zeros_like(skip_share)
        for level in range(3):
            for member in range(3):
                detail_turned[level, member] = as_float(detail[level, member]).T.astype(
                    jnp.bfloat16
                )
        skip_turned[...] = as_float(skip[...]).T.astype(jnp.bfloat16)
        detail, skip = detail_turned, skip_turned
    syn_1, syn_2, syn_3, halo_1, halo_2, halo_3, top_1, top_2, send_sem, recv_sem = rest
    me = lax.axis_index("row")
    above, below = lax.rem(me + size - 1, size), lax.rem(me + 1, size)
    if back:
        greet_all(size)
        hear_all(size)
    else:
        greet_ring(above)

    def copy(level, syn, halo):
        return pltpu.make_async_remote_copy(
            src_ref=syn.at[:, syn.shape[1] - 1],
            dst_ref=halo,
            send_sem=send_sem.at[level],
            recv_sem=recv_sem.at[level],
            device_id={"row": below},
            device_id_type=MESH,
        )

    def mixed(level, member, band):
        return jnp.dot(detail[level, member], band, preferred_element_type=jnp.float32).astype(
            jnp.bfloat16
        )

    def one(level, row, top, out, turned, syn):
        half = out.shape[3] // 2
        if half % 128 == 0:
            low = [top[row], mixed(level, 0, out[0, row, :, half:])]
            high = [mixed(level, 1, out[1, row, :, :half]), mixed(level, 2, out[1, row, :, half:])]
            low, high = jnp.concatenate(low, axis=1), jnp.concatenate(high, axis=1)
        else:
            bands, lower = out[1, row], lax.broadcasted_iota(jnp.int32, out.shape[2:], 1) < half
            low = jnp.where(lower, as_float(top[row]), as_float(mixed(level, 0, out[0, row])))
            high = jnp.where(
                lower, as_float(mixed(level, 1, bands)), as_float(mixed(level, 2, bands))
            )
            low, high = low.astype(jnp.bfloat16), high.astype(jnp.bfloat16)
        both = jnp.concatenate([low, high], axis=0)
        done = lax.dot_general(
            both, turned[...], NT, preferred_element_type=jnp.float32
        ).astype(jnp.bfloat16)
        count = low.shape[0]
        syn[0, row] = done[:count]
        syn[1, row] = done[count:]

    def joined(syn, row, previous):
        low_now, high_now = as_float(syn[0, row]), as_float(syn[1, row])
        low_prev, high_prev = as_float(previous(0)), as_float(previous(1))
        pair = []
        for parity in range(2):
            running = taps[0, parity] * low_now + taps[1, parity] * high_now
            running = running + taps[0, parity + 2] * low_prev
            pair.append(running + taps[1, parity + 2] * high_prev)
        return pair

    def combine(syn, row, halo, top):
        previous = (lambda part: halo[part]) if halo is not None else lambda part: syn[part, row - 1]
        pair = joined(syn, row, previous)
        for parity in range(2):
            top[2 * row + parity] = pair[parity].astype(jnp.bfloat16)

    def last(row, halo):
        previous = (
            (lambda part: halo[part]) if halo is not None else lambda part: syn_1[part, row - 1]
        )
        pair = joined(syn_1, row, previous)
        for parity in range(2):
            here = 2 * row + parity
            value = pair[parity] + jnp.dot(
                skip[...], plain[here], preferred_element_type=jnp.float32
            )
            if not back:
                value = (as_float(cotangent[here]) * gelu_slope(value)).astype(jnp.bfloat16)
                skip_share[...] += channel_product(plain[here], value)
            result[here] = value

    def span(first, stop, call):
        def body(row, carry):
            call(row)
            return carry

        lax.fori_loop(first, stop, body, 0, unroll=1 if (stop - first) % 2 else 2)

    level_3 = lambda row: one(2, row, image, out_3, turned_3, syn_3)
    level_2 = lambda row: one(1, row, top_2, out_2, turned_2, syn_2)
    level_1 = lambda row: one(0, row, top_1, out_1, turned_1, syn_1)
    rows_3, rows_2, rows_1 = syn_3.shape[1], syn_2.shape[1], syn_1.shape[1]
    level_3(rows_3 - 1)
    third = copy(2, syn_3, halo_3)
    third.start()
    if back:
        chunk = share.shape[0]
        target = pl.ds(pl.multiple_of(me * chunk, chunk), chunk)
        for step in range(1, size):
            pltpu.make_async_remote_copy(
                src_ref=share,
                dst_ref=gathered.at[target],
                send_sem=send_more.at[0],
                recv_sem=recv_more.at[0],
                device_id={"row": lax.rem(me + step, size)},
                device_id_type=MESH,
            ).start()
        gathered[target, :] = share[...]
    span(0, rows_3 - 1, level_3)
    combine(syn_3, rows_3 - 1, None, top_2)
    level_2(rows_2 - 1)
    second = copy(1, syn_2, halo_2)
    second.start()
    level_2(rows_2 - 2)
    combine(syn_2, rows_2 - 1, None, top_1)
    level_1(rows_1 - 1)
    first = copy(0, syn_1, halo_1)
    first.start()
    level_1(rows_1 - 2)
    last(rows_1 - 1, None)
    span(1, rows_3 - 1, lambda row: combine(syn_3, row, None, top_2))
    third.wait()
    combine(syn_3, 0, halo_3, top_2)
    span(0, rows_2 - 2, level_2)
    span(1, rows_2 - 1, lambda row: combine(syn_2, row, None, top_1))
    span(2, rows_1 - 2, level_1)
    span(3, rows_1 - 1, lambda row: last(row, None))
    second.wait()
    combine(syn_2, 0, halo_2, top_1)
    span(0, 2, level_1)
    span(1, 3, lambda row: last(row, None))
    first.wait()
    last(0, halo_1)
    if back:
        tiles_copy(size, chunk, gathered, gathered, send_more.at[0], recv_more.at[0], 0).wait()


def synthesis_call(image, bands, row_filters, matrices, detail, skip, plain, extra, back):
    size = lax.axis_size("row")
    vmem = pl.BlockSpec(memory_space=pltpu.VMEM)
    smem = pl.BlockSpec(memory_space=pltpu.SMEM)
    channels = plain.shape[1]
    result = jax.ShapeDtypeStruct(plain.shape, jnp.float32 if back else jnp.bfloat16)
    own = [pltpu.VMEM(detail.shape, jnp.bfloat16), pltpu.VMEM(skip.shape, jnp.bfloat16)]
    second = jax.ShapeDtypeStruct(skip.shape, jnp.float32)
    if back:
        whole = (extra.shape[0] * size, channels)
        second = jax.ShapeDtypeStruct(whole, jnp.bfloat16)
        own = [pltpu.SemaphoreType.DMA((1,)), pltpu.SemaphoreType.DMA((1,))]
    return pl.pallas_call(
        functools.partial(synthesis_kernel, size, back),
        out_shape=(result, second),
        in_specs=[vmem] * 4 + [smem] + [vmem] * 7,
        out_specs=(vmem, vmem),
        scratch_shapes=[
            *own,
            *(pltpu.VMEM(band.shape, jnp.bfloat16) for band in bands),
            *(pltpu.VMEM((2, channels, band.shape[3]), jnp.bfloat16) for band in bands),
            pltpu.VMEM((plain.shape[0] // 2, channels, bands[0].shape[3] // 2), jnp.bfloat16),
            pltpu.VMEM((plain.shape[0] // 4, channels, bands[1].shape[3] // 2), jnp.bfloat16),
            pltpu.SemaphoreType.DMA((3,)),
            pltpu.SemaphoreType.DMA((3,)),
        ],
        compiler_params=pltpu.CompilerParams(
            collective_id=5 if back else 4,
            has_side_effects=True,
            vmem_limit_bytes=24 * 1024 * 1024,
        ),
        cost_estimate=pl.CostEstimate(
            flops=6 * plain.size * plain.shape[2],
            bytes_accessed=32 * plain.size,
            transcendentals=plain.size,
        ),
        name="synthesis_back" if back else "synthesis",
    )(image, *bands, row_filters, *matrices, detail, skip, plain, extra)


def split_bands(full):
    band_list = []
    for both in full:
        half = both.shape[3] // 2
        band_list.append((both[0, :, :, half:], both[1, :, :, :half], both[1, :, :, half:]))
    return full[2][0, :, :, : full[2].shape[3] // 2], band_list


def per_device(
    field,
    cotangent,
    row_filters,
    col_filter_1,
    col_filter_2,
    col_filter_3,
    detail_weight,
    skip_weight,
    spectral_weight,
    row_modes,
    col_modes,
):
    matrices = (col_filter_1, col_filter_2, col_filter_3)
    devices = lax.axis_size("row")
    full_field = analysis_call(field, row_filters, matrices, False)
    coarse_field, bands_field = split_bands(full_field)
    total_rows, total_cols = field.shape[0] * devices, field.shape[2]
    scales = [
        1.0 / math.sqrt((total_rows >> octave + 1) * (total_cols >> octave + 1))
        for octave in range(3)
    ] + [1.0 / math.sqrt(total_rows * total_cols)]
    sum_rows = 10 * field.shape[1]
    sum_rows = -(-sum_rows // (16 * devices)) * 16 * devices
    local_rows, channels, columns = coarse_field.shape
    height = local_rows * devices
    factor = 1.0 / (height * columns)
    weight_real = spectral_weight[0]
    weight_imag = spectral_weight[1]
    mode_rows, mode_cols = row_modes.shape[0], col_modes.shape[0]
    whole_tiles = (
        mode_rows % devices == 0
        and mode_cols % devices == 0
        and (2 * local_rows * mode_cols // devices) % 8 == 0
        and (2 * (mode_rows // devices) * (mode_cols // devices)) % 8 == 0
    )
    if whole_tiles:
        near_cols = mode_cols // devices
        tables = spectral_tables(row_modes, col_modes, local_rows, columns, devices)
        coarse_image, spec_field = spectral_path(
            full_field[2], spectral_weight, tables, near_cols, (), scales, sum_rows
        )
    else:
        spec_real, spec_imag = owned_modes(coarse_field, row_modes, col_modes)
        out_real, out_imag = mix_modes(spec_real, spec_imag, weight_real, weight_imag, factor)
        coarse_image = owned_image(out_real, out_imag, row_modes, col_modes, local_rows, columns)
        coarse_image = jnp.pad(coarse_image, ((0, 0), (0, 0), (0, columns)))
    upstream, skip_share = synthesis_call(
        coarse_image,
        full_field,
        row_filters,
        matrices,
        detail_weight,
        skip_weight,
        field,
        cotangent,
        False,
    )
    full_slope = analysis_call(upstream, row_filters, matrices, True)
    coarse_slope, bands_slope = split_bands(full_slope)
    if whole_tiles:
        extra = (*full_field, *full_slope[:2], skip_share)
        image_back, spec_back, share = spectral_path(
            full_slope[2], spectral_weight, tables, near_cols, extra, scales, sum_rows
        )
    else:
        back_real, back_imag = owned_modes(coarse_slope, row_modes, col_modes)
        turned_real, turned_imag = mix_modes_back(
            back_real, back_imag, weight_real, weight_imag, factor
        )
        image_back = owned_image(
            turned_real, turned_imag, row_modes, col_modes, local_rows, columns
        )
        image_back = jnp.pad(image_back, ((0, 0), (0, 0), (0, columns)))
        shares = [
            narrow("hcw,how->co", bands_field[octave][member], bands_slope[octave][member])
            * scales[octave]
            for octave in range(3)
            for member in range(3)
        ] + [skip_share * scales[3]]
        sums = jnp.concatenate(shares, axis=0)
        sums = jnp.pad(sums, ((0, sum_rows - sums.shape[0]), (0, 0)))
        share = lax.psum_scatter(sums, "row", scatter_dimension=0, tiled=True)
        share = share.astype(jnp.bfloat16)
    grad_field, gathered = synthesis_call(
        image_back,
        full_slope,
        row_filters,
        matrices,
        detail_weight,
        skip_weight,
        upstream,
        share,
        True,
    )
    gathered = as_float(gathered[: 10 * channels])
    grad_detail = gathered[: 9 * channels].reshape(3, 3, channels, channels)
    grad_skip = gathered[9 * channels :]
    if whole_tiles:
        spec_real, spec_imag = spec_parts(spec_field, mode_rows, mode_cols, devices)
        back_real, back_imag = spec_parts(spec_back, mode_rows, mode_cols, devices)
    beside_real = jnp.stack([back_real, back_imag]) * factor
    beside_imag = jnp.stack([back_imag, -back_real]) * factor
    grad_spectral = (
        spec_real[None, :, :, None] * beside_real[:, :, None, :]
        + spec_imag[None, :, :, None] * beside_imag[:, :, None, :]
    )
    return (grad_field, grad_detail, grad_skip, grad_spectral)


def solution(mesh):
    placed = (
        P(("groups", "row"), None, None),
        P(("groups", "row"), None, None),
        P(),
        P(),
        P(),
        P(),
        P(),
        P(),
        P(None, "row", None, None),
        P(),
        P(),
    )
    return jax.shard_map(
        per_device,
        mesh=mesh,
        in_specs=placed,
        out_specs=(
            P(("groups", "row"), None, None),
            P("groups", None, None, None),
            P("groups", None),
            P("groups", "row", None, None),
        ),
        check_vma=False,
    )
```
